32 devices in a mesh: tm: 16 (over z, x, core), section: 2 (over y).
Axes of the slice: x: 2, y: 2, z: 4, core: 2. Of those that a mesh axis runs over, the one named last changes fastest.
Arguments:
- layer_inputs: bfloat16 [2, 2048, 1024], P('section', 'tm')
- top_grad: bfloat16 [2048, 1024], P('tm'), may hold values from -6 to 6
- w_query: bfloat16 [2, 1024, 512], P('section')
- w_key: bfloat16 [2, 1024, 512], P('section')
- w_value: bfloat16 [2, 1024, 512], P('section'), may hold values from -0.1875 to 0.1875
- w_out: bfloat16 [2, 512, 1024], P('section'), may hold values from -0.25 to 0.25
- conv_kernel: float32 [2, 31, 1024], P('section'), may hold values from -1 to 1
- norm_gain: float32 [2, 1024], P('section'), may hold values from 0.5 to 1.5
- group_valid: int32 [16], replicated, may hold values from 1 to 128, as said below
Outputs:
- input_grads: bfloat16 [2, 2048, 1024], P('section', 'tm')
The draws below stay inside these ranges and needn't reach their ends.
Inputs may be any that keep to these rules, and one draw needn't show every extreme that they name: `group_valid`: entry c counts the valid frames at the start of group c; the rest of that group is padding. The first group is full and the last one is ragged.
All inputs are finite; a program needn't handle non-finite values.
Results may differ from the reference program's by a relative error of at most 0.017.
The reference program's roundings to bfloat16 on the way count: a program that leaves them out, or rounds other values in their place, can miss the bound.
Values may be sent and summed in bfloat16 or wider, within the bound.
No kernel may reach another device: no remote copies, remote signals or barrier semaphores. Data moves between devices by JAX's collectives and lax.ppermute only.
A program may use at most 64 MiB of HBM per device.

```python
import math
import jax
import jax.numpy as jnp
from jax import lax

D = 1024
HEADS = 8
HEAD_DIM = 64
GROUP = 128
LEFT = 4
KERNEL = 31
TOK_DEV = 128
ATT_WIDTH = 512
LAYERS = 2
TOKENS = 2048
NCHUNKS = 16
N_TM = 16


def draw_group_valid(key, part):
    first_key, second_key = jax.random.split(key)
    ragged = jax.random.randint(first_key, (NCHUNKS,), 0, 4) == 0
    shorter = jax.random.randint(second_key, (NCHUNKS,), 1, GROUP)
    counts = jnp.where(ragged, shorter, GROUP)
    positions = jnp.arange(NCHUNKS)
    counts = jnp.where(positions == 0, GROUP, counts)
    counts = jnp.where(positions == NCHUNKS - 1, shorter, counts)
    return counts.astype(jnp.int32)


def draw_layer_inputs(key, part):
    pieces = jax.random.split(key, 3)
    low_end = math.log(0.3)
    high_end = math.log(3.0)
    column_scale = jnp.exp(jax.random.uniform(pieces[1], (LAYERS, 1, D), jnp.float32, low_end, high_end))
    row_scale = jnp.exp(jax.random.uniform(pieces[2], (LAYERS, TOKENS, 1), jnp.float32, low_end, high_end))
    values = jax.random.normal(pieces[0], (LAYERS, TOKENS, D), jnp.float32) * column_scale * row_scale
    return values.astype(jnp.bfloat16)


def query_key_pair(key):
    first = jax.random.normal(jax.random.fold_in(key, 11), (LAYERS, D, ATT_WIDTH), jnp.float32) * D ** (-0.5)
    second = jax.random.normal(jax.random.fold_in(key, 13), (LAYERS, D, ATT_WIDTH), jnp.float32) * D ** (-0.5)
    return (first, second)


def draw_w_query(key, part):
    return query_key_pair(key)[0].astype(jnp.bfloat16)


def draw_w_key(key, part):
    return query_key_pair(key)[1].astype(jnp.bfloat16)


def levels(own_key, extent, cuts, least, high):
    def one(axis_at, parts):
        draws = jax.random.uniform(jax.random.fold_in(jax.random.fold_in(own_key, 6), axis_at), (parts,), jnp.float32, least / len(cuts), high / len(cuts))
        return jnp.repeat(jnp.exp(draws), extent[axis_at] // parts).reshape((-1,) + (1,) * (len(extent) - axis_at - 1))

    loudness = one(*cuts[0])
    for cut in cuts[1:]:
        loudness = loudness * one(*cut)
    return loudness


def scatter_about(own_key, shape, scale, reach, cuts=(), held_as=jnp.bfloat16):
    drawn = jax.random.normal(own_key, shape, jnp.float32) * scale
    if len(cuts) > 0:
        drawn = levels(own_key, shape, cuts, -0.22, 0.18) * drawn
    return jnp.clip(drawn, min=-reach, max=reach).astype(held_as)


def setup_inputs(seed: int = 0) -> dict:
    splits = jax.random.split(jax.random.key(seed), 10)
    layer_inputs = draw_layer_inputs(jax.random.fold_in(splits[9], 71), 0)
    top_grad = scatter_about(splits[1], (TOKENS, D), 1.0, 6.0, ((0, 16),))
    w_query = draw_w_query(jax.random.fold_in(splits[9], 71), 0)
    w_key = draw_w_key(jax.random.fold_in(splits[9], 71), 0)
    w_value = scatter_about(splits[4], (LAYERS, D, ATT_WIDTH), D ** -0.5, 0.1875, ((0, 2),))
    w_out = scatter_about(splits[5], (LAYERS, ATT_WIDTH, D), ATT_WIDTH ** -0.5, 0.25, ((0, 2),))
    conv_kernel = scatter_about(splits[6], (LAYERS, KERNEL, D), KERNEL ** -0.5, 1.0, ((0, 2),), jnp.float32)
    norm_gain = jnp.clip(1.0 + 0.1 * jax.random.normal(splits[7], (LAYERS, D), jnp.float32), 0.5, 1.5)
    group_valid = draw_group_valid(jax.random.fold_in(splits[9], 71), 0)
    return dict(layer_inputs=layer_inputs, top_grad=top_grad, w_query=w_query, w_key=w_key, w_value=w_value, w_out=w_out, conv_kernel=conv_kernel, norm_gain=norm_gain, group_valid=group_valid)


NEGATIVE = -1e+30
EPSILON = 1e-05

def rounded(values):
    return lax.optimization_barrier(values.astype(jnp.bfloat16)).astype(jnp.float32)

def frame_mask(counts):
    within = jnp.arange(GROUP, dtype=jnp.int32)[None, :] < counts[:, None]
    return within.reshape(-1).astype(jnp.float32)

def normalize(values):
    center = values - lax.optimization_barrier(jnp.mean(values, axis=-1, keepdims=True))
    spread = lax.optimization_barrier(jnp.mean(center * center, axis=-1, keepdims=True))
    inverse = lax.rsqrt(spread + EPSILON)
    return (center * inverse, inverse)

def allowed_pairs(query_first, query_count, key_first, key_count, key_valid):
    query_group = (query_first + jnp.arange(query_count, dtype=jnp.int32)) // GROUP
    key_index = key_first + jnp.arange(key_count, dtype=jnp.int32)
    key_group = jnp.floor_divide(key_index, GROUP)
    allowed = (key_group[None, :] <= query_group[:, None]) & (key_group[None, :] >= query_group[:, None] - LEFT)
    return allowed & (key_valid[None, :] > 0) & (key_index[None, :] >= 0)

def head_split(matrix):
    return matrix.reshape(matrix.shape[0], HEADS, HEAD_DIM).astype(jnp.float32)

def attend_ref(queries, key_rows, value_rows, allowed):
    score_scale = HEAD_DIM ** (-0.5)
    scores = jnp.einsum('qhe,khe->hqk', head_split(queries), head_split(key_rows)) * score_scale
    scores = jnp.where(allowed[None], scores, NEGATIVE)
    highest = lax.optimization_barrier(jnp.max(scores, axis=-1, keepdims=True))
    log_total = highest[..., 0] + jnp.log(lax.optimization_barrier(jnp.sum(jnp.exp(scores - highest), axis=-1)))
    shares = jnp.exp(scores - log_total[..., None])
    shares_low = rounded(shares)
    attended = jnp.einsum('hqk,khe->qhe', shares_low, head_split(value_rows))
    return (attended.reshape(queries.shape[0], -1).astype(jnp.bfloat16), shares, shares_low)

def attend_back_ref(queries, key_rows, value_rows, attended, shares, shares_low, out_grad):
    score_scale = HEAD_DIM ** (-0.5)
    grad_heads = head_split(out_grad)
    row_dot = lax.optimization_barrier(jnp.sum(grad_heads * head_split(attended), axis=-1)).T
    share_grad = jnp.einsum('qhe,khe->hqk', grad_heads, head_split(value_rows))
    score_grad = rounded(shares * (share_grad - row_dot[..., None]))
    query_grad = score_scale * jnp.einsum('hqk,khe->qhe', score_grad, head_split(key_rows))
    key_grad = score_scale * jnp.einsum('hqk,qhe->khe', score_grad, head_split(queries))
    value_grad = jnp.einsum('hqk,qhe->khe', shares_low, grad_heads)
    count = key_rows.shape[0]
    return (query_grad.reshape(queries.shape[0], -1).astype(jnp.bfloat16), key_grad.reshape(count, -1), value_grad.reshape(count, -1))

def layer_grad(inputs, upstream, query_weight, key_weight, value_weight, out_weight, kernel, norm_scale, frame_valid, key_valid):
    frames = TOK_DEV
    span_back = -(-(LEFT * GROUP) // frames)
    window_rows = (span_back + 1) * frames
    widened = inputs.astype(jnp.float32)
    unit, inverse = normalize(widened)
    normed = (unit * norm_scale).astype(jnp.bfloat16)
    queries = jnp.dot(normed, query_weight, preferred_element_type=jnp.float32).astype(jnp.bfloat16)
    key_rows = jnp.dot(normed, key_weight, preferred_element_type=jnp.float32).astype(jnp.bfloat16)
    value_rows = jnp.dot(normed, value_weight, preferred_element_type=jnp.float32).astype(jnp.bfloat16)
    width = queries.shape[1]
    pad_rows = jnp.zeros((span_back * frames, width), jnp.bfloat16)
    key_pad = jnp.concatenate([pad_rows, key_rows])
    value_pad = jnp.concatenate([pad_rows, value_rows])
    blocks = jnp.arange(N_TM, dtype=jnp.int32)

    def block_pieces(block_index):
        first_row = block_index * frames
        block_queries = lax.dynamic_slice_in_dim(queries, first_row, frames)
        block_keys = lax.dynamic_slice_in_dim(key_pad, first_row, window_rows)
        block_values = lax.dynamic_slice_in_dim(value_pad, first_row, window_rows)
        block_valid = lax.dynamic_slice_in_dim(key_valid, first_row, window_rows)
        allowed = allowed_pairs(first_row, frames, first_row - span_back * frames, window_rows, block_valid)
        return (block_queries, block_keys, block_values, allowed)

    def forward_block(block_index):
        return attend_ref(*block_pieces(block_index))[0]
    attended = lax.map(forward_block, blocks).reshape(TOKENS, width)
    residual = widened + jnp.dot(attended, out_weight, preferred_element_type=jnp.float32)
    mixer_input = (residual * frame_valid[:, None]).astype(jnp.bfloat16)
    mixer_pad = jnp.concatenate([jnp.zeros((KERNEL - 1, D), jnp.float32), rounded(mixer_input)])
    mixer_output = jnp.zeros((TOKENS, D), jnp.float32)
    for offset in range(KERNEL):
        mixer_output = mixer_output + kernel[offset] * mixer_pad[offset:offset + TOKENS]
    gate_value = jax.nn.sigmoid(mixer_output)
    swish_slope = gate_value * (1.0 + mixer_output * (1.0 - gate_value))
    mixer_grad = (upstream.astype(jnp.float32) * swish_slope).astype(jnp.bfloat16)
    grad_pad = jnp.concatenate([rounded(mixer_grad), jnp.zeros((KERNEL - 1, D), jnp.float32)])
    mixer_back = jnp.zeros((TOKENS, D), jnp.float32)
    for offset in range(KERNEL):
        mixer_back = mixer_back + kernel[offset] * grad_pad[KERNEL - 1 - offset:KERNEL - 1 - offset + TOKENS]
    total_grad = upstream.astype(jnp.float32) + mixer_back * frame_valid[:, None]
    total_low = total_grad.astype(jnp.bfloat16)
    out_grad = jnp.dot(total_low, out_weight.T, preferred_element_type=jnp.float32).astype(jnp.bfloat16)

    def backward_block(state_pair, block_index):
        key_sum, value_sum = state_pair
        block_queries, block_keys, block_values, allowed = block_pieces(block_index)
        attended_block, shares, shares_low = attend_ref(block_queries, block_keys, block_values, allowed)
        block_grad = lax.dynamic_slice_in_dim(out_grad, block_index * frames, frames)
        query_grad, key_part, value_part = attend_back_ref(block_queries, block_keys, block_values, attended_block, shares, shares_low, block_grad)
        first_row = block_index * frames
        key_now = lax.dynamic_slice_in_dim(key_sum, first_row, window_rows) + rounded(key_part)
        value_now = lax.dynamic_slice_in_dim(value_sum, first_row, window_rows) + rounded(value_part)
        key_sum = lax.dynamic_update_slice_in_dim(key_sum, key_now, first_row, 0)
        value_sum = lax.dynamic_update_slice_in_dim(value_sum, value_now, first_row, 0)
        return ((key_sum, value_sum), query_grad)
    zero_sum = jnp.zeros(((span_back + N_TM) * frames, width), jnp.float32)
    (key_sum, value_sum), query_grads = lax.scan(backward_block, (zero_sum, zero_sum), blocks)
    query_grad = query_grads.reshape(TOKENS, width)
    key_grad = key_sum[span_back * frames:].astype(jnp.bfloat16)
    value_grad = value_sum[span_back * frames:].astype(jnp.bfloat16)
    normed_grad = jnp.dot(query_grad, query_weight.T, preferred_element_type=jnp.float32)
    normed_grad = normed_grad + jnp.dot(key_grad, key_weight.T, preferred_element_type=jnp.float32)
    normed_grad = normed_grad + jnp.dot(value_grad, value_weight.T, preferred_element_type=jnp.float32)
    scaled = normed_grad * norm_scale
    norm_back = inverse * (scaled - lax.optimization_barrier(jnp.mean(scaled, axis=-1, keepdims=True)) - unit * lax.optimization_barrier(jnp.mean(scaled * unit, axis=-1, keepdims=True)))
    return (total_grad + norm_back).astype(jnp.bfloat16)

def reference(layer_inputs, top_grad, w_query, w_key, w_value, w_out, conv_kernel, norm_gain, group_valid):
    frame_valid = frame_mask(group_valid)
    span_back = -(-(LEFT * GROUP) // TOK_DEV)
    key_valid = jnp.concatenate([jnp.zeros((span_back * TOK_DEV,), jnp.float32), frame_valid])
    upstream = top_grad
    collected = []
    for layer_number in range(LAYERS - 1, -1, -1):
        upstream = layer_grad(layer_inputs[layer_number], upstream, w_query[layer_number], w_key[layer_number], w_value[layer_number], w_out[layer_number], conv_kernel[layer_number], norm_gain[layer_number], frame_valid, key_valid)
        collected.append(upstream)
    return jnp.stack(collected[::-1])
```

```python
import functools

import jax
import jax.numpy as jnp
from jax import lax
from jax.experimental import pallas as pl
from jax.experimental.pallas import tpu as pltpu
from jax.sharding import PartitionSpec as P

HEAD_DIM = 64
PAIR = 128
ROWS = 128
LEFT = 4
EDGE = 32
SCALE = HEAD_DIM ** (-0.5)
NEGATIVE = -1e30
EPSILON = 1e-05
F32 = jnp.float32
BF16 = jnp.bfloat16
VMEM_LIMIT = 56 * 1024 * 1024


def dot_nn(a, b):
    return lax.dot_general(a, b, (((1,), (0,)), ((), ())), preferred_element_type=F32)


def dot_nt(a, b):
    return lax.dot_general(a, b, (((1,), (1,)), ((), ())), preferred_element_type=F32)


def valid_count(valid_ref, block):
    groups = valid_ref.shape[0]
    inside = (block >= 0) & (block < groups)
    return jnp.where(inside, valid_ref[jnp.clip(block, 0, groups - 1)], 0)


def even_half(rows):
    return lax.broadcasted_iota(jnp.int32, (rows, PAIR), 1) < HEAD_DIM


def unit_rows(values):
    center = values - jnp.mean(values, axis=-1, keepdims=True)
    spread = jnp.mean(center * center, axis=-1, keepdims=True)
    inverse = lax.rsqrt(spread + EPSILON)
    return center * inverse, inverse


def three_parts(value):
    first = value.astype(BF16)
    rest = value - first.astype(F32)
    second = rest.astype(BF16)
    third = (rest - second.astype(F32)).astype(BF16)
    return first, second, third


def shift_rows(value, amount):
    if amount == 0:
        return value
    return pltpu.roll(value, value.shape[0] - amount, 0)


def tap_sum(padded, kernel_ref, lanes, first, step, rows):
    taps = kernel_ref.shape[0]
    total = jnp.zeros((rows, padded.shape[1]), F32)
    for phase in range(8):
        moved = None
        for tap in range(taps):
            offset = first + step * tap
            if offset % 8 != phase:
                continue
            if moved is None:
                moved = shift_rows(padded, phase)
            base = offset - phase
            total = total + kernel_ref[tap : tap + 1, lanes] * moved[base : base + rows]
    return total


def forward_kernel(
    valid_ref,
    own_ref,
    back2_ref,
    back4_ref,
    back5_ref,
    next2_ref,
    next4_ref,
    peer_ref,
    peer_back2_ref,
    peer_back4_ref,
    peer_next2_ref,
    peer_next4_ref,
    w_query_ref,
    w_key_ref,
    w_value_ref,
    w_out_ref,
    kernel_ref,
    gain_ref,
    slope_ref,
    queries_ref,
    keys_ref,
    values_ref,
    attended_ref,
    log_ref,
    normed,
    key_all,
    value_all,
    query_all,
    attended_all,
    mixed,
):
    place = lax.axis_index("tm")
    odd = lax.rem(place, 2) == 1
    sources = (
        (peer_back4_ref, back5_ref),
        (back4_ref, back4_ref),
        (peer_back2_ref, peer_back4_ref),
        (back2_ref, back2_ref),
        (peer_ref, peer_back2_ref),
        (own_ref, own_ref),
        (peer_next2_ref, peer_ref),
        (next2_ref, next2_ref),
        (peer_next4_ref, peer_next2_ref),
        (next4_ref, next4_ref),
    )
    chunk = 16
    gain = gain_ref[...]

    def block_rows(index, rows):
        when_odd, when_even = sources[index]
        if when_odd is when_even:
            return when_odd[rows, :].astype(F32)
        return jnp.where(odd, when_odd[rows, :].astype(F32), when_even[rows, :].astype(F32))

    for index in range(len(sources)):

        def norm_step(step, carry, index=index):
            row = pl.multiple_of(step * chunk, chunk)
            unit, _ = unit_rows(block_rows(index, pl.ds(row, chunk)))
            normed[pl.ds(pl.multiple_of(index * ROWS + row, chunk), chunk), :] = (unit * gain).astype(BF16)
            return carry

        lax.fori_loop(0, ROWS // chunk, norm_step, 0, unroll=2)

    key_rows = 7 * ROWS
    lane_even = lax.rem(lax.broadcasted_iota(jnp.int32, (ROWS, w_key_ref.shape[1]), 1), PAIR) < HEAD_DIM
    zero = jnp.zeros((ROWS, w_key_ref.shape[1]), F32)
    keys = dot_nn(normed[0:key_rows, :], w_key_ref[...])
    for block in range(7):
        part = keys[block * ROWS : (block + 1) * ROWS]
        key_all[0, block * ROWS : (block + 1) * ROWS, :] = jnp.where(lane_even, part, zero).astype(BF16)
        key_all[1, block * ROWS : (block + 1) * ROWS, :] = jnp.where(lane_even, zero, part).astype(BF16)
        if 1 <= block <= 5:
            keys_ref[(block - 1) * ROWS : block * ROWS, :] = part.astype(BF16)
    values = dot_nn(normed[0:key_rows, :], w_value_ref[...])
    for block in range(7):
        part = values[block * ROWS : (block + 1) * ROWS]
        value_all[0, block * ROWS : (block + 1) * ROWS, :] = jnp.where(lane_even, part, zero).astype(BF16)
        value_all[1, block * ROWS : (block + 1) * ROWS, :] = jnp.where(lane_even, zero, part).astype(BF16)
        if 1 <= block <= 5:
            values_ref[(block - 1) * ROWS : block * ROWS, :] = part.astype(BF16)
    query_first = 5 * ROWS - EDGE
    query_all[...] = dot_nn(normed[query_first:, :], w_query_ref[...]).astype(BF16)
    queries_ref[...] = query_all[EDGE:, :]

    counts = [valid_count(valid_ref, place + block - 5) for block in range(7)]
    key_lane = lax.broadcasted_iota(jnp.int32, (1, ROWS), 1)
    allowed = jnp.concatenate([key_lane < count for count in counts], axis=1)
    span = (LEFT + 1) * ROWS
    groups = (
        (0, EDGE, 0),
        (EDGE, EDGE + ROWS, ROWS),
        (EDGE + ROWS, 2 * EDGE + ROWS, 2 * ROWS),
    )
    log_lane = lax.broadcasted_iota(jnp.int32, (ROWS, PAIR), 1)
    logs = jnp.zeros((ROWS, PAIR), F32)
    query_rows = ROWS + 2 * EDGE
    for pair in range(w_key_ref.shape[1] // PAIR):
        lanes = slice(pair * PAIR, (pair + 1) * PAIR)
        query_pair = query_all[0:query_rows, lanes]
        scores = [dot_nt(query_pair, key_all[half, :, lanes]) * SCALE for half in range(2)]
        for low, high, first in groups:
            total = None
            for half in range(2):
                part = jnp.where(
                    allowed[:, first : first + span],
                    scores[half][low:high, first : first + span],
                    NEGATIVE,
                )
                highest = jnp.max(part, axis=-1, keepdims=True)
                exped = jnp.exp(part - highest)
                summed = jnp.sum(exped, axis=-1, keepdims=True)
                shares_low = (exped * (1.0 / summed)).astype(BF16)
                product = dot_nn(shares_low, value_all[half, first : first + span, lanes])
                total = product if total is None else total + product
                if low == EDGE:
                    logs = jnp.where(log_lane == 2 * pair + half, highest + jnp.log(summed), logs)
            attended_all[low:high, lanes] = total.astype(BF16)
    log_ref[...] = logs
    attended_ref[...] = attended_all[EDGE : EDGE + ROWS, :]

    projected = dot_nn(attended_all[...], w_out_ref[...])
    row_ids = lax.broadcasted_iota(jnp.int32, (ROWS, 1), 0)
    edge_ids = lax.broadcasted_iota(jnp.int32, (EDGE, 1), 0)
    before = projected[0:EDGE] + block_rows(4, slice(ROWS - EDGE, ROWS))
    here = projected[EDGE : EDGE + ROWS] + own_ref[...].astype(F32)
    after = projected[EDGE + ROWS :] + block_rows(6, slice(0, EDGE))
    mixed[0:EDGE, :] = jnp.where(edge_ids + (ROWS - EDGE) < counts[4], before, 0.0).astype(BF16).astype(F32)
    mixed[EDGE : EDGE + ROWS, :] = jnp.where(row_ids < counts[5], here, 0.0).astype(BF16).astype(F32)
    mixed[EDGE + ROWS :, :] = jnp.where(edge_ids < counts[6], after, 0.0).astype(BF16).astype(F32)

    taps = kernel_ref.shape[0]

    def conv_step(step, carry):
        lanes = pl.ds(pl.multiple_of(step * PAIR, PAIR), PAIR)
        output = tap_sum(mixed[:, lanes], kernel_ref, lanes, EDGE - (taps - 1), 1, ROWS + EDGE)
        gate = 1.0 / (1.0 + jnp.exp(-output))
        slope_ref[:, lanes] = gate * (1.0 + output * (1.0 - gate))
        return carry

    lax.fori_loop(0, own_ref.shape[1] // PAIR, conv_step, 0)


def mixer_kernel(
    valid_ref,
    upstream_ref,
    next_ref,
    slope_ref,
    kernel_ref,
    w_out_ref,
    attended_ref,
    log_ref,
    total_ref,
    message_ref,
    dot_ref,
    total_low,
):
    place = lax.axis_index("tm")
    count = valid_count(valid_ref, place)
    row_ids = lax.broadcasted_iota(jnp.int32, (ROWS, PAIR), 0)
    taps = kernel_ref.shape[0]

    def conv_step(step, carry):
        lanes = pl.ds(pl.multiple_of(step * PAIR, PAIR), PAIR)
        upper = upstream_ref[:, lanes].astype(F32)
        stacked = jnp.concatenate([upper, next_ref[:, lanes].astype(F32)], axis=0)
        grads = (stacked * slope_ref[:, lanes]).astype(BF16).astype(F32)
        back = tap_sum(grads, kernel_ref, lanes, taps - 1, -1, ROWS)
        total = upper + jnp.where(row_ids < count, back, 0.0)
        total_ref[:, lanes] = total
        total_low[:, lanes] = total.astype(BF16)
        return carry

    lax.fori_loop(0, upstream_ref.shape[1] // PAIR, conv_step, 0)
    out_grad = dot_nt(total_low[...], w_out_ref[...]).astype(BF16)
    message_ref[0:ROWS, :] = out_grad
    product = out_grad.astype(F32) * attended_ref[...].astype(F32)
    high = product.astype(BF16)
    low = (product - high.astype(F32)).astype(BF16)
    width = product.shape[1]
    head_of = lax.broadcasted_iota(jnp.int32, (PAIR, width), 1) // HEAD_DIM
    chosen = (head_of == lax.broadcasted_iota(jnp.int32, (PAIR, width), 0)).astype(F32).astype(BF16)
    dots = dot_nt(high, chosen) + dot_nt(low, chosen)
    dot_ref[...] = dots
    stacked = jnp.concatenate([log_ref[...].T[0:8], dots.T[0:8]], axis=0)
    message_ref[ROWS : ROWS + 16, :] = jnp.zeros((16, width), BF16)
    for index, part in enumerate(three_parts(stacked)):
        message_ref[ROWS : ROWS + 16, index * PAIR : (index + 1) * PAIR] = part


def query_kernel(
    valid_ref,
    queries_ref,
    keys_ref,
    values_ref,
    message_ref,
    log_ref,
    dot_ref,
    w_query_ref,
    out_ref,
    query_grad,
):
    place = lax.axis_index("tm")
    key_lane = lax.broadcasted_iota(jnp.int32, (1, ROWS), 1)
    allowed = jnp.concatenate(
        [key_lane < valid_count(valid_ref, place + block - LEFT) for block in range(LEFT + 1)], axis=1
    )
    span = (LEFT + 1) * ROWS
    halves = even_half(span)
    nothing = jnp.zeros((span, PAIR), BF16)
    for pair in range(keys_ref.shape[1] // PAIR):
        lanes = slice(pair * PAIR, (pair + 1) * PAIR)
        query_pair = queries_ref[:, lanes]
        grad_pair = message_ref[0:ROWS, lanes]
        key_pair = keys_ref[:, lanes]
        value_pair = values_ref[:, lanes]
        total = None
        for half in range(2):
            keep = halves if half == 0 else jnp.logical_not(halves)
            key_half = jnp.where(keep, key_pair, nothing)
            value_half = jnp.where(keep, value_pair, nothing)
            head = 2 * pair + half
            scores = dot_nt(query_pair, key_half) * SCALE
            shares = jnp.exp(jnp.where(allowed, scores, NEGATIVE) - log_ref[:, head : head + 1])
            share_grad = dot_nt(grad_pair, value_half)
            score_grad = (shares * (share_grad - dot_ref[:, head : head + 1])).astype(BF16)
            product = dot_nn(score_grad, key_half)
            total = product if total is None else total + product
        query_grad[:, lanes] = (total * SCALE).astype(BF16)
    out_ref[...] = dot_nt(query_grad[...], w_query_ref[...])


def key_kernel(
    valid_ref,
    queries_ref,
    keys_ref,
    values_ref,
    message_ref,
    next2_ref,
    next4_ref,
    peer_ref,
    peer_next2_ref,
    peer_next4_ref,
    w_key_ref,
    w_value_ref,
    gain_ref,
    own_ref,
    total_ref,
    partial_ref,
    out_ref,
    grads,
    stats,
    key_grad,
    value_grad,
):
    place = lax.axis_index("tm")
    odd = lax.rem(place, 2) == 1
    count = valid_count(valid_ref, place)
    sources = (
        (message_ref, message_ref),
        (peer_next2_ref, peer_ref),
        (next2_ref, next2_ref),
        (peer_next4_ref, peer_next2_ref),
        (next4_ref, next4_ref),
    )
    for block, (when_odd, when_even) in enumerate(sources):
        if when_odd is when_even:
            part = when_odd[...]
        else:
            part = jnp.where(odd, when_odd[...].astype(F32), when_even[...].astype(F32)).astype(BF16)
        grads[block * ROWS : (block + 1) * ROWS, :] = part[0:ROWS]
        tail = part[ROWS : ROWS + 16].astype(F32)
        stats[:, block * ROWS : (block + 1) * ROWS] = (
            tail[:, 0:PAIR] + tail[:, PAIR : 2 * PAIR] + tail[:, 2 * PAIR : 3 * PAIR]
        )
    span = (LEFT + 1) * ROWS
    halves = even_half(span)
    nothing = jnp.zeros((span, PAIR), BF16)
    key_valid = lax.broadcasted_iota(jnp.int32, (ROWS, span), 0) < count
    for pair in range(keys_ref.shape[1] // PAIR):
        lanes = slice(pair * PAIR, (pair + 1) * PAIR)
        key_pair = keys_ref[span - ROWS : span, lanes]
        value_pair = values_ref[span - ROWS : span, lanes]
        query_pair = queries_ref[:, lanes]
        grad_pair = grads[:, lanes]
        query_halves = []
        grad_halves = []
        share_halves = []
        score_halves = []
        for half in range(2):
            keep = halves if half == 0 else jnp.logical_not(halves)
            query_half = jnp.where(keep, query_pair, nothing)
            grad_half = jnp.where(keep, grad_pair, nothing)
            head = 2 * pair + half
            scores = dot_nt(key_pair, query_half) * SCALE
            shares = jnp.exp(jnp.where(key_valid, scores, NEGATIVE) - stats[head : head + 1, :])
            share_grad = dot_nt(value_pair, grad_half)
            score_grad = (shares * (share_grad - stats[8 + head : 9 + head, :])).astype(BF16)
            query_halves.append(query_half)
            grad_halves.append(grad_half)
            share_halves.append(shares.astype(BF16))
            score_halves.append(score_grad)
        key_sum = None
        value_sum = None
        for block in range(LEFT + 1):
            rows = slice(block * ROWS, (block + 1) * ROWS)
            key_term = dot_nn(
                jnp.concatenate([score_halves[0][:, rows], score_halves[1][:, rows]], axis=1),
                jnp.concatenate([query_halves[0][rows], query_halves[1][rows]], axis=0),
            )
            value_term = dot_nn(
                jnp.concatenate([share_halves[0][:, rows], share_halves[1][:, rows]], axis=1),
                jnp.concatenate([grad_halves[0][rows], grad_halves[1][rows]], axis=0),
            )
            key_term = (key_term * SCALE).astype(BF16).astype(F32)
            value_term = value_term.astype(BF16).astype(F32)
            key_sum = key_term if key_sum is None else key_sum + key_term
            value_sum = value_term if value_sum is None else value_sum + value_term
        key_grad[:, lanes] = key_sum.astype(BF16)
        value_grad[:, lanes] = value_sum.astype(BF16)
    normed_grad = partial_ref[...] + dot_nt(key_grad[...], w_key_ref[...])
    normed_grad = normed_grad + dot_nt(value_grad[...], w_value_ref[...])
    scaled = normed_grad * gain_ref[...]
    unit, inverse = unit_rows(own_ref[...].astype(F32))
    back = inverse * (
        scaled
        - jnp.mean(scaled, axis=-1, keepdims=True)
        - unit * jnp.mean(scaled * unit, axis=-1, keepdims=True)
    )
    out_ref[...] = (total_ref[...] + back).astype(BF16)


def call(kernel, name, n_inputs, outs, scratch, flops):
    vmem = pl.BlockSpec(memory_space=pltpu.VMEM)
    return pl.pallas_call(
        kernel,
        name=name,
        in_specs=[pl.BlockSpec(memory_space=pltpu.SMEM)] + [vmem] * (n_inputs - 1),
        out_specs=[vmem] * len(outs),
        out_shape=[jax.ShapeDtypeStruct(shape, dtype) for shape, dtype in outs],
        scratch_shapes=[pltpu.VMEM(shape, dtype) for shape, dtype in scratch],
        compiler_params=pltpu.CompilerParams(vmem_limit_bytes=VMEM_LIMIT),
        cost_estimate=pl.CostEstimate(flops=flops, bytes_accessed=4 << 20, transcendentals=0),
    )


def shards(
    layer_inputs, top_grad, w_query, w_key, w_value, w_out, conv_kernel, norm_gain, group_valid
):
    own = layer_inputs[0]
    width = own.shape[1]
    heads_width = w_query.shape[2]
    query_weight = w_query[0]
    key_weight = w_key[0]
    value_weight = w_value[0]
    out_weight = w_out[0]
    kernel = conv_kernel[0]
    sections = lax.axis_size("section")
    count = lax.axis_size("tm")
    section_index = lax.axis_index("section")
    place = lax.axis_index("tm")
    odd = lax.rem(place, 2) == 1

    def at(layer, frame):
        return frame * sections + layer

    def moved(value, pairs):
        return lax.ppermute(value, ("tm", "section"), pairs)

    def across(steps, chosen):
        return [
            (at(section, source), at(section, source + steps))
            for section in chosen
            for source in range(max(0, -steps), min(count, count - steps))
        ]

    def swapped(chosen):
        return [
            (at(section, source), at(section, source ^ 1))
            for section in chosen
            for source in range(count)
        ]

    every = range(sections)
    next2 = moved(own, across(-2, every))
    back2 = moved(own, across(2, every))
    back4 = moved(own, across(4, every))
    next4 = moved(own, across(-4, every))
    mixed_pairs = []
    for section in every:
        for source in range(1, count - 5, 2):
            mixed_pairs.append((at(section, source), at(section, source + 5)))
        for source in range(2, count, 2):
            mixed_pairs.append((at(section, source), at(section, source - 1)))
    back5 = moved(jnp.where(odd, own, top_grad), mixed_pairs)
    swap = swapped(every)
    peer = moved(own, swap)
    peer_top = moved(top_grad[:EDGE], swap)
    peer_back2 = moved(back2, swap)
    peer_back4 = moved(back4, swap)
    peer_next2 = moved(next2, swap)
    peer_next4 = moved(next4, swap)
    top_next = jnp.where(odd, back5[:EDGE], peer_top)

    span = (LEFT + 1) * ROWS
    slope, queries, keys, values, attended, logs = call(
        forward_kernel,
        "forward",
        18,
        [
            ((ROWS + EDGE, width), F32),
            ((span, heads_width), BF16),
            ((span, heads_width), BF16),
            ((span, heads_width), BF16),
            ((ROWS, heads_width), BF16),
            ((ROWS, PAIR), F32),
        ],
        [
            ((10 * ROWS, width), BF16),
            ((2, 7 * ROWS, heads_width), BF16),
            ((2, 7 * ROWS, heads_width), BF16),
            ((span + EDGE, heads_width), BF16),
            ((ROWS + 2 * EDGE, heads_width), BF16),
            ((ROWS + 2 * EDGE, width), F32),
        ],
        4 << 30,
    )(
        group_valid,
        own,
        back2,
        back4,
        back5,
        next2,
        next4,
        peer,
        peer_back2,
        peer_back4,
        peer_next2,
        peer_next4,
        query_weight,
        key_weight,
        value_weight,
        out_weight,
        kernel,
        norm_gain,
    )

    upstream = top_grad
    upstream_next = top_next
    result = None
    for step in range(sections):
        layer = sections - 1 - step
        total, message, dots = call(
            mixer_kernel,
            "mixer",
            8,
            [((ROWS, width), F32), ((ROWS + 16, heads_width), BF16), ((ROWS, PAIR), F32)],
            [((ROWS, width), BF16)],
            1 << 30,
        )(group_valid, upstream, upstream_next, slope, kernel, out_weight, attended, logs)
        here = [layer]
        step_swap = swapped(here)
        grad2 = moved(message, across(-2, here))
        grad4 = moved(message, across(-4, here))
        peer_grad = moved(message, step_swap)
        peer_grad2 = moved(grad2, step_swap)
        peer_grad4 = moved(grad4, step_swap)
        (partial,) = call(
            query_kernel,
            "own_queries",
            8,
            [((ROWS, width), F32)],
            [((ROWS, heads_width), BF16)],
            1 << 30,
        )(group_valid, queries[:ROWS], keys, values, message, logs, dots, query_weight)
        (input_grad,) = call(
            key_kernel,
            "own_keys",
            16,
            [((ROWS, width), BF16)],
            [
                ((span, heads_width), BF16),
                ((16, span), F32),
                ((ROWS, heads_width), BF16),
                ((ROWS, heads_width), BF16),
            ],
            1 << 30,
        )(
            group_valid,
            queries,
            keys,
            values,
            message,
            grad2,
            grad4,
            peer_grad,
            peer_grad2,
            peer_grad4,
            key_weight,
            value_weight,
            norm_gain,
            own,
            total,
            partial,
        )
        result = input_grad if result is None else jnp.where(section_index == layer, input_grad, result)
        if layer > 0:
            upstream = moved(
                input_grad,
                [(at(layer, source), at(layer - 1, source)) for source in range(count)],
            )
            upstream_next = moved(
                input_grad[:EDGE],
                [(at(layer, source), at(layer - 1, source - 1)) for source in range(1, count)],
            )
    return result[None]


def solution(mesh):
    placed = (
        P("section", "tm", None),
        P("tm", None),
        P("section", None, None),
        P("section", None, None),
        P("section", None, None),
        P("section", None, None),
        P("section", None, None),
        P("section", None),
        P(),
    )
    return jax.shard_map(
        shards, mesh=mesh, in_specs=placed, out_specs=P("section", "tm", None), check_vma=False
    )
```

```python
import jax
import jax.numpy as jnp
from jax import lax
from jax.experimental import pallas as pl
from jax.experimental.pallas import tpu as pltpu
from jax.sharding import PartitionSpec as P

HEAD_DIM = 64
PAIR = 128
ROWS = 128
LEFT = 4
EDGE = 32
SCALE = HEAD_DIM ** (-0.5)
NEGATIVE = -1e30
EPSILON = 1e-05
F32 = jnp.float32
BF16 = jnp.bfloat16
VMEM_LIMIT = 56 * 1024 * 1024


def dot_nn(a, b):
    return lax.dot_general(a, b, (((1,), (0,)), ((), ())), preferred_element_type=F32)


def dot_nt(a, b):
    return lax.dot_general(a, b, (((1,), (1,)), ((), ())), preferred_element_type=F32)


def valid_count(valid_ref, block):
    groups = valid_ref.shape[0]
    inside = (block >= 0) & (block < groups)
    return jnp.where(inside, valid_ref[jnp.clip(block, 0, groups - 1)], 0)


def even_half(rows):
    return lax.broadcasted_iota(jnp.int32, (rows, PAIR), 1) < HEAD_DIM


def unit_rows(values):
    center = values - jnp.mean(values, axis=-1, keepdims=True)
    spread = jnp.mean(center * center, axis=-1, keepdims=True)
    inverse = lax.rsqrt(spread + EPSILON)
    return center * inverse, inverse


def three_parts(value):
    first = value.astype(BF16)
    rest = value - first.astype(F32)
    second = rest.astype(BF16)
    third = (rest - second.astype(F32)).astype(BF16)
    return first, second, third


def shift_rows(value, amount):
    if amount == 0:
        return value
    return pltpu.roll(value, value.shape[0] - amount, 0)


def tap_sum(padded, kernel_ref, lanes, first, step, rows):
    taps = kernel_ref.shape[0]
    total = jnp.zeros((rows, padded.shape[1]), F32)
    for phase in range(8):
        moved = None
        for tap in range(taps):
            offset = first + step * tap
            if offset % 8 != phase:
                continue
            if moved is None:
                moved = shift_rows(padded, phase)
            base = offset - phase
            total = total + kernel_ref[tap : tap + 1, lanes] * moved[base : base + rows]
    return total


def project_kernel(
    own_ref,
    top_ref,
    gain_ref,
    w_query_ref,
    w_key_ref,
    w_value_ref,
    queries_ref,
    kept_ref,
    ahead_ref,
    behind_ref,
    normed,
):
    chunk = 16

    def norm_step(step, carry):
        rows = pl.ds(pl.multiple_of(step * chunk, chunk), chunk)
        unit, _ = unit_rows(own_ref[rows, :].astype(F32))
        normed[rows, :] = (unit * gain_ref[...]).astype(BF16)
        return carry

    lax.fori_loop(0, ROWS // chunk, norm_step, 0, unroll=2)
    wide = w_key_ref.shape[1]
    half = EDGE // 2
    keys = dot_nn(normed[...], w_key_ref[...]).astype(BF16)
    values = dot_nn(normed[...], w_value_ref[...]).astype(BF16)
    for ref in (kept_ref, ahead_ref, behind_ref):
        ref[0:ROWS, 0:wide] = keys
        ref[0:ROWS, wide : 2 * wide] = values
    queries = dot_nn(normed[...], w_query_ref[...]).astype(BF16)
    queries_ref[...] = queries
    ahead_ref[ROWS : ROWS + EDGE, :] = own_ref[ROWS - EDGE : ROWS, :]
    ahead_ref[ROWS + EDGE : ROWS + EDGE + half, 0:wide] = queries[ROWS - EDGE : ROWS - half]
    ahead_ref[ROWS + EDGE : ROWS + EDGE + half, wide : 2 * wide] = queries[ROWS - half : ROWS]
    behind_ref[ROWS : ROWS + EDGE, :] = own_ref[0:EDGE, :]
    behind_ref[ROWS + EDGE : ROWS + EDGE + half, 0:wide] = queries[0:half]
    behind_ref[ROWS + EDGE : ROWS + EDGE + half, wide : 2 * wide] = queries[half:EDGE]
    behind_ref[ROWS + EDGE + half : ROWS + 2 * EDGE + half, :] = top_ref[0:EDGE, :]


def chosen_rows(odd, when_odd, when_even, rows):
    if when_odd is when_even:
        return when_odd[rows, :]
    return jnp.where(odd, when_odd[rows, :].astype(F32), when_even[rows, :].astype(F32)).astype(BF16)


def gather_window(odd, sources, window):
    for index, (when_odd, when_even) in enumerate(sources):
        window[index * ROWS : (index + 1) * ROWS, :] = chosen_rows(odd, when_odd, when_even, slice(0, ROWS))


def masked_half(value, half):
    keep = even_half(value.shape[0])
    if half:
        keep = jnp.logical_not(keep)
    return jnp.where(keep, value, jnp.zeros_like(value))


def pair_shares(scores, allowed):
    part = jnp.where(allowed, scores, NEGATIVE)
    highest = jnp.max(part, axis=-1, keepdims=True)
    exped = jnp.exp(part - highest)
    summed = jnp.sum(exped, axis=-1, keepdims=True)
    return (exped * (1.0 / summed)).astype(BF16), highest, summed


def attend_kernel(
    valid_ref,
    queries_ref,
    kept_ref,
    back2_ref,
    back4_ref,
    peer_ref,
    peer_back2_ref,
    peer_back4_ref,
    after_ref,
    attended_ref,
    log_ref,
    window,
    query_all,
):
    place = lax.axis_index("tm")
    odd = lax.rem(place, 2) == 1
    wide = queries_ref.shape[1]
    half_edge = EDGE // 2
    gather_window(
        odd,
        (
            (back4_ref, back4_ref),
            (peer_back2_ref, peer_back4_ref),
            (back2_ref, back2_ref),
            (peer_ref, peer_back2_ref),
            (kept_ref, kept_ref),
            (after_ref, after_ref),
        ),
        window,
    )
    query_all[0:ROWS, :] = queries_ref[...]
    query_all[ROWS : ROWS + half_edge, :] = after_ref[ROWS + EDGE : ROWS + EDGE + half_edge, 0:wide]
    query_all[ROWS + half_edge : ROWS + EDGE, :] = after_ref[
        ROWS + EDGE : ROWS + EDGE + half_edge, wide : 2 * wide
    ]
    key_lane = lax.broadcasted_iota(jnp.int32, (1, ROWS), 1)
    allowed = jnp.concatenate(
        [key_lane < valid_count(valid_ref, place + block - LEFT) for block in range(LEFT + 2)], axis=1
    )
    span = (LEFT + 1) * ROWS
    log_lane = lax.broadcasted_iota(jnp.int32, (ROWS, PAIR), 1)
    logs = jnp.zeros((ROWS, PAIR), F32)
    for pair in range(wide // PAIR):
        lanes = slice(pair * PAIR, (pair + 1) * PAIR)
        value_lanes = slice(wide + pair * PAIR, wide + (pair + 1) * PAIR)
        totals = [None, None]
        for half in range(2):
            scores = dot_nt(query_all[:, lanes], masked_half(window[:, lanes], half)) * SCALE
            value_half = masked_half(window[:, value_lanes], half)
            for group, (low, high, first) in enumerate(((0, ROWS, 0), (ROWS, ROWS + EDGE, ROWS))):
                shares_low, highest, summed = pair_shares(
                    scores[low:high, first : first + span], allowed[:, first : first + span]
                )
                product = dot_nn(shares_low, value_half[first : first + span])
                totals[group] = product if totals[group] is None else totals[group] + product
                if group == 0:
                    logs = jnp.where(log_lane == 2 * pair + half, highest + jnp.log(summed), logs)
        attended_ref[0:ROWS, lanes] = totals[0].astype(BF16)
        attended_ref[ROWS : ROWS + EDGE, lanes] = totals[1].astype(BF16)
    log_ref[...] = logs


def mixer_body(
    count, upstream_ref, next_rows, slope_ref, kernel_ref, w_out_ref, attended, log_ref, total_ref, message_ref, dot_ref, total_low
):
    row_ids = lax.broadcasted_iota(jnp.int32, (ROWS, PAIR), 0)
    taps = kernel_ref.shape[0]

    def conv_step(step, carry):
        lanes = pl.ds(pl.multiple_of(step * PAIR, PAIR), PAIR)
        upper = upstream_ref[:, lanes].astype(F32)
        stacked = jnp.concatenate([upper, next_rows(lanes)], axis=0)
        grads = (stacked * slope_ref[:, lanes]).astype(BF16).astype(F32)
        back = tap_sum(grads, kernel_ref, lanes, taps - 1, -1, ROWS)
        total = upper + jnp.where(row_ids < count, back, 0.0)
        total_ref[:, lanes] = total
        total_low[:, lanes] = total.astype(BF16)
        return carry

    lax.fori_loop(0, upstream_ref.shape[1] // PAIR, conv_step, 0)
    out_grad = dot_nt(total_low[...], w_out_ref[...]).astype(BF16)
    message_ref[0:ROWS, :] = out_grad
    product = out_grad.astype(F32) * attended.astype(F32)
    high = product.astype(BF16)
    low = (product - high.astype(F32)).astype(BF16)
    width = product.shape[1]
    head_of = lax.broadcasted_iota(jnp.int32, (PAIR, width), 1) // HEAD_DIM
    chosen = (head_of == lax.broadcasted_iota(jnp.int32, (PAIR, width), 0)).astype(F32).astype(BF16)
    dots = dot_nt(high, chosen) + dot_nt(low, chosen)
    dot_ref[...] = dots
    stacked = jnp.concatenate([log_ref[...].T[0:8], dots.T[0:8]], axis=0)
    message_ref[ROWS : ROWS + 16, :] = jnp.zeros((16, width), BF16)
    for index, part in enumerate(three_parts(stacked)):
        message_ref[ROWS : ROWS + 16, index * PAIR : (index + 1) * PAIR] = part


def mix_kernel(
    valid_ref,
    own_ref,
    top_ref,
    attended_ref,
    log_ref,
    back2_ref,
    back4_ref,
    back5_ref,
    peer_ref,
    peer_back2_ref,
    peer_back4_ref,
    after_ref,
    w_out_ref,
    kernel_ref,
    slope_ref,
    total_ref,
    message_ref,
    dot_ref,
    window,
    query_tail,
    attended_all,
    mixed,
    total_low,
):
    place = lax.axis_index("tm")
    odd = lax.rem(place, 2) == 1
    wide = attended_ref.shape[1]
    half_edge = EDGE // 2
    counts = [valid_count(valid_ref, place + block - LEFT - 1) for block in range(LEFT + 3)]
    gather_window(
        odd,
        (
            (peer_back4_ref, back5_ref),
            (back4_ref, back4_ref),
            (peer_back2_ref, peer_back4_ref),
            (back2_ref, back2_ref),
            (peer_ref, peer_back2_ref),
        ),
        window,
    )
    packed = chosen_rows(odd, peer_ref, peer_back2_ref, slice(ROWS + EDGE, ROWS + EDGE + half_edge))
    query_tail[0:half_edge, :] = packed[:, 0:wide]
    query_tail[half_edge:EDGE, :] = packed[:, wide : 2 * wide]
    key_lane = lax.broadcasted_iota(jnp.int32, (1, ROWS), 1)
    allowed = jnp.concatenate([key_lane < count for count in counts[: LEFT + 1]], axis=1)
    for pair in range(wide // PAIR):
        lanes = slice(pair * PAIR, (pair + 1) * PAIR)
        value_lanes = slice(wide + pair * PAIR, wide + (pair + 1) * PAIR)
        total = None
        for half in range(2):
            scores = dot_nt(query_tail[:, lanes], masked_half(window[:, lanes], half)) * SCALE
            shares_low, _, _ = pair_shares(scores, allowed)
            product = dot_nn(shares_low, masked_half(window[:, value_lanes], half))
            total = product if total is None else total + product
        attended_all[0:EDGE, lanes] = total.astype(BF16)
    attended_all[EDGE:, :] = attended_ref[...]

    projected = dot_nn(attended_all[...], w_out_ref[...])
    row_ids = lax.broadcasted_iota(jnp.int32, (ROWS, 1), 0)
    edge_ids = lax.broadcasted_iota(jnp.int32, (EDGE, 1), 0)
    x_before = chosen_rows(odd, peer_ref, peer_back2_ref, slice(ROWS, ROWS + EDGE)).astype(F32)
    before = projected[0:EDGE] + x_before
    here = projected[EDGE : EDGE + ROWS] + own_ref[...].astype(F32)
    after = projected[EDGE + ROWS :] + after_ref[ROWS : ROWS + EDGE, :].astype(F32)
    before = jnp.where(edge_ids + (ROWS - EDGE) < counts[LEFT], before, 0.0)
    here = jnp.where(row_ids < counts[LEFT + 1], here, 0.0)
    after = jnp.where(edge_ids < counts[LEFT + 2], after, 0.0)
    mixed[0:EDGE, :] = before.astype(BF16).astype(F32)
    mixed[EDGE : EDGE + ROWS, :] = here.astype(BF16).astype(F32)
    mixed[EDGE + ROWS :, :] = after.astype(BF16).astype(F32)
    taps = kernel_ref.shape[0]

    def conv_step(step, carry):
        lanes = pl.ds(pl.multiple_of(step * PAIR, PAIR), PAIR)
        output = tap_sum(mixed[:, lanes], kernel_ref, lanes, EDGE - (taps - 1), 1, ROWS + EDGE)
        gate = 1.0 / (1.0 + jnp.exp(-output))
        slope_ref[:, lanes] = gate * (1.0 + output * (1.0 - gate))
        return carry

    lax.fori_loop(0, own_ref.shape[1] // PAIR, conv_step, 0)
    first = ROWS + EDGE + half_edge
    mixer_body(
        counts[LEFT + 1],
        top_ref,
        lambda lanes: after_ref[first : first + EDGE, lanes].astype(F32),
        slope_ref,
        kernel_ref,
        w_out_ref,
        attended_ref[0:ROWS, :],
        log_ref,
        total_ref,
        message_ref,
        dot_ref,
        total_low,
    )


def mixer_kernel(
    valid_ref,
    upstream_ref,
    next_ref,
    slope_ref,
    kernel_ref,
    w_out_ref,
    attended_ref,
    log_ref,
    total_ref,
    message_ref,
    dot_ref,
    total_low,
):
    mixer_body(
        valid_count(valid_ref, lax.axis_index("tm")),
        upstream_ref,
        lambda lanes: next_ref[:, lanes].astype(F32),
        slope_ref,
        kernel_ref,
        w_out_ref,
        attended_ref[0:ROWS, :],
        log_ref,
        total_ref,
        message_ref,
        dot_ref,
        total_low,
    )


def key_terms(key_pair, value_pair, query_pair, grad_pair, logs, dots, key_valid):
    share_halves = []
    score_halves = []
    query_halves = [masked_half(query_pair, half) for half in range(2)]
    grad_halves = [masked_half(grad_pair, half) for half in range(2)]
    for half in range(2):
        scores = dot_nt(key_pair, query_halves[half]) * SCALE
        shares = jnp.exp(jnp.where(key_valid, scores, NEGATIVE) - logs[half])
        share_grad = dot_nt(value_pair, grad_halves[half])
        score_halves.append((shares * (share_grad - dots[half])).astype(BF16))
        share_halves.append(shares.astype(BF16))
    key_sum = None
    value_sum = None
    for block in range(query_pair.shape[0] // ROWS):
        rows = slice(block * ROWS, (block + 1) * ROWS)
        key_term = dot_nn(
            jnp.concatenate([score[:, rows] for score in score_halves], axis=1),
            jnp.concatenate([query[rows] for query in query_halves], axis=0),
        )
        value_term = dot_nn(
            jnp.concatenate([share[:, rows] for share in share_halves], axis=1),
            jnp.concatenate([grad[rows] for grad in grad_halves], axis=0),
        )
        key_term = (key_term * SCALE).astype(BF16).astype(F32)
        value_term = value_term.astype(BF16).astype(F32)
        key_sum = key_term if key_sum is None else key_sum + key_term
        value_sum = value_term if value_sum is None else value_sum + value_term
    return key_sum, value_sum


def message_stats(tail):
    tail = tail.astype(F32)
    return tail[:, 0:PAIR] + tail[:, PAIR : 2 * PAIR] + tail[:, 2 * PAIR : 3 * PAIR]


def query_kernel(
    valid_ref,
    queries_ref,
    kept_ref,
    back2_ref,
    back4_ref,
    peer_ref,
    peer_back2_ref,
    peer_back4_ref,
    message_ref,
    log_ref,
    dot_ref,
    w_query_ref,
    out_ref,
    key_sum_ref,
    value_sum_ref,
    window,
    query_grad,
):
    place = lax.axis_index("tm")
    odd = lax.rem(place, 2) == 1
    wide = queries_ref.shape[1]
    gather_window(
        odd,
        (
            (back4_ref, back4_ref),
            (peer_back2_ref, peer_back4_ref),
            (back2_ref, back2_ref),
            (peer_ref, peer_back2_ref),
            (kept_ref, kept_ref),
        ),
        window,
    )
    key_lane = lax.broadcasted_iota(jnp.int32, (1, ROWS), 1)
    allowed = jnp.concatenate(
        [key_lane < valid_count(valid_ref, place + block - LEFT) for block in range(LEFT + 1)], axis=1
    )
    key_valid = lax.broadcasted_iota(jnp.int32, (ROWS, ROWS), 0) < valid_count(valid_ref, place)
    stats = message_stats(message_ref[ROWS : ROWS + 16, :])
    for pair in range(wide // PAIR):
        lanes = slice(pair * PAIR, (pair + 1) * PAIR)
        value_lanes = slice(wide + pair * PAIR, wide + (pair + 1) * PAIR)
        query_pair = queries_ref[:, lanes]
        grad_pair = message_ref[0:ROWS, lanes]
        total = None
        for half in range(2):
            key_half = masked_half(window[:, lanes], half)
            value_half = masked_half(window[:, value_lanes], half)
            head = 2 * pair + half
            scores = dot_nt(query_pair, key_half) * SCALE
            shares = jnp.exp(jnp.where(allowed, scores, NEGATIVE) - log_ref[:, head : head + 1])
            share_grad = dot_nt(grad_pair, value_half)
            score_grad = (shares * (share_grad - dot_ref[:, head : head + 1])).astype(BF16)
            product = dot_nn(score_grad, key_half)
            total = product if total is None else total + product
        query_grad[:, lanes] = (total * SCALE).astype(BF16)
        heads = (2 * pair, 2 * pair + 1)
        key_sum_ref[:, lanes], value_sum_ref[:, lanes] = key_terms(
            kept_ref[:, lanes],
            kept_ref[:, value_lanes],
            query_pair,
            grad_pair,
            [stats[head : head + 1] for head in heads],
            [stats[8 + head : 9 + head] for head in heads],
            key_valid,
        )
    out_ref[...] = dot_nt(query_grad[...], w_query_ref[...])


def key_kernel(
    valid_ref,
    kept_ref,
    query_next2_ref,
    query_next4_ref,
    query_peer_ref,
    query_peer_next2_ref,
    query_peer_next4_ref,
    next2_ref,
    next4_ref,
    peer_ref,
    peer_next2_ref,
    peer_next4_ref,
    w_key_ref,
    w_value_ref,
    gain_ref,
    own_ref,
    total_ref,
    partial_ref,
    key_sum_ref,
    value_sum_ref,
    result_ref,
    keep_ref,
    out_ref,
    held_ref,
    grads,
    queries,
    stats,
    key_grad,
    value_grad,
):
    place = lax.axis_index("tm")
    odd = lax.rem(place, 2) == 1
    count = valid_count(valid_ref, place)
    wide = grads.shape[1]
    messages = (
        (peer_next2_ref, peer_ref),
        (next2_ref, next2_ref),
        (peer_next4_ref, peer_next2_ref),
        (next4_ref, next4_ref),
    )
    gather_window(odd, messages, grads)
    gather_window(
        odd,
        (
            (query_peer_next2_ref, query_peer_ref),
            (query_next2_ref, query_next2_ref),
            (query_peer_next4_ref, query_peer_next2_ref),
            (query_next4_ref, query_next4_ref),
        ),
        queries,
    )
    for block, (when_odd, when_even) in enumerate(messages):
        stats[:, block * ROWS : (block + 1) * ROWS] = message_stats(
            chosen_rows(odd, when_odd, when_even, slice(ROWS, ROWS + 16))
        )
    key_valid = lax.broadcasted_iota(jnp.int32, (ROWS, LEFT * ROWS), 0) < count
    for pair in range(wide // PAIR):
        lanes = slice(pair * PAIR, (pair + 1) * PAIR)
        heads = (2 * pair, 2 * pair + 1)
        key_sum, value_sum = key_terms(
            kept_ref[:, lanes],
            kept_ref[:, slice(wide + pair * PAIR, wide + (pair + 1) * PAIR)],
            queries[:, lanes],
            grads[:, lanes],
            [stats[head : head + 1, :] for head in heads],
            [stats[8 + head : 9 + head, :] for head in heads],
            key_valid,
        )
        key_grad[:, lanes] = (key_sum_ref[:, lanes] + key_sum).astype(BF16)
        value_grad[:, lanes] = (value_sum_ref[:, lanes] + value_sum).astype(BF16)
    normed_grad = partial_ref[...] + dot_nt(key_grad[...], w_key_ref[...])
    normed_grad = normed_grad + dot_nt(value_grad[...], w_value_ref[...])
    scaled = normed_grad * gain_ref[...]
    unit, inverse = unit_rows(own_ref[...].astype(F32))
    back = inverse * (
        scaled
        - jnp.mean(scaled, axis=-1, keepdims=True)
        - unit * jnp.mean(scaled * unit, axis=-1, keepdims=True)
    )
    result = total_ref[...] + back
    out_ref[...] = result.astype(BF16)
    mine = lax.axis_index("section") == keep_ref[0]
    held_ref[...] = jnp.where(mine, result, result_ref[...].astype(F32)).astype(BF16)


def call(kernel, name, operands, outs, scratch, flops, scalars=(0,)):
    vmem = pl.BlockSpec(memory_space=pltpu.VMEM)
    smem = pl.BlockSpec(memory_space=pltpu.SMEM)
    return pl.pallas_call(
        kernel,
        name=name,
        in_specs=[smem if index in scalars else vmem for index in range(len(operands))],
        out_specs=[vmem] * len(outs),
        out_shape=[jax.ShapeDtypeStruct(shape, dtype) for shape, dtype in outs],
        scratch_shapes=[pltpu.VMEM(shape, dtype) for shape, dtype in scratch],
        compiler_params=pltpu.CompilerParams(vmem_limit_bytes=VMEM_LIMIT),
        cost_estimate=pl.CostEstimate(flops=flops, bytes_accessed=4 << 20, transcendentals=0),
    )(*operands)


def after(value, *others):
    return lax.optimization_barrier((value, *others))[0]


def shards(
    layer_inputs, top_grad, w_query, w_key, w_value, w_out, conv_kernel, norm_gain, group_valid
):
    own = layer_inputs[0]
    width = own.shape[1]
    wide = w_query.shape[2]
    query_weight = w_query[0]
    key_weight = w_key[0]
    value_weight = w_value[0]
    out_weight = w_out[0]
    kernel = conv_kernel[0]
    sections = lax.axis_size("section")
    count = lax.axis_size("tm")

    def moved(value, pairs):
        return lax.ppermute(value, ("tm", "section"), pairs)

    def at(layer, frame):
        return frame * sections + layer

    def across(steps, chosen):
        return [
            (at(section, source), at(section, source + steps))
            for section in chosen
            for source in range(max(0, -steps), min(count, count - steps))
        ]

    def swapped(chosen, parities):
        return [
            (at(section, source), at(section, source ^ 1))
            for section in chosen
            for source in range(count)
            if source % 2 in parities
        ]

    every = range(sections)
    half_edge = EDGE // 2
    queries, kept, ahead, behind = call(
        project_kernel,
        "project",
        (own, top_grad, norm_gain, query_weight, key_weight, value_weight),
        [
            ((ROWS, wide), BF16),
            ((ROWS, 2 * wide), BF16),
            ((ROWS + EDGE + half_edge, width), BF16),
            ((ROWS + 2 * EDGE + half_edge, width), BF16),
        ],
        [((ROWS, width), BF16)],
        1 << 30,
        scalars=(),
    )
    back2 = moved(ahead, across(2, every))
    back4 = moved(kept, across(4, every))
    peer = moved(ahead, swapped(every, (0,)))
    after1 = moved(behind, across(-1, every))
    peer_back2 = moved(back2, swapped(every, (0, 1)))
    peer_back4 = moved(back4, swapped(every, (0, 1)))
    far_pairs = [
        (at(section, source), at(section, source + 5))
        for section in every
        for source in range(1, count - 5, 2)
    ]
    back5 = moved(after(kept, back2), far_pairs)
    query_next2 = moved(after(queries, back2), across(-2, every))
    query_next4 = moved(after(queries, back2), across(-4, every))

    attended, logs = call(
        attend_kernel,
        "attend",
        (group_valid, queries, kept, back2, back4, peer, peer_back2, peer_back4, after1),
        [((ROWS + EDGE, wide), BF16), ((ROWS, PAIR), F32)],
        [(((LEFT + 2) * ROWS, 2 * wide), BF16), ((ROWS + EDGE, wide), BF16)],
        1 << 30,
    )
    back5 = after(back5, attended)
    span = (LEFT + 1) * ROWS
    step_outs = [((ROWS, width), F32), ((ROWS + 16, wide), BF16), ((ROWS, PAIR), F32)]
    slope, total, message, dots = call(
        mix_kernel,
        "mix",
        (
            group_valid,
            own,
            top_grad,
            attended,
            logs,
            back2,
            back4,
            back5,
            peer,
            peer_back2,
            peer_back4,
            after1,
            out_weight,
            kernel,
        ),
        [((ROWS + EDGE, width), F32)] + step_outs,
        [
            ((span, 2 * wide), BF16),
            ((EDGE, wide), BF16),
            ((ROWS + 2 * EDGE, wide), BF16),
            ((ROWS + 2 * EDGE, width), F32),
            ((ROWS, width), BF16),
        ],
        1 << 30,
    )
    query_peer = moved(queries, swapped(every, (1,)))
    query_peer_next2 = moved(query_next2, swapped(every, (0, 1)))
    query_peer_next4 = moved(query_next4, swapped(every, (0,)))

    result = own
    upstream = None
    upstream_next = None
    for step in range(sections):
        layer = sections - 1 - step
        if step > 0:
            total, message, dots = call(
                mixer_kernel,
                "mixer",
                (group_valid, upstream, upstream_next, slope, kernel, out_weight, attended, logs),
                step_outs,
                [((ROWS, width), BF16)],
                1 << 30,
            )
        here = [layer]
        grad2 = moved(message, across(-2, here))
        grad4 = moved(message, across(-4, here))
        peer_grad = moved(message, swapped(here, (1,)))
        partial, key_sum, value_sum = call(
            query_kernel,
            "own_queries",
            (
                group_valid,
                queries,
                kept,
                back2,
                back4,
                peer,
                peer_back2,
                peer_back4,
                message,
                logs,
                dots,
                query_weight,
            ),
            [((ROWS, width), F32), ((ROWS, wide), F32), ((ROWS, wide), F32)],
            [((span, 2 * wide), BF16), ((ROWS, wide), BF16)],
            1 << 30,
        )
        grad2, grad4, partial = lax.optimization_barrier((grad2, grad4, partial))
        peer_grad2 = moved(grad2, swapped(here, (0, 1)))
        peer_grad4 = moved(grad4, swapped(here, (0,)))
        operands = (
            group_valid,
            kept,
            query_next2,
            query_next4,
            query_peer,
            query_peer_next2,
            query_peer_next4,
            grad2,
            grad4,
            peer_grad,
            peer_grad2,
            peer_grad4,
            key_weight,
            value_weight,
            norm_gain,
            own,
            total,
            partial,
            key_sum,
            value_sum,
            result,
            jnp.full((1,), layer, jnp.int32),
        )
        input_grad, result = call(
            key_kernel,
            "own_keys",
            operands,
            [((ROWS, width), BF16), ((ROWS, width), BF16)],
            [
                ((LEFT * ROWS, wide), BF16),
                ((LEFT * ROWS, wide), BF16),
                ((16, LEFT * ROWS), F32),
                ((ROWS, wide), BF16),
                ((ROWS, wide), BF16),
            ],
            1 << 30,
            scalars=(0, len(operands) - 1),
        )
        if layer > 0:
            upstream = moved(
                input_grad, [(at(layer, source), at(layer - 1, source)) for source in range(count)]
            )
            upstream_next = moved(
                input_grad[:EDGE],
                [(at(layer, source), at(layer - 1, source - 1)) for source in range(1, count)],
            )
    return result[None]


def solution(mesh):
    placed = (
        P("section", "tm", None),
        P("tm", None),
        P("section", None, None),
        P("section", None, None),
        P("section", None, None),
        P("section", None, None),
        P("section", None, None),
        P("section", None),
        P(),
    )
    return jax.shard_map(
        shards, mesh=mesh, in_specs=placed, out_specs=P("section", "tm", None), check_vma=False
    )
```

```python
import jax
import jax.numpy as jnp
from jax import lax
from jax.experimental import pallas as pl
from jax.experimental.pallas import tpu as pltpu
from jax.sharding import PartitionSpec as P

HEAD_DIM = 64
PAIR = 128
ROWS = 128
LEFT = 4
EDGE = 32
SCALE = HEAD_DIM ** (-0.5)
NEGATIVE = -1e30
EPSILON = 1e-05
F32 = jnp.float32
BF16 = jnp.bfloat16
VMEM_LIMIT = 56 * 1024 * 1024


def dot_nn(a, b):
    return lax.dot_general(a, b, (((1,), (0,)), ((), ())), preferred_element_type=F32)


def dot_nt(a, b):
    return lax.dot_general(a, b, (((1,), (1,)), ((), ())), preferred_element_type=F32)


def valid_count(valid_ref, block):
    groups = valid_ref.shape[0]
    inside = (block >= 0) & (block < groups)
    return jnp.where(inside, valid_ref[jnp.clip(block, 0, groups - 1)], 0)


def even_half(rows):
    return lax.broadcasted_iota(jnp.int32, (rows, PAIR), 1) < HEAD_DIM


def unit_rows(values):
    center = values - jnp.mean(values, axis=-1, keepdims=True)
    spread = jnp.mean(center * center, axis=-1, keepdims=True)
    inverse = lax.rsqrt(spread + EPSILON)
    return center * inverse, inverse


def three_parts(value):
    first = value.astype(BF16)
    rest = value - first.astype(F32)
    second = rest.astype(BF16)
    third = (rest - second.astype(F32)).astype(BF16)
    return first, second, third


def shift_rows(value, amount):
    if amount == 0:
        return value
    return pltpu.roll(value, value.shape[0] - amount, 0)


def tap_sum(padded, kernel_ref, lanes, first, step, rows):
    taps = kernel_ref.shape[0]
    total = jnp.zeros((rows, padded.shape[1]), F32)
    for phase in range(8):
        moved = None
        for tap in range(taps):
            offset = first + step * tap
            if offset % 8 != phase:
                continue
            if moved is None:
                moved = shift_rows(padded, phase)
            base = offset - phase
            total = total + kernel_ref[tap : tap + 1, lanes] * moved[base : base + rows]
    return total


def project_kernel(
    own_ref,
    top_ref,
    gain_ref,
    w_query_ref,
    w_key_ref,
    w_value_ref,
    queries_ref,
    kept_ref,
    ahead_ref,
    behind_ref,
    normed,
    w_query,
    w_key,
    w_value,
    semaphores,
):
    chunk = 16
    loader = Loader(semaphores, None)
    loader.get(w_key, w_key_ref)
    loader.get(w_value, w_value_ref)
    late = Loader(semaphores.at[2:], None)
    late.get(w_query, w_query_ref)

    def norm_step(step, carry):
        rows = pl.ds(pl.multiple_of(step * chunk, chunk), chunk)
        unit, _ = unit_rows(own_ref[rows, :].astype(F32))
        normed[rows, :] = (unit * gain_ref[...]).astype(BF16)
        return carry

    lax.fori_loop(0, ROWS // chunk, norm_step, 0, unroll=2)
    wide = w_key_ref.shape[1]
    half = EDGE // 2
    loader.wait()
    keys = dot_nn(normed[...], w_key[...]).astype(BF16)
    values = dot_nn(normed[...], w_value[...]).astype(BF16)
    for ref in (kept_ref, ahead_ref, behind_ref):
        ref[0:ROWS, 0:wide] = keys
        ref[0:ROWS, wide : 2 * wide] = values
    late.wait()
    queries = dot_nn(normed[...], w_query[...]).astype(BF16)
    queries_ref[...] = queries
    ahead_ref[ROWS : ROWS + EDGE, :] = own_ref[ROWS - EDGE : ROWS, :]
    ahead_ref[ROWS + EDGE : ROWS + EDGE + half, 0:wide] = queries[ROWS - EDGE : ROWS - half]
    ahead_ref[ROWS + EDGE : ROWS + EDGE + half, wide : 2 * wide] = queries[ROWS - half : ROWS]
    behind_ref[ROWS : ROWS + EDGE, :] = own_ref[0:EDGE, :]
    behind_ref[ROWS + EDGE : ROWS + EDGE + half, 0:wide] = queries[0:half]
    behind_ref[ROWS + EDGE : ROWS + EDGE + half, wide : 2 * wide] = queries[half:EDGE]
    behind_ref[ROWS + EDGE + half : ROWS + 2 * EDGE + half, :] = top_ref[0:EDGE, :]


class Loader:
    def __init__(self, semaphores, odd):
        self.semaphores = semaphores
        self.odd = odd
        self.used = 0
        self.waiting = []

    def get(self, target, when_odd, when_even=None, rows=None):
        semaphore = self.semaphores.at[self.used]
        self.used += 1

        def copy(source):
            view = source if rows is None else source.at[rows[0] : rows[1]]
            return pltpu.make_async_copy(view, target, semaphore)

        if when_even is None or when_even is when_odd:
            copy(when_odd).start()
        else:

            @pl.when(self.odd)
            def _():
                copy(when_odd).start()

            @pl.when(jnp.logical_not(self.odd))
            def _():
                copy(when_even).start()

        self.waiting.append(copy(when_odd))

    def window(self, target, sources):
        for index, (when_odd, when_even) in enumerate(sources):
            self.get(target.at[index * ROWS : (index + 1) * ROWS], when_odd, when_even, (0, ROWS))

    def wait(self):
        for copy in self.waiting:
            copy.wait()
        self.waiting = []


def masked_half(value, half):
    keep = even_half(value.shape[0])
    if half:
        keep = jnp.logical_not(keep)
    return jnp.where(keep, value, jnp.zeros_like(value))


def pair_shares(scores, allowed):
    part = jnp.where(allowed, scores, NEGATIVE)
    highest = jnp.max(part, axis=-1, keepdims=True)
    exped = jnp.exp(part - highest)
    summed = jnp.sum(exped, axis=-1, keepdims=True)
    return (exped * (1.0 / summed)).astype(BF16), highest, summed


def attend_kernel(
    valid_ref,
    queries_ref,
    kept_ref,
    back2_ref,
    back4_ref,
    peer_ref,
    peer_back2_ref,
    peer_back4_ref,
    after_ref,
    attended_ref,
    log_ref,
    window,
    query_all,
    packed,
    semaphores,
):
    place = lax.axis_index("tm")
    odd = lax.rem(place, 2) == 1
    wide = queries_ref.shape[1]
    half_edge = EDGE // 2
    loader = Loader(semaphores, odd)
    loader.get(query_all.at[0:ROWS], queries_ref)
    loader.get(packed, after_ref, rows=(ROWS + EDGE, ROWS + EDGE + half_edge))
    loader.window(
        window,
        (
            (back4_ref, back4_ref),
            (peer_back2_ref, peer_back4_ref),
            (back2_ref, back2_ref),
            (peer_ref, peer_back2_ref),
            (kept_ref, kept_ref),
            (after_ref, after_ref),
        ),
    )
    loader.wait()
    query_all[ROWS : ROWS + half_edge, :] = packed[:, 0:wide]
    query_all[ROWS + half_edge : ROWS + EDGE, :] = packed[:, wide : 2 * wide]
    key_lane = lax.broadcasted_iota(jnp.int32, (1, ROWS), 1)
    allowed = jnp.concatenate(
        [key_lane < valid_count(valid_ref, place + block - LEFT) for block in range(LEFT + 2)], axis=1
    )
    span = (LEFT + 1) * ROWS
    log_lane = lax.broadcasted_iota(jnp.int32, (ROWS, PAIR), 1)
    logs = jnp.zeros((ROWS, PAIR), F32)
    for pair in range(wide // PAIR):
        lanes = slice(pair * PAIR, (pair + 1) * PAIR)
        value_lanes = slice(wide + pair * PAIR, wide + (pair + 1) * PAIR)
        totals = [None, None]
        for half in range(2):
            scores = dot_nt(query_all[:, lanes], masked_half(window[:, lanes], half)) * SCALE
            value_half = masked_half(window[:, value_lanes], half)
            for group, (low, high, first) in enumerate(((0, ROWS, 0), (ROWS, ROWS + EDGE, ROWS))):
                shares_low, highest, summed = pair_shares(
                    scores[low:high, first : first + span], allowed[:, first : first + span]
                )
                product = dot_nn(shares_low, value_half[first : first + span])
                totals[group] = product if totals[group] is None else totals[group] + product
                if group == 0:
                    logs = jnp.where(log_lane == 2 * pair + half, highest + jnp.log(summed), logs)
        attended_ref[0:ROWS, lanes] = totals[0].astype(BF16)
        attended_ref[ROWS : ROWS + EDGE, lanes] = totals[1].astype(BF16)
    log_ref[...] = logs


def mixer_body(
    count, upstream_ref, next_rows, slope_ref, kernel_ref, w_out_ref, attended, log_ref, total_ref, message_ref, dot_ref, total_low, ready=lambda: None
):
    row_ids = lax.broadcasted_iota(jnp.int32, (ROWS, PAIR), 0)
    taps = kernel_ref.shape[0]

    def conv_step(step, carry):
        lanes = pl.ds(pl.multiple_of(step * PAIR, PAIR), PAIR)
        upper = upstream_ref[:, lanes].astype(F32)
        stacked = jnp.concatenate([upper, next_rows(lanes)], axis=0)
        grads = (stacked * slope_ref[:, lanes]).astype(BF16).astype(F32)
        back = tap_sum(grads, kernel_ref, lanes, taps - 1, -1, ROWS)
        total = upper + jnp.where(row_ids < count, back, 0.0)
        total_ref[:, lanes] = total
        total_low[:, lanes] = total.astype(BF16)
        return carry

    lax.fori_loop(0, upstream_ref.shape[1] // PAIR, conv_step, 0)
    ready()
    out_grad = dot_nt(total_low[...], w_out_ref[...]).astype(BF16)
    message_ref[0:ROWS, :] = out_grad
    product = out_grad.astype(F32) * attended[...].astype(F32)
    high = product.astype(BF16)
    low = (product - high.astype(F32)).astype(BF16)
    width = product.shape[1]
    head_of = lax.broadcasted_iota(jnp.int32, (PAIR, width), 1) // HEAD_DIM
    chosen = (head_of == lax.broadcasted_iota(jnp.int32, (PAIR, width), 0)).astype(F32).astype(BF16)
    dots = dot_nt(high, chosen) + dot_nt(low, chosen)
    dot_ref[...] = dots
    stacked = jnp.concatenate([log_ref[...].T[0:8], dots.T[0:8]], axis=0)
    message_ref[ROWS : ROWS + 16, :] = jnp.zeros((16, width), BF16)
    for index, part in enumerate(three_parts(stacked)):
        message_ref[ROWS : ROWS + 16, index * PAIR : (index + 1) * PAIR] = part


def mix_kernel(
    valid_ref,
    own_ref,
    top_ref,
    attended_ref,
    log_ref,
    back2_ref,
    back4_ref,
    back5_ref,
    peer_ref,
    peer_back2_ref,
    peer_back4_ref,
    after_ref,
    w_out_ref,
    kernel_ref,
    slope_ref,
    total_ref,
    message_ref,
    dot_ref,
    window,
    query_tail,
    attended_all,
    mixed,
    total_low,
    before_rows,
    after_rows,
    own,
    top,
    w_out,
    semaphores,
):
    place = lax.axis_index("tm")
    odd = lax.rem(place, 2) == 1
    wide = query_tail.shape[1]
    half_edge = EDGE // 2
    counts = [valid_count(valid_ref, place + block - LEFT - 1) for block in range(LEFT + 3)]
    loader = Loader(semaphores, odd)
    loader.get(before_rows, peer_ref, peer_back2_ref, (ROWS, ROWS + EDGE + half_edge))
    loader.window(
        window,
        (
            (peer_back4_ref, back5_ref),
            (back4_ref, back4_ref),
            (peer_back2_ref, peer_back4_ref),
            (back2_ref, back2_ref),
            (peer_ref, peer_back2_ref),
        ),
    )
    late = Loader(semaphores.at[LEFT + 2 :], odd)
    late.get(attended_all.at[EDGE : 2 * EDGE + ROWS], attended_ref)
    late.get(w_out, w_out_ref)
    late.get(own, own_ref)
    late.get(after_rows, after_ref, rows=(ROWS, ROWS + 2 * EDGE + half_edge))
    late.get(top, top_ref)
    loader.wait()
    query_tail[0:half_edge, :] = before_rows[EDGE : EDGE + half_edge, 0:wide]
    query_tail[half_edge:EDGE, :] = before_rows[EDGE : EDGE + half_edge, wide : 2 * wide]
    key_lane = lax.broadcasted_iota(jnp.int32, (1, ROWS), 1)
    allowed = jnp.concatenate([key_lane < count for count in counts[: LEFT + 1]], axis=1)
    for pair in range(wide // PAIR):
        lanes = slice(pair * PAIR, (pair + 1) * PAIR)
        value_lanes = slice(wide + pair * PAIR, wide + (pair + 1) * PAIR)
        total = None
        for half in range(2):
            scores = dot_nt(query_tail[:, lanes], masked_half(window[:, lanes], half)) * SCALE
            shares_low, _, _ = pair_shares(scores, allowed)
            product = dot_nn(shares_low, masked_half(window[:, value_lanes], half))
            total = product if total is None else total + product
        attended_all[0:EDGE, lanes] = total.astype(BF16)
    late.wait()
    projected = dot_nn(attended_all[...], w_out[...])
    row_ids = lax.broadcasted_iota(jnp.int32, (ROWS, 1), 0)
    edge_ids = lax.broadcasted_iota(jnp.int32, (EDGE, 1), 0)
    before = projected[0:EDGE] + before_rows[0:EDGE, :].astype(F32)
    here = projected[EDGE : EDGE + ROWS] + own[...].astype(F32)
    after = projected[EDGE + ROWS :] + after_rows[0:EDGE, :].astype(F32)
    before = jnp.where(edge_ids + (ROWS - EDGE) < counts[LEFT], before, 0.0)
    here = jnp.where(row_ids < counts[LEFT + 1], here, 0.0)
    after = jnp.where(edge_ids < counts[LEFT + 2], after, 0.0)
    mixed[0:EDGE, :] = before.astype(BF16).astype(F32)
    mixed[EDGE : EDGE + ROWS, :] = here.astype(BF16).astype(F32)
    mixed[EDGE + ROWS :, :] = after.astype(BF16).astype(F32)
    taps = kernel_ref.shape[0]

    def conv_step(step, carry):
        lanes = pl.ds(pl.multiple_of(step * PAIR, PAIR), PAIR)
        output = tap_sum(mixed[:, lanes], kernel_ref, lanes, EDGE - (taps - 1), 1, ROWS + EDGE)
        gate = 1.0 / (1.0 + jnp.exp(-output))
        slope_ref[:, lanes] = gate * (1.0 + output * (1.0 - gate))
        return carry

    lax.fori_loop(0, own.shape[1] // PAIR, conv_step, 0)
    first = EDGE + half_edge
    mixer_body(
        counts[LEFT + 1],
        top,
        lambda lanes: after_rows[first : first + EDGE, lanes].astype(F32),
        slope_ref,
        kernel_ref,
        w_out,
        attended_all[EDGE : EDGE + ROWS, :],
        log_ref,
        total_ref,
        message_ref,
        dot_ref,
        total_low,
    )


def mixer_kernel(
    valid_ref,
    upstream_ref,
    next_ref,
    slope_ref,
    kernel_ref,
    w_out_ref,
    attended_ref,
    log_ref,
    total_ref,
    message_ref,
    dot_ref,
    total_low,
    upstream,
    next_rows,
    slope,
    w_out,
    attended,
    semaphores,
):
    loader = Loader(semaphores, None)
    loader.get(upstream, upstream_ref)
    loader.get(next_rows, next_ref)
    loader.get(slope, slope_ref)
    late = Loader(semaphores.at[3:], None)
    late.get(attended, attended_ref, rows=(0, ROWS))
    late.get(w_out, w_out_ref)
    loader.wait()
    mixer_body(
        valid_count(valid_ref, lax.axis_index("tm")),
        upstream,
        lambda lanes: next_rows[:, lanes].astype(F32),
        slope,
        kernel_ref,
        w_out,
        attended,
        log_ref,
        total_ref,
        message_ref,
        dot_ref,
        total_low,
        late.wait,
    )


def key_terms(key_pair, value_pair, query_pair, grad_pair, logs, dots, key_valid):
    share_halves = []
    score_halves = []
    query_halves = [masked_half(query_pair, half) for half in range(2)]
    grad_halves = [masked_half(grad_pair, half) for half in range(2)]
    for half in range(2):
        scores = dot_nt(key_pair, query_halves[half]) * SCALE
        shares = jnp.exp(jnp.where(key_valid, scores, NEGATIVE) - logs[half])
        share_grad = dot_nt(value_pair, grad_halves[half])
        score_halves.append((shares * (share_grad - dots[half])).astype(BF16))
        share_halves.append(shares.astype(BF16))
    key_sum = None
    value_sum = None
    for block in range(query_pair.shape[0] // ROWS):
        rows = slice(block * ROWS, (block + 1) * ROWS)
        key_term = dot_nn(
            jnp.concatenate([score[:, rows] for score in score_halves], axis=1),
            jnp.concatenate([query[rows] for query in query_halves], axis=0),
        )
        value_term = dot_nn(
            jnp.concatenate([share[:, rows] for share in share_halves], axis=1),
            jnp.concatenate([grad[rows] for grad in grad_halves], axis=0),
        )
        key_term = (key_term * SCALE).astype(BF16).astype(F32)
        value_term = value_term.astype(BF16).astype(F32)
        key_sum = key_term if key_sum is None else key_sum + key_term
        value_sum = value_term if value_sum is None else value_sum + value_term
    return key_sum, value_sum


def message_stats(tail):
    tail = tail.astype(F32)
    return tail[:, 0:PAIR] + tail[:, PAIR : 2 * PAIR] + tail[:, 2 * PAIR : 3 * PAIR]


def query_kernel(
    valid_ref,
    queries_ref,
    kept_ref,
    back2_ref,
    back4_ref,
    peer_ref,
    peer_back2_ref,
    peer_back4_ref,
    message_ref,
    log_ref,
    dot_ref,
    w_query_ref,
    out_ref,
    key_sum_ref,
    value_sum_ref,
    window,
    query_grad,
    queries,
    message,
    w_query,
    semaphores,
):
    place = lax.axis_index("tm")
    odd = lax.rem(place, 2) == 1
    wide = queries_ref.shape[1]
    loader = Loader(semaphores, odd)
    loader.get(queries, queries_ref)
    loader.get(message, message_ref)
    loader.window(
        window,
        (
            (back4_ref, back4_ref),
            (peer_back2_ref, peer_back4_ref),
            (back2_ref, back2_ref),
            (peer_ref, peer_back2_ref),
            (kept_ref, kept_ref),
        ),
    )
    late = Loader(semaphores.at[LEFT + 3 :], odd)
    late.get(w_query, w_query_ref)
    loader.wait()
    own_rows = slice(LEFT * ROWS, (LEFT + 1) * ROWS)
    key_lane = lax.broadcasted_iota(jnp.int32, (1, ROWS), 1)
    allowed = jnp.concatenate(
        [key_lane < valid_count(valid_ref, place + block - LEFT) for block in range(LEFT + 1)], axis=1
    )
    key_valid = lax.broadcasted_iota(jnp.int32, (ROWS, ROWS), 0) < valid_count(valid_ref, place)
    stats = message_stats(message[ROWS : ROWS + 16, :])
    for pair in range(wide // PAIR):
        lanes = slice(pair * PAIR, (pair + 1) * PAIR)
        value_lanes = slice(wide + pair * PAIR, wide + (pair + 1) * PAIR)
        query_pair = queries[:, lanes]
        grad_pair = message[0:ROWS, lanes]
        total = None
        for half in range(2):
            key_half = masked_half(window[:, lanes], half)
            value_half = masked_half(window[:, value_lanes], half)
            head = 2 * pair + half
            scores = dot_nt(query_pair, key_half) * SCALE
            shares = jnp.exp(jnp.where(allowed, scores, NEGATIVE) - log_ref[:, head : head + 1])
            share_grad = dot_nt(grad_pair, value_half)
            score_grad = (shares * (share_grad - dot_ref[:, head : head + 1])).astype(BF16)
            product = dot_nn(score_grad, key_half)
            total = product if total is None else total + product
        query_grad[:, lanes] = (total * SCALE).astype(BF16)
        heads = (2 * pair, 2 * pair + 1)
        key_sum_ref[:, lanes], value_sum_ref[:, lanes] = key_terms(
            window[own_rows, lanes],
            window[own_rows, value_lanes],
            query_pair,
            grad_pair,
            [stats[head : head + 1] for head in heads],
            [stats[8 + head : 9 + head] for head in heads],
            key_valid,
        )
    late.wait()
    out_ref[...] = dot_nt(query_grad[...], w_query[...])


def key_kernel(
    valid_ref,
    kept_ref,
    query_next2_ref,
    query_next4_ref,
    query_peer_ref,
    query_peer_next2_ref,
    query_peer_next4_ref,
    next2_ref,
    next4_ref,
    peer_ref,
    peer_next2_ref,
    peer_next4_ref,
    w_key_ref,
    w_value_ref,
    gain_ref,
    own_ref,
    total_ref,
    partial_ref,
    key_sum_ref,
    value_sum_ref,
    result_ref,
    keep_ref,
    out_ref,
    edge_ref,
    held_ref,
    grads,
    queries,
    tails,
    stats,
    key_grad,
    value_grad,
    kept,
    w_key,
    w_value,
    own,
    total,
    partial,
    result,
    semaphores,
):
    place = lax.axis_index("tm")
    odd = lax.rem(place, 2) == 1
    count = valid_count(valid_ref, place)
    wide = grads.shape[1]
    loader = Loader(semaphores, odd)
    messages = (
        (peer_next2_ref, peer_ref),
        (next2_ref, next2_ref),
        (peer_next4_ref, peer_next2_ref),
        (next4_ref, next4_ref),
    )
    loader.get(kept, kept_ref)
    loader.window(grads, messages)
    for block, (when_odd, when_even) in enumerate(messages):
        loader.get(tails.at[block * 16 : block * 16 + 16], when_odd, when_even, (ROWS, ROWS + 16))
    loader.window(
        queries,
        (
            (query_peer_next2_ref, query_peer_ref),
            (query_next2_ref, query_next2_ref),
            (query_peer_next4_ref, query_peer_next2_ref),
            (query_next4_ref, query_next4_ref),
        ),
    )
    late = Loader(semaphores.at[loader.used :], odd)
    late.get(w_key, w_key_ref)
    late.get(w_value, w_value_ref)
    late.get(own, own_ref)
    late.get(total, total_ref)
    late.get(partial, partial_ref)
    late.get(result, result_ref)
    loader.wait()
    for block in range(LEFT):
        stats[:, block * ROWS : (block + 1) * ROWS] = message_stats(tails[block * 16 : block * 16 + 16, :])
    key_valid = lax.broadcasted_iota(jnp.int32, (ROWS, LEFT * ROWS), 0) < count
    for pair in range(wide // PAIR):
        lanes = slice(pair * PAIR, (pair + 1) * PAIR)
        heads = (2 * pair, 2 * pair + 1)
        key_sum, value_sum = key_terms(
            kept[:, lanes],
            kept[:, slice(wide + pair * PAIR, wide + (pair + 1) * PAIR)],
            queries[:, lanes],
            grads[:, lanes],
            [stats[head : head + 1, :] for head in heads],
            [stats[8 + head : 9 + head, :] for head in heads],
            key_valid,
        )
        key_grad[:, lanes] = (key_sum_ref[:, lanes] + key_sum).astype(BF16)
        value_grad[:, lanes] = (value_sum_ref[:, lanes] + value_sum).astype(BF16)
    late.wait()
    normed_grad = partial[...] + dot_nt(key_grad[...], w_key[...])
    normed_grad = normed_grad + dot_nt(value_grad[...], w_value[...])
    scaled = normed_grad * gain_ref[...]
    unit, inverse = unit_rows(own[...].astype(F32))
    back = inverse * (
        scaled
        - jnp.mean(scaled, axis=-1, keepdims=True)
        - unit * jnp.mean(scaled * unit, axis=-1, keepdims=True)
    )
    grad = total[...] + back
    out_ref[...] = grad.astype(BF16)
    edge_ref[...] = grad[0:EDGE].astype(BF16)
    mine = lax.axis_index("section") == keep_ref[0]
    held_ref[...] = jnp.where(mine, grad, result[...].astype(F32)).astype(BF16)


def call(kernel, name, operands, outs, scratch, copies, flops):
    kinds = {
        "s": pl.BlockSpec(memory_space=pltpu.SMEM),
        "v": pl.BlockSpec(memory_space=pltpu.VMEM),
        "a": pl.BlockSpec(memory_space=pl.ANY),
    }
    return pl.pallas_call(
        kernel,
        name=name,
        in_specs=[kinds[place] for _, place in operands],
        out_specs=[kinds["v"]] * len(outs),
        out_shape=[jax.ShapeDtypeStruct(shape, dtype) for shape, dtype in outs],
        scratch_shapes=[pltpu.VMEM(shape, dtype) for shape, dtype in scratch]
        + [pltpu.SemaphoreType.DMA((copies,))],
        compiler_params=pltpu.CompilerParams(vmem_limit_bytes=VMEM_LIMIT),
        cost_estimate=pl.CostEstimate(flops=flops, bytes_accessed=4 << 20, transcendentals=0),
    )(*[array for array, _ in operands])


def placed(kinds, *arrays):
    return list(zip(arrays, kinds, strict=True))


def after(value, *others):
    return lax.optimization_barrier((value, *others))[0]


def shards(
    layer_inputs, top_grad, w_query, w_key, w_value, w_out, conv_kernel, norm_gain, group_valid
):
    own = layer_inputs[0]
    width = own.shape[1]
    wide = w_query.shape[2]
    query_weight = w_query[0]
    key_weight = w_key[0]
    value_weight = w_value[0]
    out_weight = w_out[0]
    kernel = conv_kernel[0]
    sections = lax.axis_size("section")
    count = lax.axis_size("tm")

    def moved(value, pairs):
        return lax.ppermute(value, ("tm", "section"), pairs)

    def at(layer, frame):
        return frame * sections + layer

    def across(steps, chosen):
        return [
            (at(section, source), at(section, source + steps))
            for section in chosen
            for source in range(max(0, -steps), min(count, count - steps))
        ]

    every = range(sections)
    half_edge = EDGE // 2
    swap = [(at(section, source), at(section, source ^ 1)) for section in every for source in range(count)]
    weight = ((width, wide), BF16)
    queries, kept, ahead, behind = call(
        project_kernel,
        "project",
        placed("vvvaaa", own, top_grad, norm_gain, query_weight, key_weight, value_weight),
        [
            ((ROWS, wide), BF16),
            ((ROWS, 2 * wide), BF16),
            ((ROWS + EDGE + half_edge, width), BF16),
            ((ROWS + 2 * EDGE + half_edge, width), BF16),
        ],
        [((ROWS, width), BF16), weight, weight, weight],
        3,
        1 << 30,
    )
    back2 = moved(ahead, across(2, every))
    back4 = moved(kept, across(4, every))
    after1 = moved(behind, across(-1, every))
    query_next2 = moved(queries, across(-2, every))
    query_next4 = moved(queries, across(-4, every))
    peer = moved(ahead, swap)
    query_peer = moved(queries, swap)
    peer_back2 = moved(back2, swap)
    peer_back4 = moved(back4, swap)
    query_peer_next2 = moved(query_next2, swap)
    query_peer_next4 = moved(query_next4, swap)
    far_pairs = [
        (at(section, source), at(section, source + 5))
        for section in every
        for source in range(1, count - 5, 2)
    ]
    back5 = moved(after(kept, back2), far_pairs)
    query_next2, query_next4, query_peer, query_peer_next2, query_peer_next4, after1 = (
        lax.optimization_barrier(
            (query_next2, query_next4, query_peer, query_peer_next2, query_peer_next4, after1)
        )
    )

    span = (LEFT + 1) * ROWS
    attended, logs = call(
        attend_kernel,
        "attend",
        placed("saaaaaaaa", group_valid, queries, kept, back2, back4, peer, peer_back2, peer_back4, after1),
        [((ROWS + EDGE, wide), BF16), ((ROWS, PAIR), F32)],
        [(((LEFT + 2) * ROWS, 2 * wide), BF16), ((ROWS + EDGE, wide), BF16), ((half_edge, 2 * wide), BF16)],
        LEFT + 4,
        1 << 30,
    )
    back5 = after(back5, attended)
    step_outs = [((ROWS, width), F32), ((ROWS + 16, wide), BF16), ((ROWS, PAIR), F32)]
    slope, total, message, dots = call(
        mix_kernel,
        "mix",
        placed(
            "saaavaaaaaaaav",
            group_valid,
            own,
            top_grad,
            attended,
            logs,
            back2,
            back4,
            back5,
            peer,
            peer_back2,
            peer_back4,
            after1,
            out_weight,
            kernel,
        ),
        [((ROWS + EDGE, width), F32)] + step_outs,
        [
            ((span, 2 * wide), BF16),
            ((EDGE, wide), BF16),
            ((ROWS + 2 * EDGE, wide), BF16),
            ((ROWS + 2 * EDGE, width), F32),
            ((ROWS, width), BF16),
            ((EDGE + half_edge, width), BF16),
            ((2 * EDGE + half_edge, width), BF16),
            ((ROWS, width), BF16),
            ((ROWS, width), BF16),
            ((wide, width), BF16),
        ],
        LEFT + 7,
        1 << 30,
    )

    result = own
    upstream = None
    upstream_next = None
    for step in range(sections):
        layer = sections - 1 - step
        if step > 0:
            total, message, dots = call(
                mixer_kernel,
                "mixer",
                placed(
                    "saaavaav", group_valid, upstream, upstream_next, slope, kernel, out_weight, attended, logs
                ),
                step_outs,
                [
                    ((ROWS, width), BF16),
                    ((ROWS, width), BF16),
                    ((EDGE, width), BF16),
                    ((ROWS + EDGE, width), F32),
                    ((wide, width), BF16),
                    ((ROWS, wide), BF16),
                ],
                5,
                1 << 30,
            )
        here = [layer]
        grad2 = moved(message, across(-2, here))
        grad4 = moved(message, across(-4, here))
        peer_grad = moved(message, swap)
        partial, key_sum, value_sum = call(
            query_kernel,
            "own_queries",
            placed(
                "saaaaaaaavva",
                group_valid,
                queries,
                kept,
                back2,
                back4,
                peer,
                peer_back2,
                peer_back4,
                message,
                logs,
                dots,
                query_weight,
            ),
            [((ROWS, width), F32), ((ROWS, wide), F32), ((ROWS, wide), F32)],
            [
                ((span, 2 * wide), BF16),
                ((ROWS, wide), BF16),
                ((ROWS, wide), BF16),
                ((ROWS + 16, wide), BF16),
                weight,
            ],
            LEFT + 4,
            1 << 30,
        )
        grad2, grad4, partial = lax.optimization_barrier((grad2, grad4, partial))
        peer_grad2 = moved(grad2, swap)
        peer_grad4 = moved(grad4, swap)
        input_grad, edge, result = call(
            key_kernel,
            "own_keys",
            placed(
                "saaaaaaaaaaaaavaaavvas",
                group_valid,
                kept,
                query_next2,
                query_next4,
                query_peer,
                query_peer_next2,
                query_peer_next4,
                grad2,
                grad4,
                peer_grad,
                peer_grad2,
                peer_grad4,
                key_weight,
                value_weight,
                norm_gain,
                own,
                total,
                partial,
                key_sum,
                value_sum,
                result,
                jnp.full((1,), layer, jnp.int32),
            ),
            [((ROWS, width), BF16), ((EDGE, width), BF16), ((ROWS, width), BF16)],
            [
                ((LEFT * ROWS, wide), BF16),
                ((LEFT * ROWS, wide), BF16),
                ((LEFT * 16, wide), BF16),
                ((16, LEFT * ROWS), F32),
                ((ROWS, wide), BF16),
                ((ROWS, wide), BF16),
                ((ROWS, 2 * wide), BF16),
                weight,
                weight,
                ((ROWS, width), BF16),
                ((ROWS, width), F32),
                ((ROWS, width), F32),
                ((ROWS, width), BF16),
            ],
            3 * LEFT + 7,
            1 << 30,
        )
        if layer > 0:
            upstream = moved(
                input_grad,
                [(at(layer, source), at(layer - 1, source)) for source in range(count)]
                + [(at(layer - 1, source), at(layer, source)) for source in range(count)],
            )
            upstream_next = moved(
                edge, [(at(layer, source), at(layer - 1, source - 1)) for source in range(1, count)]
            )
    return result[None]


def solution(mesh):
    placed = (
        P("section", "tm", None),
        P("tm", None),
        P("section", None, None),
        P("section", None, None),
        P("section", None, None),
        P("section", None, None),
        P("section", None, None),
        P("section", None),
        P(),
    )
    return jax.shard_map(
        shards, mesh=mesh, in_specs=placed, out_specs=P("section", "tm", None), check_vma=False
    )
```

```python
import jax
import jax.numpy as jnp
from jax import lax
from jax.experimental import pallas as pl
from jax.experimental.pallas import tpu as pltpu
from jax.sharding import PartitionSpec as P

HEAD_DIM = 64
PAIR = 128
ROWS = 128
LEFT = 4
EDGE = 32
SCALE = HEAD_DIM ** (-0.5)
NEGATIVE = -1e30
EPSILON = 1e-05
F32 = jnp.float32
BF16 = jnp.bfloat16
VMEM_LIMIT = 20 << 20
VMEM_WHOLE = 56 << 20


def dot_nn(a, b):
    return lax.dot_general(a, b, (((1,), (0,)), ((), ())), preferred_element_type=F32)


def dot_nt(a, b):
    return lax.dot_general(a, b, (((1,), (1,)), ((), ())), preferred_element_type=F32)


def valid_count(valid_ref, block):
    groups = valid_ref.shape[0]
    inside = (block >= 0) & (block < groups)
    return jnp.where(inside, valid_ref[jnp.clip(block, 0, groups - 1)], 0)


def even_half(rows):
    return lax.broadcasted_iota(jnp.int32, (rows, PAIR), 1) < HEAD_DIM


def unit_rows(values):
    center = values - jnp.mean(values, axis=-1, keepdims=True)
    spread = jnp.mean(center * center, axis=-1, keepdims=True)
    inverse = lax.rsqrt(spread + EPSILON)
    return center * inverse, inverse


def three_parts(value):
    first = value.astype(BF16)
    rest = value - first.astype(F32)
    second = rest.astype(BF16)
    third = (rest - second.astype(F32)).astype(BF16)
    return first, second, third


def shift_rows(value, amount):
    if amount == 0:
        return value
    return pltpu.roll(value, value.shape[0] - amount, 0)


def tap_sum(padded, kernel_ref, lanes, first, step, rows):
    taps = kernel_ref.shape[0]
    total = jnp.zeros((rows, padded.shape[1]), F32)
    for phase in range(8):
        moved = None
        for tap in range(taps):
            offset = first + step * tap
            if offset % 8 != phase:
                continue
            if moved is None:
                moved = shift_rows(padded, phase)
            base = offset - phase
            total = total + kernel_ref[tap : tap + 1, lanes] * moved[base : base + rows]
    return total


def project_kernel(
    own_ref,
    top_ref,
    gain_ref,
    w_query_ref,
    w_key_ref,
    w_value_ref,
    queries_ref,
    kept_ref,
    ahead_ref,
    behind_ref,
    normed,
    w_query,
    w_key,
    w_value,
    semaphores,
):
    chunk = 16
    loader = Loader(semaphores, None)
    loader.get(w_key, w_key_ref)
    loader.get(w_value, w_value_ref)
    late = Loader(semaphores.at[2:], None)
    late.get(w_query, w_query_ref)

    def norm_step(step, carry):
        rows = pl.ds(pl.multiple_of(step * chunk, chunk), chunk)
        unit, _ = unit_rows(own_ref[rows, :].astype(F32))
        normed[rows, :] = (unit * gain_ref[...]).astype(BF16)
        return carry

    lax.fori_loop(0, ROWS // chunk, norm_step, 0, unroll=2)
    wide = w_key_ref.shape[1]
    half = EDGE // 2
    loader.wait()
    keys = dot_nn(normed[...], w_key[...]).astype(BF16)
    values = dot_nn(normed[...], w_value[...]).astype(BF16)
    for ref in (kept_ref, ahead_ref, behind_ref):
        ref[0:ROWS, 0:wide] = keys
        ref[0:ROWS, wide : 2 * wide] = values
    late.wait()
    queries = dot_nn(normed[...], w_query[...]).astype(BF16)
    queries_ref[...] = queries
    ahead_ref[ROWS : ROWS + EDGE, :] = own_ref[ROWS - EDGE : ROWS, :]
    ahead_ref[ROWS + EDGE : ROWS + EDGE + half, 0:wide] = queries[ROWS - EDGE : ROWS - half]
    ahead_ref[ROWS + EDGE : ROWS + EDGE + half, wide : 2 * wide] = queries[ROWS - half : ROWS]
    behind_ref[ROWS : ROWS + EDGE, :] = own_ref[0:EDGE, :]
    behind_ref[ROWS + EDGE : ROWS + EDGE + half, 0:wide] = queries[0:half]
    behind_ref[ROWS + EDGE : ROWS + EDGE + half, wide : 2 * wide] = queries[half:EDGE]
    behind_ref[ROWS + EDGE + half : ROWS + 2 * EDGE + half, :] = top_ref[0:EDGE, :]


class Loader:
    def __init__(self, semaphores, odd):
        self.semaphores = semaphores
        self.odd = odd
        self.used = 0
        self.waiting = []

    def get(self, target, when_odd, when_even=None, rows=None):
        semaphore = self.semaphores.at[self.used]
        self.used += 1

        def copy(source):
            view = source if rows is None else source.at[rows[0] : rows[1]]
            return pltpu.make_async_copy(view, target, semaphore)

        if when_even is None or when_even is when_odd:
            copy(when_odd).start()
        else:

            @pl.when(self.odd)
            def _():
                copy(when_odd).start()

            @pl.when(jnp.logical_not(self.odd))
            def _():
                copy(when_even).start()

        self.waiting.append(copy(when_odd))

    def window(self, target, sources):
        for index, (when_odd, when_even) in enumerate(sources):
            self.get(target.at[index * ROWS : (index + 1) * ROWS], when_odd, when_even, (0, ROWS))

    def wait(self):
        for copy in self.waiting:
            copy.wait()
        self.waiting = []


def masked_half(value, half):
    keep = even_half(value.shape[0])
    if half:
        keep = jnp.logical_not(keep)
    return jnp.where(keep, value, jnp.zeros_like(value))


def pair_shares(scores, allowed):
    part = jnp.where(allowed, scores, NEGATIVE)
    highest = jnp.max(part, axis=-1, keepdims=True)
    exped = jnp.exp(part - highest)
    summed = jnp.sum(exped, axis=-1, keepdims=True)
    return (exped * (1.0 / summed)).astype(BF16), highest, summed


def attend_kernel(
    valid_ref,
    queries_ref,
    kept_ref,
    back2_ref,
    back4_ref,
    peer_ref,
    peer_back2_ref,
    peer_back4_ref,
    after_ref,
    attended_ref,
    log_ref,
    window,
    query_all,
    packed,
    semaphores,
):
    place = lax.axis_index("tm")
    odd = lax.rem(place, 2) == 1
    wide = queries_ref.shape[1]
    half_edge = EDGE // 2
    loader = Loader(semaphores, odd)
    loader.get(query_all.at[0:ROWS], queries_ref)
    loader.get(packed, after_ref, rows=(ROWS + EDGE, ROWS + EDGE + half_edge))
    loader.window(
        window,
        (
            (back4_ref, back4_ref),
            (peer_back2_ref, peer_back4_ref),
            (back2_ref, back2_ref),
            (peer_ref, peer_back2_ref),
            (kept_ref, kept_ref),
            (after_ref, after_ref),
        ),
    )
    loader.wait()
    query_all[ROWS : ROWS + half_edge, :] = packed[:, 0:wide]
    query_all[ROWS + half_edge : ROWS + EDGE, :] = packed[:, wide : 2 * wide]
    key_lane = lax.broadcasted_iota(jnp.int32, (1, ROWS), 1)
    allowed = jnp.concatenate(
        [key_lane < valid_count(valid_ref, place + block - LEFT) for block in range(LEFT + 2)], axis=1
    )
    span = (LEFT + 1) * ROWS
    log_lane = lax.broadcasted_iota(jnp.int32, (ROWS, PAIR), 1)
    logs = jnp.zeros((ROWS, PAIR), F32)
    for pair in range(wide // PAIR):
        lanes = slice(pair * PAIR, (pair + 1) * PAIR)
        value_lanes = slice(wide + pair * PAIR, wide + (pair + 1) * PAIR)
        totals = [None, None]
        for half in range(2):
            scores = dot_nt(query_all[:, lanes], masked_half(window[:, lanes], half)) * SCALE
            value_half = masked_half(window[:, value_lanes], half)
            for group, (low, high, first) in enumerate(((0, ROWS, 0), (ROWS, ROWS + EDGE, ROWS))):
                shares_low, highest, summed = pair_shares(
                    scores[low:high, first : first + span], allowed[:, first : first + span]
                )
                product = dot_nn(shares_low, value_half[first : first + span])
                totals[group] = product if totals[group] is None else totals[group] + product
                if group == 0:
                    logs = jnp.where(log_lane == 2 * pair + half, highest + jnp.log(summed), logs)
        attended_ref[0:ROWS, lanes] = totals[0].astype(BF16)
        attended_ref[ROWS : ROWS + EDGE, lanes] = totals[1].astype(BF16)
    log_ref[...] = logs


def mixer_body(
    count, upstream_ref, next_rows, slope_ref, kernel_ref, w_out_ref, attended, log_ref, total_ref, message_ref, dot_ref, total_low, ready=lambda: None
):
    row_ids = lax.broadcasted_iota(jnp.int32, (ROWS, PAIR), 0)
    taps = kernel_ref.shape[0]

    def conv_step(step, carry):
        lanes = pl.ds(pl.multiple_of(step * PAIR, PAIR), PAIR)
        upper = upstream_ref[:, lanes].astype(F32)
        stacked = jnp.concatenate([upper, next_rows(lanes)], axis=0)
        grads = (stacked * slope_ref[:, lanes]).astype(BF16).astype(F32)
        back = tap_sum(grads, kernel_ref, lanes, taps - 1, -1, ROWS)
        total = upper + jnp.where(row_ids < count, back, 0.0)
        total_ref[:, lanes] = total
        total_low[:, lanes] = total.astype(BF16)
        return carry

    lax.fori_loop(0, upstream_ref.shape[1] // PAIR, conv_step, 0)
    ready()
    out_grad = dot_nt(total_low[...], w_out_ref[...]).astype(BF16)
    message_ref[0:ROWS, :] = out_grad
    product = out_grad.astype(F32) * attended[...].astype(F32)
    high = product.astype(BF16)
    low = (product - high.astype(F32)).astype(BF16)
    width = product.shape[1]
    head_of = lax.broadcasted_iota(jnp.int32, (PAIR, width), 1) // HEAD_DIM
    chosen = (head_of == lax.broadcasted_iota(jnp.int32, (PAIR, width), 0)).astype(F32).astype(BF16)
    dots = dot_nt(high, chosen) + dot_nt(low, chosen)
    dot_ref[...] = dots
    stacked = jnp.concatenate([log_ref[...].T[0:8], dots.T[0:8]], axis=0)
    message_ref[ROWS : ROWS + 16, :] = jnp.zeros((16, width), BF16)
    for index, part in enumerate(three_parts(stacked)):
        message_ref[ROWS : ROWS + 16, index * PAIR : (index + 1) * PAIR] = part


def mix_kernel(
    valid_ref,
    own_ref,
    top_ref,
    attended_ref,
    log_ref,
    back2_ref,
    back4_ref,
    back5_ref,
    peer_ref,
    peer_back2_ref,
    peer_back4_ref,
    after_ref,
    w_out_ref,
    kernel_ref,
    slope_ref,
    total_ref,
    message_ref,
    dot_ref,
    window,
    query_tail,
    attended_all,
    mixed,
    total_low,
    before_rows,
    after_rows,
    own,
    top,
    w_out,
    semaphores,
):
    place = lax.axis_index("tm")
    odd = lax.rem(place, 2) == 1
    wide = query_tail.shape[1]
    half_edge = EDGE // 2
    counts = [valid_count(valid_ref, place + block - LEFT - 1) for block in range(LEFT + 3)]
    loader = Loader(semaphores, odd)
    loader.get(before_rows, peer_ref, peer_back2_ref, (ROWS, ROWS + EDGE + half_edge))
    loader.window(
        window,
        (
            (peer_back4_ref, back5_ref),
            (back4_ref, back4_ref),
            (peer_back2_ref, peer_back4_ref),
            (back2_ref, back2_ref),
            (peer_ref, peer_back2_ref),
        ),
    )
    late = Loader(semaphores.at[LEFT + 2 :], odd)
    late.get(attended_all.at[EDGE : 2 * EDGE + ROWS], attended_ref)
    late.get(w_out, w_out_ref)
    late.get(own, own_ref)
    late.get(after_rows, after_ref, rows=(ROWS, ROWS + 2 * EDGE + half_edge))
    late.get(top, top_ref)
    loader.wait()
    query_tail[0:half_edge, :] = before_rows[EDGE : EDGE + half_edge, 0:wide]
    query_tail[half_edge:EDGE, :] = before_rows[EDGE : EDGE + half_edge, wide : 2 * wide]
    key_lane = lax.broadcasted_iota(jnp.int32, (1, ROWS), 1)
    allowed = jnp.concatenate([key_lane < count for count in counts[: LEFT + 1]], axis=1)
    for pair in range(wide // PAIR):
        lanes = slice(pair * PAIR, (pair + 1) * PAIR)
        value_lanes = slice(wide + pair * PAIR, wide + (pair + 1) * PAIR)
        total = None
        for half in range(2):
            scores = dot_nt(query_tail[:, lanes], masked_half(window[:, lanes], half)) * SCALE
            shares_low, _, _ = pair_shares(scores, allowed)
            product = dot_nn(shares_low, masked_half(window[:, value_lanes], half))
            total = product if total is None else total + product
        attended_all[0:EDGE, lanes] = total.astype(BF16)
    late.wait()
    projected = dot_nn(attended_all[...], w_out[...])
    row_ids = lax.broadcasted_iota(jnp.int32, (ROWS, 1), 0)
    edge_ids = lax.broadcasted_iota(jnp.int32, (EDGE, 1), 0)
    before = projected[0:EDGE] + before_rows[0:EDGE, :].astype(F32)
    here = projected[EDGE : EDGE + ROWS] + own[...].astype(F32)
    after = projected[EDGE + ROWS :] + after_rows[0:EDGE, :].astype(F32)
    before = jnp.where(edge_ids + (ROWS - EDGE) < counts[LEFT], before, 0.0)
    here = jnp.where(row_ids < counts[LEFT + 1], here, 0.0)
    after = jnp.where(edge_ids < counts[LEFT + 2], after, 0.0)
    mixed[0:EDGE, :] = before.astype(BF16).astype(F32)
    mixed[EDGE : EDGE + ROWS, :] = here.astype(BF16).astype(F32)
    mixed[EDGE + ROWS :, :] = after.astype(BF16).astype(F32)
    taps = kernel_ref.shape[0]

    def conv_step(step, carry):
        lanes = pl.ds(pl.multiple_of(step * PAIR, PAIR), PAIR)
        output = tap_sum(mixed[:, lanes], kernel_ref, lanes, EDGE - (taps - 1), 1, ROWS + EDGE)
        gate = 1.0 / (1.0 + jnp.exp(-output))
        slope_ref[:, lanes] = gate * (1.0 + output * (1.0 - gate))
        return carry

    lax.fori_loop(0, own.shape[1] // PAIR, conv_step, 0)
    first = EDGE + half_edge
    mixer_body(
        counts[LEFT + 1],
        top,
        lambda lanes: after_rows[first : first + EDGE, lanes].astype(F32),
        slope_ref,
        kernel_ref,
        w_out,
        attended_all[EDGE : EDGE + ROWS, :],
        log_ref,
        total_ref,
        message_ref,
        dot_ref,
        total_low,
    )


def mixer_kernel(
    valid_ref,
    upstream_ref,
    next_ref,
    slope_ref,
    kernel_ref,
    w_out_ref,
    attended_ref,
    log_ref,
    total_ref,
    message_ref,
    dot_ref,
    total_low,
    upstream,
    next_rows,
    slope,
    w_out,
    attended,
    semaphores,
):
    loader = Loader(semaphores, None)
    loader.get(upstream, upstream_ref)
    loader.get(next_rows, next_ref)
    loader.get(slope, slope_ref)
    late = Loader(semaphores.at[3:], None)
    late.get(attended, attended_ref, rows=(0, ROWS))
    late.get(w_out, w_out_ref)
    loader.wait()
    mixer_body(
        valid_count(valid_ref, lax.axis_index("tm")),
        upstream,
        lambda lanes: next_rows[:, lanes].astype(F32),
        slope,
        kernel_ref,
        w_out,
        attended,
        log_ref,
        total_ref,
        message_ref,
        dot_ref,
        total_low,
        late.wait,
    )


def key_terms(key_pair, value_pair, query_pair, grad_pair, logs, dots, key_valid):
    share_halves = []
    score_halves = []
    query_halves = [masked_half(query_pair, half) for half in range(2)]
    grad_halves = [masked_half(grad_pair, half) for half in range(2)]
    for half in range(2):
        scores = dot_nt(key_pair, query_halves[half]) * SCALE
        shares = jnp.exp(jnp.where(key_valid, scores, NEGATIVE) - logs[half])
        share_grad = dot_nt(value_pair, grad_halves[half])
        score_halves.append((shares * (share_grad - dots[half])).astype(BF16))
        share_halves.append(shares.astype(BF16))
    key_sum = None
    value_sum = None
    for block in range(query_pair.shape[0] // ROWS):
        rows = slice(block * ROWS, (block + 1) * ROWS)
        key_term = dot_nn(
            jnp.concatenate([score[:, rows] for score in score_halves], axis=1),
            jnp.concatenate([query[rows] for query in query_halves], axis=0),
        )
        value_term = dot_nn(
            jnp.concatenate([share[:, rows] for share in share_halves], axis=1),
            jnp.concatenate([grad[rows] for grad in grad_halves], axis=0),
        )
        key_term = (key_term * SCALE).astype(BF16).astype(F32)
        value_term = value_term.astype(BF16).astype(F32)
        key_sum = key_term if key_sum is None else key_sum + key_term
        value_sum = value_term if value_sum is None else value_sum + value_term
    return key_sum, value_sum


def message_stats(tail):
    tail = tail.astype(F32)
    return tail[:, 0:PAIR] + tail[:, PAIR : 2 * PAIR] + tail[:, 2 * PAIR : 3 * PAIR]


def query_kernel(
    valid_ref,
    queries_ref,
    kept_ref,
    back2_ref,
    back4_ref,
    peer_ref,
    peer_back2_ref,
    peer_back4_ref,
    message_ref,
    log_ref,
    dot_ref,
    w_query_ref,
    out_ref,
    key_sum_ref,
    value_sum_ref,
    window,
    query_grad,
    queries,
    message,
    w_query,
    semaphores,
):
    place = lax.axis_index("tm")
    odd = lax.rem(place, 2) == 1
    wide = queries_ref.shape[1]
    loader = Loader(semaphores, odd)
    loader.get(queries, queries_ref)
    loader.get(message, message_ref)
    loader.window(
        window,
        (
            (back4_ref, back4_ref),
            (peer_back2_ref, peer_back4_ref),
            (back2_ref, back2_ref),
            (peer_ref, peer_back2_ref),
            (kept_ref, kept_ref),
        ),
    )
    late = Loader(semaphores.at[LEFT + 3 :], odd)
    late.get(w_query, w_query_ref)
    loader.wait()
    own_rows = slice(LEFT * ROWS, (LEFT + 1) * ROWS)
    key_lane = lax.broadcasted_iota(jnp.int32, (1, ROWS), 1)
    allowed = jnp.concatenate(
        [key_lane < valid_count(valid_ref, place + block - LEFT) for block in range(LEFT + 1)], axis=1
    )
    key_valid = lax.broadcasted_iota(jnp.int32, (ROWS, ROWS), 0) < valid_count(valid_ref, place)
    stats = message_stats(message[ROWS : ROWS + 16, :])
    for pair in range(wide // PAIR):
        lanes = slice(pair * PAIR, (pair + 1) * PAIR)
        value_lanes = slice(wide + pair * PAIR, wide + (pair + 1) * PAIR)
        query_pair = queries[:, lanes]
        grad_pair = message[0:ROWS, lanes]
        total = None
        for half in range(2):
            key_half = masked_half(window[:, lanes], half)
            value_half = masked_half(window[:, value_lanes], half)
            head = 2 * pair + half
            scores = dot_nt(query_pair, key_half) * SCALE
            shares = jnp.exp(jnp.where(allowed, scores, NEGATIVE) - log_ref[:, head : head + 1])
            share_grad = dot_nt(grad_pair, value_half)
            score_grad = (shares * (share_grad - dot_ref[:, head : head + 1])).astype(BF16)
            product = dot_nn(score_grad, key_half)
            total = product if total is None else total + product
        query_grad[:, lanes] = (total * SCALE).astype(BF16)
        heads = (2 * pair, 2 * pair + 1)
        key_sum_ref[:, lanes], value_sum_ref[:, lanes] = key_terms(
            window[own_rows, lanes],
            window[own_rows, value_lanes],
            query_pair,
            grad_pair,
            [stats[head : head + 1] for head in heads],
            [stats[8 + head : 9 + head] for head in heads],
            key_valid,
        )
    late.wait()
    out_ref[...] = dot_nt(query_grad[...], w_query[...])


def key_kernel(
    valid_ref,
    kept_ref,
    query_next2_ref,
    query_next4_ref,
    query_peer_ref,
    query_peer_next2_ref,
    query_peer_next4_ref,
    next2_ref,
    next4_ref,
    peer_ref,
    peer_next2_ref,
    peer_next4_ref,
    w_key_ref,
    w_value_ref,
    gain_ref,
    own_ref,
    total_ref,
    partial_ref,
    key_sum_ref,
    value_sum_ref,
    result_ref,
    keep_ref,
    out_ref,
    edge_ref,
    held_ref,
    grads,
    queries,
    tails,
    stats,
    key_grad,
    value_grad,
    kept,
    w_key,
    w_value,
    own,
    total,
    partial,
    result,
    semaphores,
):
    place = lax.axis_index("tm")
    odd = lax.rem(place, 2) == 1
    count = valid_count(valid_ref, place)
    wide = grads.shape[1]
    loader = Loader(semaphores, odd)
    messages = (
        (peer_next2_ref, peer_ref),
        (next2_ref, next2_ref),
        (peer_next4_ref, peer_next2_ref),
        (next4_ref, next4_ref),
    )
    loader.get(kept, kept_ref)
    loader.window(grads, messages)
    for block, (when_odd, when_even) in enumerate(messages):
        loader.get(tails.at[block * 16 : block * 16 + 16], when_odd, when_even, (ROWS, ROWS + 16))
    loader.window(
        queries,
        (
            (query_peer_next2_ref, query_peer_ref),
            (query_next2_ref, query_next2_ref),
            (query_peer_next4_ref, query_peer_next2_ref),
            (query_next4_ref, query_next4_ref),
        ),
    )
    late = Loader(semaphores.at[loader.used :], odd)
    late.get(w_key, w_key_ref)
    late.get(w_value, w_value_ref)
    late.get(own, own_ref)
    late.get(total, total_ref)
    late.get(partial, partial_ref)
    late.get(result, result_ref)
    loader.wait()
    for block in range(LEFT):
        stats[:, block * ROWS : (block + 1) * ROWS] = message_stats(tails[block * 16 : block * 16 + 16, :])
    key_valid = lax.broadcasted_iota(jnp.int32, (ROWS, LEFT * ROWS), 0) < count
    for pair in range(wide // PAIR):
        lanes = slice(pair * PAIR, (pair + 1) * PAIR)
        heads = (2 * pair, 2 * pair + 1)
        key_sum, value_sum = key_terms(
            kept[:, lanes],
            kept[:, slice(wide + pair * PAIR, wide + (pair + 1) * PAIR)],
            queries[:, lanes],
            grads[:, lanes],
            [stats[head : head + 1, :] for head in heads],
            [stats[8 + head : 9 + head, :] for head in heads],
            key_valid,
        )
        key_grad[:, lanes] = (key_sum_ref[:, lanes] + key_sum).astype(BF16)
        value_grad[:, lanes] = (value_sum_ref[:, lanes] + value_sum).astype(BF16)
    late.wait()
    normed_grad = partial[...] + dot_nt(key_grad[...], w_key[...])
    normed_grad = normed_grad + dot_nt(value_grad[...], w_value[...])
    scaled = normed_grad * gain_ref[...]
    unit, inverse = unit_rows(own[...].astype(F32))
    back = inverse * (
        scaled
        - jnp.mean(scaled, axis=-1, keepdims=True)
        - unit * jnp.mean(scaled * unit, axis=-1, keepdims=True)
    )
    grad = total[...] + back
    out_ref[...] = grad.astype(BF16)
    edge_ref[...] = grad[0:EDGE].astype(BF16)
    mine = lax.axis_index("section") == keep_ref[0]
    held_ref[...] = jnp.where(mine, grad, result[...].astype(F32)).astype(BF16)


def call(kernel, name, operands, outs, scratch, copies, flops, limit=VMEM_LIMIT):
    kinds = {
        "s": pl.BlockSpec(memory_space=pltpu.SMEM),
        "v": pl.BlockSpec(memory_space=pltpu.VMEM),
        "a": pl.BlockSpec(memory_space=pl.ANY),
    }
    return pl.pallas_call(
        kernel,
        name=name,
        in_specs=[kinds[place] for _, place in operands],
        out_specs=[kinds["v"]] * len(outs),
        out_shape=[jax.ShapeDtypeStruct(shape, dtype) for shape, dtype in outs],
        scratch_shapes=[pltpu.VMEM(shape, dtype) for shape, dtype in scratch]
        + [pltpu.SemaphoreType.DMA((copies,))],
        compiler_params=pltpu.CompilerParams(vmem_limit_bytes=limit),
        cost_estimate=pl.CostEstimate(flops=flops, bytes_accessed=4 << 20, transcendentals=0),
    )(*[array for array, _ in operands])


def placed(kinds, *arrays):
    return list(zip(arrays, kinds, strict=True))


def after(value, *others):
    return lax.optimization_barrier((value, *others))[0]


def shards(
    layer_inputs, top_grad, w_query, w_key, w_value, w_out, conv_kernel, norm_gain, group_valid
):
    own = layer_inputs[0]
    width = own.shape[1]
    wide = w_query.shape[2]
    query_weight = w_query[0]
    key_weight = w_key[0]
    value_weight = w_value[0]
    out_weight = w_out[0]
    kernel = conv_kernel[0]
    sections = lax.axis_size("section")
    count = lax.axis_size("tm")

    def moved(value, pairs):
        return lax.ppermute(value, ("tm", "section"), pairs)

    def at(layer, frame):
        return frame * sections + layer

    def across(steps, chosen):
        return [
            (at(section, source), at(section, source + steps))
            for section in chosen
            for source in range(max(0, -steps), min(count, count - steps))
        ]

    every = range(sections)
    half_edge = EDGE // 2
    swap = [(at(section, source), at(section, source ^ 1)) for section in every for source in range(count)]
    weight = ((width, wide), BF16)
    queries, kept, ahead, behind = call(
        project_kernel,
        "project",
        placed("vvvaaa", own, top_grad, norm_gain, query_weight, key_weight, value_weight),
        [
            ((ROWS, wide), BF16),
            ((ROWS, 2 * wide), BF16),
            ((ROWS + EDGE + half_edge, width), BF16),
            ((ROWS + 2 * EDGE + half_edge, width), BF16),
        ],
        [((ROWS, width), BF16), weight, weight, weight],
        3,
        1 << 30,
        VMEM_WHOLE,
    )
    back2 = moved(ahead, across(2, every))
    back4 = moved(kept, across(4, every))
    after1 = moved(behind, across(-1, every))
    query_next2 = moved(queries, across(-2, every))
    query_next4 = moved(queries, across(-4, every))
    peer = moved(ahead, swap)
    query_peer = moved(queries, swap)
    peer_back2 = moved(back2, swap)
    peer_back4 = moved(back4, swap)
    query_peer_next2 = moved(query_next2, swap)
    query_peer_next4 = moved(query_next4, swap)
    far_pairs = [
        (at(section, source), at(section, source + 5))
        for section in every
        for source in range(1, count - 5, 2)
    ]
    back5 = moved(after(kept, back2), far_pairs)
    query_next2, query_next4, query_peer, query_peer_next2, query_peer_next4, after1 = (
        lax.optimization_barrier(
            (query_next2, query_next4, query_peer, query_peer_next2, query_peer_next4, after1)
        )
    )

    span = (LEFT + 1) * ROWS
    attended, logs = call(
        attend_kernel,
        "attend",
        placed("saaaaaaaa", group_valid, queries, kept, back2, back4, peer, peer_back2, peer_back4, after1),
        [((ROWS + EDGE, wide), BF16), ((ROWS, PAIR), F32)],
        [(((LEFT + 2) * ROWS, 2 * wide), BF16), ((ROWS + EDGE, wide), BF16), ((half_edge, 2 * wide), BF16)],
        LEFT + 4,
        1 << 30,
    )
    back5 = after(back5, attended)
    step_outs = [((ROWS, width), F32), ((ROWS + 16, wide), BF16), ((ROWS, PAIR), F32)]
    slope, total, message, dots = call(
        mix_kernel,
        "mix",
        placed(
            "saaavaaaaaaaav",
            group_valid,
            own,
            top_grad,
            attended,
            logs,
            back2,
            back4,
            back5,
            peer,
            peer_back2,
            peer_back4,
            after1,
            out_weight,
            kernel,
        ),
        [((ROWS + EDGE, width), F32)] + step_outs,
        [
            ((span, 2 * wide), BF16),
            ((EDGE, wide), BF16),
            ((ROWS + 2 * EDGE, wide), BF16),
            ((ROWS + 2 * EDGE, width), F32),
            ((ROWS, width), BF16),
            ((EDGE + half_edge, width), BF16),
            ((2 * EDGE + half_edge, width), BF16),
            ((ROWS, width), BF16),
            ((ROWS, width), BF16),
            ((wide, width), BF16),
        ],
        LEFT + 7,
        1 << 30,
    )

    result = own
    upstream = None
    upstream_next = None
    for step in range(sections):
        layer = sections - 1 - step
        if step > 0:
            total, message, dots = call(
                mixer_kernel,
                "mixer",
                placed(
                    "saaavaav", group_valid, upstream, upstream_next, slope, kernel, out_weight, attended, logs
                ),
                step_outs,
                [
                    ((ROWS, width), BF16),
                    ((ROWS, width), BF16),
                    ((EDGE, width), BF16),
                    ((ROWS + EDGE, width), F32),
                    ((wide, width), BF16),
                    ((ROWS, wide), BF16),
                ],
                5,
                1 << 30,
            )
        here = [layer]
        grad2 = moved(message, across(-2, here))
        grad4 = moved(message, across(-4, here))
        peer_grad = moved(message, swap)
        partial, key_sum, value_sum = call(
            query_kernel,
            "own_queries",
            placed(
                "saaaaaaaavva",
                group_valid,
                queries,
                kept,
                back2,
                back4,
                peer,
                peer_back2,
                peer_back4,
                message,
                logs,
                dots,
                query_weight,
            ),
            [((ROWS, width), F32), ((ROWS, wide), F32), ((ROWS, wide), F32)],
            [
                ((span, 2 * wide), BF16),
                ((ROWS, wide), BF16),
                ((ROWS, wide), BF16),
                ((ROWS + 16, wide), BF16),
                weight,
            ],
            LEFT + 4,
            1 << 30,
        )
        grad2, grad4, partial = lax.optimization_barrier((grad2, grad4, partial))
        peer_grad2 = moved(grad2, swap)
        peer_grad4 = moved(grad4, swap)
        input_grad, edge, result = call(
            key_kernel,
            "own_keys",
            placed(
                "saaaaaaaaaaaaavaaavvas",
                group_valid,
                kept,
                query_next2,
                query_next4,
                query_peer,
                query_peer_next2,
                query_peer_next4,
                grad2,
                grad4,
                peer_grad,
                peer_grad2,
                peer_grad4,
                key_weight,
                value_weight,
                norm_gain,
                own,
                total,
                partial,
                key_sum,
                value_sum,
                result,
                jnp.full((1,), layer, jnp.int32),
            ),
            [((ROWS, width), BF16), ((EDGE, width), BF16), ((ROWS, width), BF16)],
            [
                ((LEFT * ROWS, wide), BF16),
                ((LEFT * ROWS, wide), BF16),
                ((LEFT * 16, wide), BF16),
                ((16, LEFT * ROWS), F32),
                ((ROWS, wide), BF16),
                ((ROWS, wide), BF16),
                ((ROWS, 2 * wide), BF16),
                weight,
                weight,
                ((ROWS, width), BF16),
                ((ROWS, width), F32),
                ((ROWS, width), F32),
                ((ROWS, width), BF16),
            ],
            3 * LEFT + 7,
            1 << 30,
        )
        if layer > 0:
            upstream = moved(
                input_grad,
                [(at(layer, source), at(layer - 1, source)) for source in range(count)]
                + [(at(layer - 1, source), at(layer, source)) for source in range(count)],
            )
            upstream_next = moved(
                edge, [(at(layer, source), at(layer - 1, source - 1)) for source in range(1, count)]
            )
    return result[None]


def solution(mesh):
    placed = (
        P("section", "tm", None),
        P("tm", None),
        P("section", None, None),
        P("section", None, None),
        P("section", None, None),
        P("section", None, None),
        P("section", None, None),
        P("section", None),
        P(),
    )
    return jax.shard_map(
        shards, mesh=mesh, in_specs=placed, out_specs=P("section", "tm", None), check_vma=False
    )
```

```python
import jax
import jax.numpy as jnp
from jax import lax
from jax.experimental import pallas as pl
from jax.experimental.pallas import tpu as pltpu
from jax.sharding import PartitionSpec as P

HEAD_DIM = 64
PAIR = 128
ROWS = 128
LEFT = 4
EDGE = 32
SCALE = HEAD_DIM ** (-0.5)
NEGATIVE = -1e30
EPSILON = 1e-05
F32 = jnp.float32
BF16 = jnp.bfloat16
VMEM_LIMIT = 20 << 20
VMEM_WHOLE = 60 << 20


def dot_nn(a, b):
    return lax.dot_general(a, b, (((1,), (0,)), ((), ())), preferred_element_type=F32)


def dot_nt(a, b):
    return lax.dot_general(a, b, (((1,), (1,)), ((), ())), preferred_element_type=F32)


def valid_count(valid_ref, block):
    groups = valid_ref.shape[0]
    inside = (block >= 0) & (block < groups)
    return jnp.where(inside, valid_ref[jnp.clip(block, 0, groups - 1)], 0)


def even_half(rows):
    return lax.broadcasted_iota(jnp.int32, (rows, PAIR), 1) < HEAD_DIM


def unit_rows(values):
    center = values - jnp.mean(values, axis=-1, keepdims=True)
    spread = jnp.mean(center * center, axis=-1, keepdims=True)
    inverse = lax.rsqrt(spread + EPSILON)
    return center * inverse, inverse


def three_parts(value):
    first = value.astype(BF16)
    rest = value - first.astype(F32)
    second = rest.astype(BF16)
    third = (rest - second.astype(F32)).astype(BF16)
    return first, second, third


def shift_rows(value, amount):
    if amount == 0:
        return value
    return pltpu.roll(value, value.shape[0] - amount, 0)


def tap_sum(padded, kernel_ref, lanes, first, step, rows):
    taps = kernel_ref.shape[0]
    total = jnp.zeros((rows, padded.shape[1]), F32)
    for phase in range(8):
        moved = None
        for tap in range(taps):
            offset = first + step * tap
            if offset % 8 != phase:
                continue
            if moved is None:
                moved = shift_rows(padded, phase)
            base = offset - phase
            total = total + kernel_ref[tap : tap + 1, lanes] * moved[base : base + rows]
    return total


def project_kernel(
    own_ref,
    top_ref,
    gain_ref,
    w_query_ref,
    w_key_ref,
    w_value_ref,
    queries_ref,
    kept_ref,
    ahead_ref,
    behind_ref,
    normed,
    own,
    top,
    w_query,
    w_key,
    w_value,
    semaphores,
):
    chunk = 16
    loads = [
        pltpu.make_async_copy(source, target, semaphores.at[index])
        for index, (source, target) in enumerate(
            (
                (own_ref, own),
                (w_key_ref, w_key),
                (w_value_ref, w_value),
                (w_query_ref, w_query),
                (top_ref.at[0:EDGE], top),
            )
        )
    ]
    for load in loads:
        load.start()
    loads[0].wait()

    def norm_step(step, carry):
        rows = pl.ds(pl.multiple_of(step * chunk, chunk), chunk)
        unit, _ = unit_rows(own[rows, :].astype(F32))
        normed[rows, :] = (unit * gain_ref[...]).astype(BF16)
        return carry

    lax.fori_loop(0, ROWS // chunk, norm_step, 0, unroll=2)
    wide = w_key_ref.shape[1]
    half = EDGE // 2
    loads[1].wait()
    keys = dot_nn(normed[...], w_key[...]).astype(BF16)
    loads[2].wait()
    values = dot_nn(normed[...], w_value[...]).astype(BF16)
    for ref in (kept_ref, ahead_ref, behind_ref):
        ref[0:ROWS, 0:wide] = keys
        ref[0:ROWS, wide : 2 * wide] = values
    loads[3].wait()
    loads[4].wait()
    queries = dot_nn(normed[...], w_query[...]).astype(BF16)
    queries_ref[...] = queries
    ahead_ref[ROWS : ROWS + EDGE, :] = own[ROWS - EDGE : ROWS, :]
    ahead_ref[ROWS + EDGE : ROWS + EDGE + half, 0:wide] = queries[ROWS - EDGE : ROWS - half]
    ahead_ref[ROWS + EDGE : ROWS + EDGE + half, wide : 2 * wide] = queries[ROWS - half : ROWS]
    behind_ref[ROWS : ROWS + EDGE, :] = own[0:EDGE, :]
    behind_ref[ROWS + EDGE : ROWS + EDGE + half, 0:wide] = queries[0:half]
    behind_ref[ROWS + EDGE : ROWS + EDGE + half, wide : 2 * wide] = queries[half:EDGE]
    behind_ref[ROWS + EDGE + half : ROWS + 2 * EDGE + half, :] = top[...]


def choose_rows(target, odd, when_odd, when_even, rows):
    if when_even is when_odd:
        target[...] = when_odd[rows, :]
        return

    @pl.when(odd)
    def _():
        target[...] = when_odd[rows, :]

    @pl.when(jnp.logical_not(odd))
    def _():
        target[...] = when_even[rows, :]


def choose_blocks(target, odd, sources):
    for index, (when_odd, when_even) in enumerate(sources):
        choose_rows(target.at[index * ROWS : (index + 1) * ROWS], odd, when_odd, when_even, slice(0, ROWS))


def masked_half(value, half):
    keep = even_half(value.shape[0])
    if half:
        keep = jnp.logical_not(keep)
    return jnp.where(keep, value, jnp.zeros_like(value))


def pair_shares(scores, allowed):
    part = jnp.where(allowed, scores, NEGATIVE)
    highest = jnp.max(part, axis=-1, keepdims=True)
    exped = jnp.exp(part - highest)
    summed = jnp.sum(exped, axis=-1, keepdims=True)
    return (exped * (1.0 / summed)).astype(BF16), highest, summed


def attend_kernel(
    valid_ref,
    queries_ref,
    kept_ref,
    back2_ref,
    back4_ref,
    peer_ref,
    peer_back2_ref,
    peer_back4_ref,
    after_ref,
    attended_ref,
    log_ref,
    window,
    query_all,
):
    place = lax.axis_index("tm")
    odd = lax.rem(place, 2) == 1
    wide = queries_ref.shape[1]
    half_edge = EDGE // 2
    packed = after_ref[ROWS + EDGE : ROWS + EDGE + half_edge, :]
    query_all[0:ROWS, :] = queries_ref[...]
    choose_blocks(
        window,
        odd,
        (
            (back4_ref, back4_ref),
            (peer_back2_ref, peer_back4_ref),
            (back2_ref, back2_ref),
            (peer_ref, peer_back2_ref),
            (kept_ref, kept_ref),
            (after_ref, after_ref),
        ),
    )
    query_all[ROWS : ROWS + half_edge, :] = packed[:, 0:wide]
    query_all[ROWS + half_edge : ROWS + EDGE, :] = packed[:, wide : 2 * wide]
    key_lane = lax.broadcasted_iota(jnp.int32, (1, ROWS), 1)
    allowed = jnp.concatenate(
        [key_lane < valid_count(valid_ref, place + block - LEFT) for block in range(LEFT + 2)], axis=1
    )
    span = (LEFT + 1) * ROWS
    log_lane = lax.broadcasted_iota(jnp.int32, (ROWS, PAIR), 1)
    logs = jnp.zeros((ROWS, PAIR), F32)
    for pair in range(wide // PAIR):
        lanes = slice(pair * PAIR, (pair + 1) * PAIR)
        value_lanes = slice(wide + pair * PAIR, wide + (pair + 1) * PAIR)
        totals = [None, None]
        for half in range(2):
            scores = dot_nt(query_all[:, lanes], masked_half(window[:, lanes], half)) * SCALE
            value_half = masked_half(window[:, value_lanes], half)
            for group, (low, high, first) in enumerate(((0, ROWS, 0), (ROWS, ROWS + EDGE, ROWS))):
                shares_low, highest, summed = pair_shares(
                    scores[low:high, first : first + span], allowed[:, first : first + span]
                )
                product = dot_nn(shares_low, value_half[first : first + span])
                totals[group] = product if totals[group] is None else totals[group] + product
                if group == 0:
                    logs = jnp.where(log_lane == 2 * pair + half, highest + jnp.log(summed), logs)
        attended_ref[0:ROWS, lanes] = totals[0].astype(BF16)
        attended_ref[ROWS : ROWS + EDGE, lanes] = totals[1].astype(BF16)
    log_ref[...] = logs


def mixer_body(
    count, upstream_ref, next_rows, slope_ref, kernel_ref, w_out_ref, attended, log_ref, total_ref, message_ref, dot_ref, total_low
):
    row_ids = lax.broadcasted_iota(jnp.int32, (ROWS, PAIR), 0)
    taps = kernel_ref.shape[0]

    def conv_step(step, carry):
        lanes = pl.ds(pl.multiple_of(step * PAIR, PAIR), PAIR)
        upper = upstream_ref[:, lanes].astype(F32)
        stacked = jnp.concatenate([upper, next_rows(lanes)], axis=0)
        grads = (stacked * slope_ref[:, lanes]).astype(BF16).astype(F32)
        back = tap_sum(grads, kernel_ref, lanes, taps - 1, -1, ROWS)
        total = upper + jnp.where(row_ids < count, back, 0.0)
        total_ref[:, lanes] = total
        total_low[:, lanes] = total.astype(BF16)
        return carry

    lax.fori_loop(0, upstream_ref.shape[1] // PAIR, conv_step, 0)
    out_grad = dot_nt(total_low[...], w_out_ref[...]).astype(BF16)
    message_ref[0:ROWS, :] = out_grad
    product = out_grad.astype(F32) * attended[...].astype(F32)
    high = product.astype(BF16)
    low = (product - high.astype(F32)).astype(BF16)
    width = product.shape[1]
    head_of = lax.broadcasted_iota(jnp.int32, (PAIR, width), 1) // HEAD_DIM
    chosen = (head_of == lax.broadcasted_iota(jnp.int32, (PAIR, width), 0)).astype(F32).astype(BF16)
    dots = dot_nt(high, chosen) + dot_nt(low, chosen)
    dot_ref[...] = dots
    stacked = jnp.concatenate([log_ref[...].T[0:8], dots.T[0:8]], axis=0)
    message_ref[ROWS : ROWS + 16, :] = jnp.zeros((16, width), BF16)
    for index, part in enumerate(three_parts(stacked)):
        message_ref[ROWS : ROWS + 16, index * PAIR : (index + 1) * PAIR] = part


def mix_kernel(
    valid_ref,
    own_ref,
    top_ref,
    attended_ref,
    log_ref,
    back2_ref,
    back4_ref,
    back5_ref,
    peer_ref,
    peer_back2_ref,
    peer_back4_ref,
    after_ref,
    w_out_ref,
    kernel_ref,
    slope_ref,
    total_ref,
    message_ref,
    dot_ref,
    window,
    query_tail,
    attended_all,
    mixed,
    total_low,
    before_rows,
):
    place = lax.axis_index("tm")
    odd = lax.rem(place, 2) == 1
    wide = query_tail.shape[1]
    half_edge = EDGE // 2
    counts = [valid_count(valid_ref, place + block - LEFT - 1) for block in range(LEFT + 3)]
    choose_rows(before_rows, odd, peer_ref, peer_back2_ref, slice(ROWS, ROWS + EDGE + half_edge))
    choose_blocks(
        window,
        odd,
        (
            (peer_back4_ref, back5_ref),
            (back4_ref, back4_ref),
            (peer_back2_ref, peer_back4_ref),
            (back2_ref, back2_ref),
            (peer_ref, peer_back2_ref),
        ),
    )
    attended_all[EDGE:, :] = attended_ref[...]
    query_tail[0:half_edge, :] = before_rows[EDGE : EDGE + half_edge, 0:wide]
    query_tail[half_edge:EDGE, :] = before_rows[EDGE : EDGE + half_edge, wide : 2 * wide]
    key_lane = lax.broadcasted_iota(jnp.int32, (1, ROWS), 1)
    allowed = jnp.concatenate([key_lane < count for count in counts[: LEFT + 1]], axis=1)
    for pair in range(wide // PAIR):
        lanes = slice(pair * PAIR, (pair + 1) * PAIR)
        value_lanes = slice(wide + pair * PAIR, wide + (pair + 1) * PAIR)
        total = None
        for half in range(2):
            scores = dot_nt(query_tail[:, lanes], masked_half(window[:, lanes], half)) * SCALE
            shares_low, _, _ = pair_shares(scores, allowed)
            product = dot_nn(shares_low, masked_half(window[:, value_lanes], half))
            total = product if total is None else total + product
        attended_all[0:EDGE, lanes] = total.astype(BF16)
    projected = dot_nn(attended_all[...], w_out_ref[...])
    row_ids = lax.broadcasted_iota(jnp.int32, (ROWS, 1), 0)
    edge_ids = lax.broadcasted_iota(jnp.int32, (EDGE, 1), 0)
    before = projected[0:EDGE] + before_rows[0:EDGE, :].astype(F32)
    here = projected[EDGE : EDGE + ROWS] + own_ref[...].astype(F32)
    after = projected[EDGE + ROWS :] + after_ref[ROWS : ROWS + EDGE, :].astype(F32)
    before = jnp.where(edge_ids + (ROWS - EDGE) < counts[LEFT], before, 0.0)
    here = jnp.where(row_ids < counts[LEFT + 1], here, 0.0)
    after = jnp.where(edge_ids < counts[LEFT + 2], after, 0.0)
    mixed[0:EDGE, :] = before.astype(BF16).astype(F32)
    mixed[EDGE : EDGE + ROWS, :] = here.astype(BF16).astype(F32)
    mixed[EDGE + ROWS :, :] = after.astype(BF16).astype(F32)
    taps = kernel_ref.shape[0]

    def conv_step(step, carry):
        lanes = pl.ds(pl.multiple_of(step * PAIR, PAIR), PAIR)
        output = tap_sum(mixed[:, lanes], kernel_ref, lanes, EDGE - (taps - 1), 1, ROWS + EDGE)
        gate = 1.0 / (1.0 + jnp.exp(-output))
        slope_ref[:, lanes] = gate * (1.0 + output * (1.0 - gate))
        return carry

    lax.fori_loop(0, own_ref.shape[1] // PAIR, conv_step, 0)
    first = ROWS + EDGE + half_edge
    mixer_body(
        counts[LEFT + 1],
        top_ref,
        lambda lanes: after_ref[first : first + EDGE, lanes].astype(F32),
        slope_ref,
        kernel_ref,
        w_out_ref,
        attended_all[EDGE : EDGE + ROWS, :],
        log_ref,
        total_ref,
        message_ref,
        dot_ref,
        total_low,
    )


def mixer_kernel(
    valid_ref,
    upstream_ref,
    next_ref,
    slope_ref,
    kernel_ref,
    w_out_ref,
    attended_ref,
    log_ref,
    total_ref,
    message_ref,
    dot_ref,
    total_low,
):
    mixer_body(
        valid_count(valid_ref, lax.axis_index("tm")),
        upstream_ref,
        lambda lanes: next_ref[:, lanes].astype(F32),
        slope_ref,
        kernel_ref,
        w_out_ref,
        attended_ref[0:ROWS, :],
        log_ref,
        total_ref,
        message_ref,
        dot_ref,
        total_low,
    )


def key_terms(key_pair, value_pair, query_pair, grad_pair, logs, dots, key_valid):
    share_halves = []
    score_halves = []
    query_halves = [masked_half(query_pair, half) for half in range(2)]
    grad_halves = [masked_half(grad_pair, half) for half in range(2)]
    for half in range(2):
        scores = dot_nt(key_pair, query_halves[half]) * SCALE
        shares = jnp.exp(jnp.where(key_valid, scores, NEGATIVE) - logs[half])
        share_grad = dot_nt(value_pair, grad_halves[half])
        score_halves.append((shares * (share_grad - dots[half])).astype(BF16))
        share_halves.append(shares.astype(BF16))
    key_sum = None
    value_sum = None
    for block in range(query_pair.shape[0] // ROWS):
        rows = slice(block * ROWS, (block + 1) * ROWS)
        key_term = dot_nn(
            jnp.concatenate([score[:, rows] for score in score_halves], axis=1),
            jnp.concatenate([query[rows] for query in query_halves], axis=0),
        )
        value_term = dot_nn(
            jnp.concatenate([share[:, rows] for share in share_halves], axis=1),
            jnp.concatenate([grad[rows] for grad in grad_halves], axis=0),
        )
        key_term = (key_term * SCALE).astype(BF16).astype(F32)
        value_term = value_term.astype(BF16).astype(F32)
        key_sum = key_term if key_sum is None else key_sum + key_term
        value_sum = value_term if value_sum is None else value_sum + value_term
    return key_sum, value_sum


def message_stats(tail):
    tail = tail.astype(F32)
    return tail[:, 0:PAIR] + tail[:, PAIR : 2 * PAIR] + tail[:, 2 * PAIR : 3 * PAIR]


def query_kernel(
    valid_ref,
    queries_ref,
    kept_ref,
    back2_ref,
    back4_ref,
    peer_ref,
    peer_back2_ref,
    peer_back4_ref,
    message_ref,
    log_ref,
    dot_ref,
    w_query_ref,
    out_ref,
    key_sum_ref,
    value_sum_ref,
    window,
    query_grad,
):
    place = lax.axis_index("tm")
    odd = lax.rem(place, 2) == 1
    wide = queries_ref.shape[1]
    choose_blocks(
        window,
        odd,
        (
            (back4_ref, back4_ref),
            (peer_back2_ref, peer_back4_ref),
            (back2_ref, back2_ref),
            (peer_ref, peer_back2_ref),
            (kept_ref, kept_ref),
        ),
    )
    own_rows = slice(LEFT * ROWS, (LEFT + 1) * ROWS)
    key_lane = lax.broadcasted_iota(jnp.int32, (1, ROWS), 1)
    allowed = jnp.concatenate(
        [key_lane < valid_count(valid_ref, place + block - LEFT) for block in range(LEFT + 1)], axis=1
    )
    key_valid = lax.broadcasted_iota(jnp.int32, (ROWS, ROWS), 0) < valid_count(valid_ref, place)
    stats = message_stats(message_ref[ROWS : ROWS + 16, :])
    for pair in range(wide // PAIR):
        lanes = slice(pair * PAIR, (pair + 1) * PAIR)
        value_lanes = slice(wide + pair * PAIR, wide + (pair + 1) * PAIR)
        query_pair = queries_ref[:, lanes]
        grad_pair = message_ref[0:ROWS, lanes]
        total = None
        for half in range(2):
            key_half = masked_half(window[:, lanes], half)
            value_half = masked_half(window[:, value_lanes], half)
            head = 2 * pair + half
            scores = dot_nt(query_pair, key_half) * SCALE
            shares = jnp.exp(jnp.where(allowed, scores, NEGATIVE) - log_ref[:, head : head + 1])
            share_grad = dot_nt(grad_pair, value_half)
            score_grad = (shares * (share_grad - dot_ref[:, head : head + 1])).astype(BF16)
            product = dot_nn(score_grad, key_half)
            total = product if total is None else total + product
        query_grad[:, lanes] = (total * SCALE).astype(BF16)
        heads = (2 * pair, 2 * pair + 1)
        key_sum_ref[:, lanes], value_sum_ref[:, lanes] = key_terms(
            window[own_rows, lanes],
            window[own_rows, value_lanes],
            query_pair,
            grad_pair,
            [stats[head : head + 1] for head in heads],
            [stats[8 + head : 9 + head] for head in heads],
            key_valid,
        )
    out_ref[...] = dot_nt(query_grad[...], w_query_ref[...])


def key_kernel(
    valid_ref,
    kept_ref,
    query_next2_ref,
    query_next4_ref,
    query_peer_ref,
    query_peer_next2_ref,
    query_peer_next4_ref,
    next2_ref,
    next4_ref,
    peer_ref,
    peer_next2_ref,
    peer_next4_ref,
    w_key_ref,
    w_value_ref,
    gain_ref,
    own_ref,
    total_ref,
    partial_ref,
    key_sum_ref,
    value_sum_ref,
    result_ref,
    keep_ref,
    out_ref,
    edge_ref,
    held_ref,
    grads,
    queries,
    tails,
    stats,
    key_grad,
    value_grad,
):
    place = lax.axis_index("tm")
    odd = lax.rem(place, 2) == 1
    count = valid_count(valid_ref, place)
    wide = grads.shape[1]
    messages = (
        (peer_next2_ref, peer_ref),
        (next2_ref, next2_ref),
        (peer_next4_ref, peer_next2_ref),
        (next4_ref, next4_ref),
    )
    choose_blocks(grads, odd, messages)
    for block, (when_odd, when_even) in enumerate(messages):
        target = tails.at[block * 16 : block * 16 + 16]
        choose_rows(target, odd, when_odd, when_even, slice(ROWS, ROWS + 16))
    choose_blocks(
        queries,
        odd,
        (
            (query_peer_next2_ref, query_peer_ref),
            (query_next2_ref, query_next2_ref),
            (query_peer_next4_ref, query_peer_next2_ref),
            (query_next4_ref, query_next4_ref),
        ),
    )
    for block in range(LEFT):
        stats[:, block * ROWS : (block + 1) * ROWS] = message_stats(tails[block * 16 : block * 16 + 16, :])
    key_valid = lax.broadcasted_iota(jnp.int32, (ROWS, LEFT * ROWS), 0) < count
    for pair in range(wide // PAIR):
        lanes = slice(pair * PAIR, (pair + 1) * PAIR)
        heads = (2 * pair, 2 * pair + 1)
        key_sum, value_sum = key_terms(
            kept_ref[:, lanes],
            kept_ref[:, slice(wide + pair * PAIR, wide + (pair + 1) * PAIR)],
            queries[:, lanes],
            grads[:, lanes],
            [stats[head : head + 1, :] for head in heads],
            [stats[8 + head : 9 + head, :] for head in heads],
            key_valid,
        )
        key_grad[:, lanes] = (key_sum_ref[:, lanes] + key_sum).astype(BF16)
        value_grad[:, lanes] = (value_sum_ref[:, lanes] + value_sum).astype(BF16)
    normed_grad = partial_ref[...] + dot_nt(key_grad[...], w_key_ref[...])
    normed_grad = normed_grad + dot_nt(value_grad[...], w_value_ref[...])
    scaled = normed_grad * gain_ref[...]
    unit, inverse = unit_rows(own_ref[...].astype(F32))
    back = inverse * (
        scaled
        - jnp.mean(scaled, axis=-1, keepdims=True)
        - unit * jnp.mean(scaled * unit, axis=-1, keepdims=True)
    )
    grad = total_ref[...] + back
    out_ref[...] = grad.astype(BF16)
    edge_ref[...] = grad[0:EDGE].astype(BF16)
    mine = lax.axis_index("section") == keep_ref[0]
    held_ref[...] = jnp.where(mine, grad, result_ref[...].astype(F32)).astype(BF16)


def call(kernel, name, operands, outs, scratch, copies=0, limit=VMEM_LIMIT):
    kinds = {
        "s": pl.BlockSpec(memory_space=pltpu.SMEM),
        "v": pl.BlockSpec(memory_space=pltpu.VMEM),
        "h": pl.BlockSpec(memory_space=pltpu.HBM),
    }
    return pl.pallas_call(
        kernel,
        name=name,
        in_specs=[kinds[place] for _, place in operands],
        out_specs=[kinds["v"]] * len(outs),
        out_shape=[jax.ShapeDtypeStruct(shape, dtype) for shape, dtype in outs],
        scratch_shapes=[pltpu.VMEM(shape, dtype) for shape, dtype in scratch]
        + [pltpu.SemaphoreType.DMA((copies,))] * (copies > 0),
        compiler_params=pltpu.CompilerParams(vmem_limit_bytes=limit),
        cost_estimate=pl.CostEstimate(flops=1 << 30, bytes_accessed=4 << 20, transcendentals=0),
    )(*[array for array, _ in operands])


def placed(kinds, *arrays):
    return list(zip(arrays, kinds, strict=True))


def after(value, *others):
    return lax.optimization_barrier((value, *others))[0]


def shards(
    layer_inputs, top_grad, w_query, w_key, w_value, w_out, conv_kernel, norm_gain, group_valid
):
    own = layer_inputs[0]
    width = own.shape[1]
    wide = w_query.shape[2]
    query_weight = w_query[0]
    key_weight = w_key[0]
    value_weight = w_value[0]
    out_weight = w_out[0]
    kernel = conv_kernel[0]
    sections = lax.axis_size("section")
    count = lax.axis_size("tm")

    def moved(value, pairs):
        return lax.ppermute(value, ("tm", "section"), pairs)

    def at(layer, frame):
        return frame * sections + layer

    def across(steps, chosen):
        return [
            (at(section, source), at(section, source + steps))
            for section in chosen
            for source in range(max(0, -steps), min(count, count - steps))
        ]

    every = range(sections)
    half_edge = EDGE // 2
    swap = [(at(section, source), at(section, source ^ 1)) for section in every for source in range(count)]
    weight = ((width, wide), BF16)
    queries, kept, ahead, behind = call(
        project_kernel,
        "project",
        placed("hhvhhh", own, top_grad, norm_gain, query_weight, key_weight, value_weight),
        [
            ((ROWS, wide), BF16),
            ((ROWS, 2 * wide), BF16),
            ((ROWS + EDGE + half_edge, width), BF16),
            ((ROWS + 2 * EDGE + half_edge, width), BF16),
        ],
        [((ROWS, width), BF16), ((ROWS, width), BF16), ((EDGE, width), BF16), weight, weight, weight],
        5,
        VMEM_WHOLE,
    )
    back2 = moved(ahead, across(2, every))
    back4 = moved(kept, across(4, every))
    after1 = moved(behind, across(-1, every))
    query_next2 = moved(queries, across(-2, every))
    query_next4 = moved(queries, across(-4, every))
    peer = moved(ahead, swap)
    query_peer = moved(queries, swap)
    peer_back2 = moved(back2, swap)
    peer_back4 = moved(back4, swap)
    query_peer_next2 = moved(query_next2, swap)
    query_peer_next4 = moved(query_next4, swap)
    far_pairs = [
        (at(section, source), at(section, source + 5))
        for section in every
        for source in range(1, count - 5, 2)
    ]
    back5 = moved(after(kept, back2), far_pairs)
    query_next2, query_next4, query_peer, query_peer_next2, query_peer_next4, after1 = (
        lax.optimization_barrier(
            (query_next2, query_next4, query_peer, query_peer_next2, query_peer_next4, after1)
        )
    )

    span = (LEFT + 1) * ROWS
    attended, logs = call(
        attend_kernel,
        "attend",
        placed("svvvvvvvv", group_valid, queries, kept, back2, back4, peer, peer_back2, peer_back4, after1),
        [((ROWS + EDGE, wide), BF16), ((ROWS, PAIR), F32)],
        [(((LEFT + 2) * ROWS, 2 * wide), BF16), ((ROWS + EDGE, wide), BF16)],
    )
    back5 = after(back5, attended)
    step_outs = [((ROWS, width), F32), ((ROWS + 16, wide), BF16), ((ROWS, PAIR), F32)]
    slope, total, message, dots = call(
        mix_kernel,
        "mix",
        placed(
            "svvvvvvvvvvvvv",
            group_valid,
            own,
            top_grad,
            attended,
            logs,
            back2,
            back4,
            back5,
            peer,
            peer_back2,
            peer_back4,
            after1,
            out_weight,
            kernel,
        ),
        [((ROWS + EDGE, width), F32)] + step_outs,
        [
            ((span, 2 * wide), BF16),
            ((EDGE, wide), BF16),
            ((ROWS + 2 * EDGE, wide), BF16),
            ((ROWS + 2 * EDGE, width), F32),
            ((ROWS, width), BF16),
            ((EDGE + half_edge, width), BF16),
        ],
    )

    result = own
    upstream = None
    upstream_next = None
    for step in range(sections):
        layer = sections - 1 - step
        if step > 0:
            total, message, dots = call(
                mixer_kernel,
                "mixer",
                placed(
                    "svvvvvvv", group_valid, upstream, upstream_next, slope, kernel, out_weight, attended, logs
                ),
                step_outs,
                [((ROWS, width), BF16)],
                    )
        here = [layer]
        grad2 = moved(message, across(-2, here))
        grad4 = moved(message, across(-4, here))
        peer_grad = moved(message, swap)
        partial, key_sum, value_sum = call(
            query_kernel,
            "own_queries",
            placed(
                "svvvvvvvvvvv",
                group_valid,
                queries,
                kept,
                back2,
                back4,
                peer,
                peer_back2,
                peer_back4,
                message,
                logs,
                dots,
                query_weight,
            ),
            [((ROWS, width), F32), ((ROWS, wide), F32), ((ROWS, wide), F32)],
            [
                ((span, 2 * wide), BF16),
                ((ROWS, wide), BF16),
            ],
            )
        grad2, grad4, partial = lax.optimization_barrier((grad2, grad4, partial))
        peer_grad2 = moved(grad2, swap)
        peer_grad4 = moved(grad4, swap)
        input_grad, edge, result = call(
            key_kernel,
            "own_keys",
            placed(
                "svvvvvvvvvvvvvvvvvvvvs",
                group_valid,
                kept,
                query_next2,
                query_next4,
                query_peer,
                query_peer_next2,
                query_peer_next4,
                grad2,
                grad4,
                peer_grad,
                peer_grad2,
                peer_grad4,
                key_weight,
                value_weight,
                norm_gain,
                own,
                total,
                partial,
                key_sum,
                value_sum,
                result,
                jnp.full((1,), layer, jnp.int32),
            ),
            [((ROWS, width), BF16), ((EDGE, width), BF16), ((ROWS, width), BF16)],
            [
                ((LEFT * ROWS, wide), BF16),
                ((LEFT * ROWS, wide), BF16),
                ((LEFT * 16, wide), BF16),
                ((16, LEFT * ROWS), F32),
                ((ROWS, wide), BF16),
                ((ROWS, wide), BF16),
            ],
            )
        if layer > 0:
            upstream = moved(
                input_grad,
                [(at(layer, source), at(layer - 1, source)) for source in range(count)]
                + [(at(layer - 1, source), at(layer, source)) for source in range(count)],
            )
            upstream_next = moved(
                edge, [(at(layer, source), at(layer - 1, source - 1)) for source in range(1, count)]
            )
    return result[None]


def solution(mesh):
    placed = (
        P("section", "tm", None),
        P("tm", None),
        P("section", None, None),
        P("section", None, None),
        P("section", None, None),
        P("section", None, None),
        P("section", None, None),
        P("section", None),
        P(),
    )
    return jax.shard_map(
        shards, mesh=mesh, in_specs=placed, out_specs=P("section", "tm", None), check_vma=False
    )
```

```python
import functools

import jax
import jax.numpy as jnp
from jax import lax
from jax.experimental import pallas as pl
from jax.experimental.pallas import tpu as pltpu
from jax.sharding import PartitionSpec as P

HEAD_DIM = 64
PAIR = 128
ROWS = 128
LEFT = 4
EDGE = 32
SCALE = HEAD_DIM ** (-0.5)
NEGATIVE = -1e30
EPSILON = 1e-05
F32 = jnp.float32
BF16 = jnp.bfloat16
VMEM_LIMIT = 20 << 20
VMEM_WHOLE = 60 << 20


def dot_nn(a, b):
    return lax.dot_general(a, b, (((1,), (0,)), ((), ())), preferred_element_type=F32)


def dot_nt(a, b):
    return lax.dot_general(a, b, (((1,), (1,)), ((), ())), preferred_element_type=F32)


def valid_count(valid_ref, block):
    groups = valid_ref.shape[0]
    inside = (block >= 0) & (block < groups)
    return jnp.where(inside, valid_ref[jnp.clip(block, 0, groups - 1)], 0)


def even_half(rows):
    return lax.broadcasted_iota(jnp.int32, (rows, PAIR), 1) < HEAD_DIM


def unit_rows(values):
    center = values - jnp.mean(values, axis=-1, keepdims=True)
    spread = jnp.mean(center * center, axis=-1, keepdims=True)
    inverse = lax.rsqrt(spread + EPSILON)
    return center * inverse, inverse


def three_parts(value):
    first = value.astype(BF16)
    rest = value - first.astype(F32)
    second = rest.astype(BF16)
    third = (rest - second.astype(F32)).astype(BF16)
    return first, second, third


def shift_rows(value, amount):
    if amount == 0:
        return value
    return pltpu.roll(value, value.shape[0] - amount, 0)


def tap_sum(padded, kernel_ref, lanes, first, step, rows):
    taps = kernel_ref.shape[0]
    total = jnp.zeros((rows, padded.shape[1]), F32)
    for phase in range(8):
        moved = None
        for tap in range(taps):
            offset = first + step * tap
            if offset % 8 != phase:
                continue
            if moved is None:
                moved = shift_rows(padded, phase)
            base = offset - phase
            total = total + kernel_ref[tap : tap + 1, lanes] * moved[base : base + rows]
    return total


def project_kernel(
    own_ref,
    top_ref,
    gain_ref,
    w_query_ref,
    w_key_ref,
    w_value_ref,
    queries_ref,
    kept_ref,
    ahead_ref,
    behind_ref,
    normed,
    own,
    top,
    w_query,
    w_key,
    w_value,
    semaphores,
):
    chunk = 16
    loads = [
        pltpu.make_async_copy(source, target, semaphores.at[index])
        for index, (source, target) in enumerate(
            (
                (own_ref, own),
                (w_key_ref, w_key),
                (w_value_ref, w_value),
                (w_query_ref, w_query),
                (top_ref.at[0:EDGE], top),
            )
        )
    ]
    for load in loads:
        load.start()
    loads[0].wait()

    def norm_step(step, carry):
        rows = pl.ds(pl.multiple_of(step * chunk, chunk), chunk)
        unit, _ = unit_rows(own[rows, :].astype(F32))
        normed[rows, :] = (unit * gain_ref[...]).astype(BF16)
        return carry

    lax.fori_loop(0, ROWS // chunk, norm_step, 0, unroll=2)
    wide = w_key_ref.shape[1]
    half = EDGE // 2
    loads[1].wait()
    keys = dot_nn(normed[...], w_key[...]).astype(BF16)
    loads[2].wait()
    values = dot_nn(normed[...], w_value[...]).astype(BF16)
    for ref in (kept_ref, ahead_ref, behind_ref):
        ref[0:ROWS, 0:wide] = keys
        ref[0:ROWS, wide : 2 * wide] = values
    loads[3].wait()
    loads[4].wait()
    queries = dot_nn(normed[...], w_query[...]).astype(BF16)
    queries_ref[...] = queries
    ahead_ref[ROWS : ROWS + EDGE, :] = own[ROWS - EDGE : ROWS, :]
    ahead_ref[ROWS + EDGE : ROWS + EDGE + half, 0:wide] = queries[ROWS - EDGE : ROWS - half]
    ahead_ref[ROWS + EDGE : ROWS + EDGE + half, wide : 2 * wide] = queries[ROWS - half : ROWS]
    behind_ref[ROWS : ROWS + EDGE, :] = own[0:EDGE, :]
    behind_ref[ROWS + EDGE : ROWS + EDGE + half, 0:wide] = queries[0:half]
    behind_ref[ROWS + EDGE : ROWS + EDGE + half, wide : 2 * wide] = queries[half:EDGE]
    behind_ref[ROWS + EDGE + half : ROWS + 2 * EDGE + half, :] = top[...]


def choose_rows(target, odd, when_odd, when_even, rows):
    if when_even is when_odd:
        target[...] = when_odd[rows, :]
        return

    @pl.when(odd)
    def _():
        target[...] = when_odd[rows, :]

    @pl.when(jnp.logical_not(odd))
    def _():
        target[...] = when_even[rows, :]


def choose_blocks(target, odd, sources):
    for index, (when_odd, when_even) in enumerate(sources):
        choose_rows(target.at[index * ROWS : (index + 1) * ROWS], odd, when_odd, when_even, slice(0, ROWS))


def masked_half(value, half):
    keep = even_half(value.shape[0])
    if half:
        keep = jnp.logical_not(keep)
    return jnp.where(keep, value, jnp.zeros_like(value))


def pair_shares(scores, allowed):
    part = jnp.where(allowed, scores, NEGATIVE)
    highest = jnp.max(part, axis=-1, keepdims=True)
    exped = jnp.exp(part - highest)
    summed = jnp.sum(exped, axis=-1, keepdims=True)
    return (exped * (1.0 / summed)).astype(BF16), highest, summed


def attend_kernel(
    valid_ref,
    queries_ref,
    kept_ref,
    back2_ref,
    back4_ref,
    peer_ref,
    peer_back2_ref,
    peer_back4_ref,
    after_ref,
    attended_ref,
    log_ref,
    window,
    query_all,
):
    place = lax.axis_index("tm")
    odd = lax.rem(place, 2) == 1
    wide = queries_ref.shape[1]
    half_edge = EDGE // 2
    packed = after_ref[ROWS + EDGE : ROWS + EDGE + half_edge, :]
    query_all[0:ROWS, :] = queries_ref[...]
    choose_blocks(
        window,
        odd,
        (
            (back4_ref, back4_ref),
            (peer_back2_ref, peer_back4_ref),
            (back2_ref, back2_ref),
            (peer_ref, peer_back2_ref),
            (kept_ref, kept_ref),
            (after_ref, after_ref),
        ),
    )
    query_all[ROWS : ROWS + half_edge, :] = packed[:, 0:wide]
    query_all[ROWS + half_edge : ROWS + EDGE, :] = packed[:, wide : 2 * wide]
    key_lane = lax.broadcasted_iota(jnp.int32, (1, ROWS), 1)
    allowed = jnp.concatenate(
        [key_lane < valid_count(valid_ref, place + block - LEFT) for block in range(LEFT + 2)], axis=1
    )
    span = (LEFT + 1) * ROWS
    log_lane = lax.broadcasted_iota(jnp.int32, (ROWS, PAIR), 1)
    logs = jnp.zeros((ROWS, PAIR), F32)
    for pair in range(wide // PAIR):
        lanes = slice(pair * PAIR, (pair + 1) * PAIR)
        value_lanes = slice(wide + pair * PAIR, wide + (pair + 1) * PAIR)
        totals = [None, None]
        for half in range(2):
            scores = dot_nt(query_all[:, lanes], masked_half(window[:, lanes], half)) * SCALE
            value_half = masked_half(window[:, value_lanes], half)
            for group, (low, high, first) in enumerate(((0, ROWS, 0), (ROWS, ROWS + EDGE, ROWS))):
                shares_low, highest, summed = pair_shares(
                    scores[low:high, first : first + span], allowed[:, first : first + span]
                )
                product = dot_nn(shares_low, value_half[first : first + span])
                totals[group] = product if totals[group] is None else totals[group] + product
                if group == 0:
                    logs = jnp.where(log_lane == 2 * pair + half, highest + jnp.log(summed), logs)
        attended_ref[0:ROWS, lanes] = totals[0].astype(BF16)
        attended_ref[ROWS : ROWS + EDGE, lanes] = totals[1].astype(BF16)
    log_ref[...] = logs


def mixer_body(
    count, upstream_ref, next_rows, slope_ref, kernel_ref, w_out_ref, attended, log_ref, total_ref, message_ref, dot_ref, total_low
):
    row_ids = lax.broadcasted_iota(jnp.int32, (ROWS, PAIR), 0)
    taps = kernel_ref.shape[0]

    def conv_step(step, carry):
        lanes = pl.ds(pl.multiple_of(step * PAIR, PAIR), PAIR)
        upper = upstream_ref[:, lanes].astype(F32)
        stacked = jnp.concatenate([upper, next_rows(lanes)], axis=0)
        grads = (stacked * slope_ref[:, lanes]).astype(BF16).astype(F32)
        back = tap_sum(grads, kernel_ref, lanes, taps - 1, -1, ROWS)
        total = upper + jnp.where(row_ids < count, back, 0.0)
        total_ref[:, lanes] = total
        total_low[:, lanes] = total.astype(BF16)
        return carry

    lax.fori_loop(0, upstream_ref.shape[1] // PAIR, conv_step, 0, unroll=True)
    out_grad = dot_nt(total_low[...], w_out_ref[...]).astype(BF16)
    message_ref[0:ROWS, :] = out_grad
    product = out_grad.astype(F32) * attended[...].astype(F32)
    high = product.astype(BF16)
    low = (product - high.astype(F32)).astype(BF16)
    width = product.shape[1]
    head_of = lax.broadcasted_iota(jnp.int32, (PAIR, width), 1) // HEAD_DIM
    chosen = (head_of == lax.broadcasted_iota(jnp.int32, (PAIR, width), 0)).astype(F32).astype(BF16)
    dots = dot_nt(high, chosen) + dot_nt(low, chosen)
    dot_ref[...] = dots
    stacked = jnp.concatenate([log_ref[...].T[0:8], dots.T[0:8]], axis=0)
    message_ref[ROWS : ROWS + 16, :] = jnp.zeros((16, width), BF16)
    for index, part in enumerate(three_parts(stacked)):
        message_ref[ROWS : ROWS + 16, index * PAIR : (index + 1) * PAIR] = part


def mix_kernel(
    valid_ref,
    own_ref,
    top_ref,
    attended_ref,
    log_ref,
    back2_ref,
    back4_ref,
    back5_ref,
    peer_ref,
    peer_back2_ref,
    peer_back4_ref,
    after_ref,
    w_out_ref,
    kernel_ref,
    slope_ref,
    total_ref,
    message_ref,
    dot_ref,
    window,
    query_tail,
    attended_all,
    mixed,
    total_low,
    before_rows,
):
    place = lax.axis_index("tm")
    odd = lax.rem(place, 2) == 1
    wide = query_tail.shape[1]
    half_edge = EDGE // 2
    counts = [valid_count(valid_ref, place + block - LEFT - 1) for block in range(LEFT + 3)]
    choose_rows(before_rows, odd, peer_ref, peer_back2_ref, slice(ROWS, ROWS + EDGE + half_edge))
    choose_blocks(
        window,
        odd,
        (
            (peer_back4_ref, back5_ref),
            (back4_ref, back4_ref),
            (peer_back2_ref, peer_back4_ref),
            (back2_ref, back2_ref),
            (peer_ref, peer_back2_ref),
        ),
    )
    attended_all[EDGE:, :] = attended_ref[...]
    query_tail[0:half_edge, :] = before_rows[EDGE : EDGE + half_edge, 0:wide]
    query_tail[half_edge:EDGE, :] = before_rows[EDGE : EDGE + half_edge, wide : 2 * wide]
    key_lane = lax.broadcasted_iota(jnp.int32, (1, ROWS), 1)
    allowed = jnp.concatenate([key_lane < count for count in counts[: LEFT + 1]], axis=1)
    for pair in range(wide // PAIR):
        lanes = slice(pair * PAIR, (pair + 1) * PAIR)
        value_lanes = slice(wide + pair * PAIR, wide + (pair + 1) * PAIR)
        total = None
        for half in range(2):
            scores = dot_nt(query_tail[:, lanes], masked_half(window[:, lanes], half)) * SCALE
            shares_low, _, _ = pair_shares(scores, allowed)
            product = dot_nn(shares_low, masked_half(window[:, value_lanes], half))
            total = product if total is None else total + product
        attended_all[0:EDGE, lanes] = total.astype(BF16)
    projected = dot_nn(attended_all[...], w_out_ref[...])
    row_ids = lax.broadcasted_iota(jnp.int32, (ROWS, 1), 0)
    edge_ids = lax.broadcasted_iota(jnp.int32, (EDGE, 1), 0)
    before = projected[0:EDGE] + before_rows[0:EDGE, :].astype(F32)
    here = projected[EDGE : EDGE + ROWS] + own_ref[...].astype(F32)
    after = projected[EDGE + ROWS :] + after_ref[ROWS : ROWS + EDGE, :].astype(F32)
    before = jnp.where(edge_ids + (ROWS - EDGE) < counts[LEFT], before, 0.0)
    here = jnp.where(row_ids < counts[LEFT + 1], here, 0.0)
    after = jnp.where(edge_ids < counts[LEFT + 2], after, 0.0)
    mixed[0:EDGE, :] = before.astype(BF16).astype(F32)
    mixed[EDGE : EDGE + ROWS, :] = here.astype(BF16).astype(F32)
    mixed[EDGE + ROWS :, :] = after.astype(BF16).astype(F32)
    taps = kernel_ref.shape[0]

    def conv_step(step, carry):
        lanes = pl.ds(pl.multiple_of(step * PAIR, PAIR), PAIR)
        output = tap_sum(mixed[:, lanes], kernel_ref, lanes, EDGE - (taps - 1), 1, ROWS + EDGE)
        gate = 1.0 / (1.0 + jnp.exp(-output))
        slope_ref[:, lanes] = gate * (1.0 + output * (1.0 - gate))
        return carry

    lax.fori_loop(0, own_ref.shape[1] // PAIR, conv_step, 0, unroll=True)
    first = ROWS + EDGE + half_edge
    mixer_body(
        counts[LEFT + 1],
        top_ref,
        lambda lanes: after_ref[first : first + EDGE, lanes].astype(F32),
        slope_ref,
        kernel_ref,
        w_out_ref,
        attended_all[EDGE : EDGE + ROWS, :],
        log_ref,
        total_ref,
        message_ref,
        dot_ref,
        total_low,
    )


def mixer_kernel(
    valid_ref,
    upstream_ref,
    next_ref,
    slope_ref,
    kernel_ref,
    w_out_ref,
    attended_ref,
    log_ref,
    total_ref,
    message_ref,
    dot_ref,
    total_low,
):
    mixer_body(
        valid_count(valid_ref, lax.axis_index("tm")),
        upstream_ref,
        lambda lanes: next_ref[:, lanes].astype(F32),
        slope_ref,
        kernel_ref,
        w_out_ref,
        attended_ref[0:ROWS, :],
        log_ref,
        total_ref,
        message_ref,
        dot_ref,
        total_low,
    )


def key_terms(key_pair, value_pair, query_pair, grad_pair, logs, dots, key_valid):
    share_halves = []
    score_halves = []
    query_halves = [masked_half(query_pair, half) for half in range(2)]
    grad_halves = [masked_half(grad_pair, half) for half in range(2)]
    for half in range(2):
        scores = dot_nt(key_pair, query_halves[half]) * SCALE
        shares = jnp.exp(jnp.where(key_valid, scores, NEGATIVE) - logs[half])
        share_grad = dot_nt(value_pair, grad_halves[half])
        score_halves.append((shares * (share_grad - dots[half])).astype(BF16))
        share_halves.append(shares.astype(BF16))
    key_sum = None
    value_sum = None
    for block in range(query_pair.shape[0] // ROWS):
        rows = slice(block * ROWS, (block + 1) * ROWS)
        key_term = dot_nn(
            jnp.concatenate([score[:, rows] for score in score_halves], axis=1),
            jnp.concatenate([query[rows] for query in query_halves], axis=0),
        )
        value_term = dot_nn(
            jnp.concatenate([share[:, rows] for share in share_halves], axis=1),
            jnp.concatenate([grad[rows] for grad in grad_halves], axis=0),
        )
        key_term = (key_term * SCALE).astype(BF16).astype(F32)
        value_term = value_term.astype(BF16).astype(F32)
        key_sum = key_term if key_sum is None else key_sum + key_term
        value_sum = value_term if value_sum is None else value_sum + value_term
    return key_sum, value_sum


def message_stats(tail):
    tail = tail.astype(F32)
    return tail[:, 0:PAIR] + tail[:, PAIR : 2 * PAIR] + tail[:, 2 * PAIR : 3 * PAIR]


def query_kernel(
    valid_ref,
    queries_ref,
    kept_ref,
    back2_ref,
    back4_ref,
    peer_ref,
    peer_back2_ref,
    peer_back4_ref,
    message_ref,
    log_ref,
    dot_ref,
    w_query_ref,
    out_ref,
    key_sum_ref,
    value_sum_ref,
    window,
    query_grad,
):
    place = lax.axis_index("tm")
    odd = lax.rem(place, 2) == 1
    wide = queries_ref.shape[1]
    choose_blocks(
        window,
        odd,
        (
            (back4_ref, back4_ref),
            (peer_back2_ref, peer_back4_ref),
            (back2_ref, back2_ref),
            (peer_ref, peer_back2_ref),
            (kept_ref, kept_ref),
        ),
    )
    own_rows = slice(LEFT * ROWS, (LEFT + 1) * ROWS)
    key_lane = lax.broadcasted_iota(jnp.int32, (1, ROWS), 1)
    allowed = jnp.concatenate(
        [key_lane < valid_count(valid_ref, place + block - LEFT) for block in range(LEFT + 1)], axis=1
    )
    key_valid = lax.broadcasted_iota(jnp.int32, (ROWS, ROWS), 0) < valid_count(valid_ref, place)
    stats = message_stats(message_ref[ROWS : ROWS + 16, :])
    for pair in range(wide // PAIR):
        lanes = slice(pair * PAIR, (pair + 1) * PAIR)
        value_lanes = slice(wide + pair * PAIR, wide + (pair + 1) * PAIR)
        query_pair = queries_ref[:, lanes]
        grad_pair = message_ref[0:ROWS, lanes]
        total = None
        for half in range(2):
            key_half = masked_half(window[:, lanes], half)
            value_half = masked_half(window[:, value_lanes], half)
            head = 2 * pair + half
            scores = dot_nt(query_pair, key_half) * SCALE
            shares = jnp.exp(jnp.where(allowed, scores, NEGATIVE) - log_ref[:, head : head + 1])
            share_grad = dot_nt(grad_pair, value_half)
            score_grad = (shares * (share_grad - dot_ref[:, head : head + 1])).astype(BF16)
            product = dot_nn(score_grad, key_half)
            total = product if total is None else total + product
        query_grad[:, lanes] = (total * SCALE).astype(BF16)
        heads = (2 * pair, 2 * pair + 1)
        key_sum_ref[:, lanes], value_sum_ref[:, lanes] = key_terms(
            window[own_rows, lanes],
            window[own_rows, value_lanes],
            query_pair,
            grad_pair,
            [stats[head : head + 1] for head in heads],
            [stats[8 + head : 9 + head] for head in heads],
            key_valid,
        )
    out_ref[...] = dot_nt(query_grad[...], w_query_ref[...])


def key_kernel(
    valid_ref,
    kept_ref,
    query_next2_ref,
    query_next4_ref,
    query_peer_ref,
    query_peer_next2_ref,
    query_peer_next4_ref,
    next2_ref,
    next4_ref,
    peer_ref,
    peer_next2_ref,
    peer_next4_ref,
    w_key_ref,
    w_value_ref,
    gain_ref,
    own_ref,
    total_ref,
    partial_ref,
    key_sum_ref,
    value_sum_ref,
    result_ref,
    keep_ref,
    out_ref,
    edge_ref,
    held_ref,
    grads,
    queries,
    tails,
    stats,
    key_grad,
    value_grad,
):
    place = lax.axis_index("tm")
    odd = lax.rem(place, 2) == 1
    count = valid_count(valid_ref, place)
    wide = grads.shape[1]
    messages = (
        (peer_next2_ref, peer_ref),
        (next2_ref, next2_ref),
        (peer_next4_ref, peer_next2_ref),
        (next4_ref, next4_ref),
    )
    choose_blocks(grads, odd, messages)
    for block, (when_odd, when_even) in enumerate(messages):
        target = tails.at[block * 16 : block * 16 + 16]
        choose_rows(target, odd, when_odd, when_even, slice(ROWS, ROWS + 16))
    choose_blocks(
        queries,
        odd,
        (
            (query_peer_next2_ref, query_peer_ref),
            (query_next2_ref, query_next2_ref),
            (query_peer_next4_ref, query_peer_next2_ref),
            (query_next4_ref, query_next4_ref),
        ),
    )
    for block in range(LEFT):
        stats[:, block * ROWS : (block + 1) * ROWS] = message_stats(tails[block * 16 : block * 16 + 16, :])
    key_valid = lax.broadcasted_iota(jnp.int32, (ROWS, LEFT * ROWS), 0) < count
    for pair in range(wide // PAIR):
        lanes = slice(pair * PAIR, (pair + 1) * PAIR)
        heads = (2 * pair, 2 * pair + 1)
        key_sum, value_sum = key_terms(
            kept_ref[:, lanes],
            kept_ref[:, slice(wide + pair * PAIR, wide + (pair + 1) * PAIR)],
            queries[:, lanes],
            grads[:, lanes],
            [stats[head : head + 1, :] for head in heads],
            [stats[8 + head : 9 + head, :] for head in heads],
            key_valid,
        )
        key_grad[:, lanes] = (key_sum_ref[:, lanes] + key_sum).astype(BF16)
        value_grad[:, lanes] = (value_sum_ref[:, lanes] + value_sum).astype(BF16)
    normed_grad = partial_ref[...] + dot_nt(key_grad[...], w_key_ref[...])
    normed_grad = normed_grad + dot_nt(value_grad[...], w_value_ref[...])
    scaled = normed_grad * gain_ref[...]
    unit, inverse = unit_rows(own_ref[...].astype(F32))
    back = inverse * (
        scaled
        - jnp.mean(scaled, axis=-1, keepdims=True)
        - unit * jnp.mean(scaled * unit, axis=-1, keepdims=True)
    )
    grad = total_ref[...] + back
    if out_ref is not None:
        out_ref[...] = grad.astype(BF16)
        edge_ref[...] = grad[0:EDGE].astype(BF16)
    mine = lax.axis_index("section") == keep_ref[0]
    held_ref[...] = jnp.where(mine, grad, result_ref[...].astype(F32)).astype(BF16)


def last_key_kernel(operands, *refs):
    key_kernel(*refs[:operands], None, None, *refs[operands:])


def call(kernel, name, operands, outs, scratch, copies=0, limit=VMEM_LIMIT):
    kinds = {
        "s": pl.BlockSpec(memory_space=pltpu.SMEM),
        "v": pl.BlockSpec(memory_space=pltpu.VMEM),
        "h": pl.BlockSpec(memory_space=pltpu.HBM),
    }
    return pl.pallas_call(
        kernel,
        name=name,
        in_specs=[kinds[place] for _, place in operands],
        out_specs=[kinds["v"]] * len(outs),
        out_shape=[jax.ShapeDtypeStruct(shape, dtype) for shape, dtype in outs],
        scratch_shapes=[pltpu.VMEM(shape, dtype) for shape, dtype in scratch]
        + [pltpu.SemaphoreType.DMA((copies,))] * (copies > 0),
        compiler_params=pltpu.CompilerParams(vmem_limit_bytes=limit),
        cost_estimate=pl.CostEstimate(flops=1 << 30, bytes_accessed=4 << 20, transcendentals=0),
    )(*[array for array, _ in operands])


def placed(kinds, *arrays):
    return list(zip(arrays, kinds, strict=True))


def after(value, *others):
    return lax.optimization_barrier((value, *others))[0]


def shards(
    layer_inputs, top_grad, w_query, w_key, w_value, w_out, conv_kernel, norm_gain, group_valid
):
    own = layer_inputs[0]
    width = own.shape[1]
    wide = w_query.shape[2]
    query_weight = w_query[0]
    key_weight = w_key[0]
    value_weight = w_value[0]
    out_weight = w_out[0]
    kernel = conv_kernel[0]
    sections = lax.axis_size("section")
    count = lax.axis_size("tm")

    def moved(value, pairs):
        return lax.ppermute(value, ("tm", "section"), pairs)

    def at(layer, frame):
        return frame * sections + layer

    def across(steps, chosen):
        return [
            (at(section, source), at(section, source + steps))
            for section in chosen
            for source in range(max(0, -steps), min(count, count - steps))
        ]

    every = range(sections)
    half_edge = EDGE // 2
    swap = [(at(section, source), at(section, source ^ 1)) for section in every for source in range(count)]
    weight = ((width, wide), BF16)
    queries, kept, ahead, behind = call(
        project_kernel,
        "project",
        placed("hhvhhh", own, top_grad, norm_gain, query_weight, key_weight, value_weight),
        [
            ((ROWS, wide), BF16),
            ((ROWS, 2 * wide), BF16),
            ((ROWS + EDGE + half_edge, width), BF16),
            ((ROWS + 2 * EDGE + half_edge, width), BF16),
        ],
        [((ROWS, width), BF16), ((ROWS, width), BF16), ((EDGE, width), BF16), weight, weight, weight],
        5,
        VMEM_WHOLE,
    )
    back2 = moved(ahead, across(2, every))
    back4 = moved(kept, across(4, every))
    after1 = moved(behind, across(-1, every))
    query_next2 = moved(queries, across(-2, every))
    query_next4 = moved(queries, across(-4, every))
    peer = moved(ahead, swap)
    query_peer = moved(queries, swap)
    peer_back2 = moved(back2, swap)
    peer_back4 = moved(back4, swap)
    query_peer_next2 = moved(query_next2, swap)
    query_peer_next4 = moved(query_next4, swap)
    far_pairs = [
        (at(section, source), at(section, source + 5))
        for section in every
        for source in range(1, count - 5, 2)
    ]
    back5 = moved(after(kept, back2), far_pairs)
    query_next2, query_next4, query_peer, query_peer_next2, query_peer_next4, after1 = (
        lax.optimization_barrier(
            (query_next2, query_next4, query_peer, query_peer_next2, query_peer_next4, after1)
        )
    )

    span = (LEFT + 1) * ROWS
    attended, logs = call(
        attend_kernel,
        "attend",
        placed("svvvvvvvv", group_valid, queries, kept, back2, back4, peer, peer_back2, peer_back4, after1),
        [((ROWS + EDGE, wide), BF16), ((ROWS, PAIR), F32)],
        [(((LEFT + 2) * ROWS, 2 * wide), BF16), ((ROWS + EDGE, wide), BF16)],
    )
    back5 = after(back5, attended)
    step_outs = [((ROWS, width), F32), ((ROWS + 16, wide), BF16), ((ROWS, PAIR), F32)]
    slope, total, message, dots = call(
        mix_kernel,
        "mix",
        placed(
            "svvvvvvvvvvvvv",
            group_valid,
            own,
            top_grad,
            attended,
            logs,
            back2,
            back4,
            back5,
            peer,
            peer_back2,
            peer_back4,
            after1,
            out_weight,
            kernel,
        ),
        [((ROWS + EDGE, width), F32)] + step_outs,
        [
            ((span, 2 * wide), BF16),
            ((EDGE, wide), BF16),
            ((ROWS + 2 * EDGE, wide), BF16),
            ((ROWS + 2 * EDGE, width), F32),
            ((ROWS, width), BF16),
            ((EDGE + half_edge, width), BF16),
        ],
    )

    result = own
    upstream = None
    upstream_next = None
    for step in range(sections):
        layer = sections - 1 - step
        if step > 0:
            total, message, dots = call(
                mixer_kernel,
                "mixer",
                placed(
                    "svvvvvvv", group_valid, upstream, upstream_next, slope, kernel, out_weight, attended, logs
                ),
                step_outs,
                [((ROWS, width), BF16)],
                    )
        here = [layer]
        grad2 = moved(message, across(-2, here))
        grad4 = moved(message, across(-4, here))
        peer_grad = moved(message, swap)
        partial, key_sum, value_sum = call(
            query_kernel,
            "own_queries",
            placed(
                "svvvvvvvvvvv",
                group_valid,
                queries,
                kept,
                back2,
                back4,
                peer,
                peer_back2,
                peer_back4,
                message,
                logs,
                dots,
                query_weight,
            ),
            [((ROWS, width), F32), ((ROWS, wide), F32), ((ROWS, wide), F32)],
            [
                ((span, 2 * wide), BF16),
                ((ROWS, wide), BF16),
            ],
            )
        grad2 = after(grad2, partial)
        grad4 = after(grad4, partial)
        peer_grad2 = moved(grad2, swap)
        peer_grad4 = moved(grad4, swap)
        key_operands = placed(
            "svvvvvvvvvvvvvvvvvvvvs",
            group_valid,
            kept,
            query_next2,
            query_next4,
            query_peer,
            query_peer_next2,
            query_peer_next4,
            grad2,
            grad4,
            peer_grad,
            peer_grad2,
            peer_grad4,
            key_weight,
            value_weight,
            norm_gain,
            own,
            total,
            partial,
            key_sum,
            value_sum,
            result,
            jnp.full((1,), layer, jnp.int32),
            )
        key_scratch = [
            ((LEFT * ROWS, wide), BF16),
            ((LEFT * ROWS, wide), BF16),
            ((LEFT * 16, wide), BF16),
            ((16, LEFT * ROWS), F32),
            ((ROWS, wide), BF16),
            ((ROWS, wide), BF16),
        ]
        whole = ((ROWS, width), BF16)
        if layer > 0:
            input_grad, edge, result = call(
                key_kernel, "own_keys", key_operands, [whole, ((EDGE, width), BF16), whole], key_scratch
            )
        else:
            (result,) = call(
                functools.partial(last_key_kernel, len(key_operands)),
                "last_keys",
                key_operands,
                [whole],
                key_scratch,
            )
        if layer > 0:
            upstream = moved(
                input_grad,
                [(at(layer, source), at(layer - 1, source)) for source in range(count)]
                + [(at(layer - 1, source), at(layer, source)) for source in range(count)],
            )
            upstream_next = moved(
                edge, [(at(layer, source), at(layer - 1, source - 1)) for source in range(1, count)]
            )
    return result[None]


def solution(mesh):
    placed = (
        P("section", "tm", None),
        P("tm", None),
        P("section", None, None),
        P("section", None, None),
        P("section", None, None),
        P("section", None, None),
        P("section", None, None),
        P("section", None),
        P(),
    )
    return jax.shard_map(
        shards, mesh=mesh, in_specs=placed, out_specs=P("section", "tm", None), check_vma=False
    )
```

```python
import functools

import jax
import jax.numpy as jnp
from jax import lax
from jax.experimental import pallas as pl
from jax.experimental.pallas import tpu as pltpu
from jax.sharding import PartitionSpec as P

HEAD_DIM = 64
PAIR = 128
ROWS = 128
LEFT = 4
EDGE = 32
SCALE = HEAD_DIM ** (-0.5)
NEGATIVE = -1e30
EPSILON = 1e-05
F32 = jnp.float32
BF16 = jnp.bfloat16
VMEM_LIMIT = 20 << 20
VMEM_WHOLE = 60 << 20


def dot_nn(a, b):
    return lax.dot_general(a, b, (((1,), (0,)), ((), ())), preferred_element_type=F32)


def dot_nt(a, b):
    return lax.dot_general(a, b, (((1,), (1,)), ((), ())), preferred_element_type=F32)


def valid_count(valid_ref, block):
    groups = valid_ref.shape[0]
    inside = (block >= 0) & (block < groups)
    return jnp.where(inside, valid_ref[jnp.clip(block, 0, groups - 1)], 0)


def even_half(rows):
    return lax.broadcasted_iota(jnp.int32, (rows, PAIR), 1) < HEAD_DIM


def unit_rows(values):
    center = values - jnp.mean(values, axis=-1, keepdims=True)
    spread = jnp.mean(center * center, axis=-1, keepdims=True)
    inverse = lax.rsqrt(spread + EPSILON)
    return center * inverse, inverse


def three_parts(value):
    first = value.astype(BF16)
    rest = value - first.astype(F32)
    second = rest.astype(BF16)
    third = (rest - second.astype(F32)).astype(BF16)
    return first, second, third


def shift_rows(value, amount):
    if amount == 0:
        return value
    return pltpu.roll(value, value.shape[0] - amount, 0)


def tap_sum(padded, kernel_ref, lanes, first, step, rows):
    taps = kernel_ref.shape[0]
    total = jnp.zeros((rows, padded.shape[1]), F32)
    for phase in range(8):
        moved = None
        for tap in range(taps):
            offset = first + step * tap
            if offset % 8 != phase:
                continue
            if moved is None:
                moved = shift_rows(padded, phase)
            base = offset - phase
            total = total + kernel_ref[tap : tap + 1, lanes] * moved[base : base + rows]
    return total


def project_kernel(
    own_ref,
    top_ref,
    gain_ref,
    w_query_ref,
    w_key_ref,
    w_value_ref,
    queries_ref,
    kept_ref,
    ahead_ref,
    behind_ref,
    normed,
    own,
    top,
    w_query,
    w_key,
    w_value,
    semaphores,
):
    chunk = 16
    loads = [
        pltpu.make_async_copy(source, target, semaphores.at[index])
        for index, (source, target) in enumerate(
            (
                (own_ref, own),
                (w_key_ref, w_key),
                (w_value_ref, w_value),
                (w_query_ref, w_query),
                (top_ref.at[0:EDGE], top),
            )
        )
    ]
    for load in loads:
        load.start()
    loads[0].wait()

    def norm_step(step, carry):
        rows = pl.ds(pl.multiple_of(step * chunk, chunk), chunk)
        unit, _ = unit_rows(own[rows, :].astype(F32))
        normed[rows, :] = (unit * gain_ref[...]).astype(BF16)
        return carry

    lax.fori_loop(0, ROWS // chunk, norm_step, 0, unroll=2)
    wide = w_key_ref.shape[1]
    half = EDGE // 2
    loads[1].wait()
    keys = dot_nn(normed[...], w_key[...]).astype(BF16)
    loads[2].wait()
    values = dot_nn(normed[...], w_value[...]).astype(BF16)
    for ref in (kept_ref, ahead_ref, behind_ref):
        ref[0:ROWS, 0:wide] = keys
        ref[0:ROWS, wide : 2 * wide] = values
    loads[3].wait()
    loads[4].wait()
    queries = dot_nn(normed[...], w_query[...]).astype(BF16)
    queries_ref[...] = queries
    ahead_ref[ROWS : ROWS + EDGE, :] = own[ROWS - EDGE : ROWS, :]
    ahead_ref[ROWS + EDGE : ROWS + EDGE + half, 0:wide] = queries[ROWS - EDGE : ROWS - half]
    ahead_ref[ROWS + EDGE : ROWS + EDGE + half, wide : 2 * wide] = queries[ROWS - half : ROWS]
    behind_ref[ROWS : ROWS + EDGE, :] = own[0:EDGE, :]
    behind_ref[ROWS + EDGE : ROWS + EDGE + half, 0:wide] = queries[0:half]
    behind_ref[ROWS + EDGE : ROWS + EDGE + half, wide : 2 * wide] = queries[half:EDGE]
    behind_ref[ROWS + EDGE + half : ROWS + 2 * EDGE + half, :] = top[...]


def choose_rows(target, odd, when_odd, when_even, rows):
    if when_even is when_odd:
        target[...] = when_odd[rows, :]
        return

    @pl.when(odd)
    def _():
        target[...] = when_odd[rows, :]

    @pl.when(jnp.logical_not(odd))
    def _():
        target[...] = when_even[rows, :]


def choose_blocks(target, odd, sources):
    for index, (when_odd, when_even) in enumerate(sources):
        choose_rows(target.at[index * ROWS : (index + 1) * ROWS], odd, when_odd, when_even, slice(0, ROWS))


def masked_half(value, half):
    keep = even_half(value.shape[0])
    if half:
        keep = jnp.logical_not(keep)
    return jnp.where(keep, value, jnp.zeros_like(value))


def pair_shares(scores, allowed):
    part = jnp.where(allowed, scores, NEGATIVE)
    highest = jnp.max(part, axis=-1, keepdims=True)
    exped = jnp.exp(part - highest)
    summed = jnp.sum(exped, axis=-1, keepdims=True)
    return (exped * (1.0 / summed)).astype(BF16), highest, summed


def attend_kernel(
    valid_ref,
    queries_ref,
    kept_ref,
    back2_ref,
    back4_ref,
    peer_ref,
    peer_back2_ref,
    peer_back4_ref,
    after_ref,
    attended_ref,
    log_ref,
    window,
    query_all,
):
    place = lax.axis_index("tm")
    odd = lax.rem(place, 2) == 1
    wide = queries_ref.shape[1]
    half_edge = EDGE // 2
    packed = after_ref[ROWS + EDGE : ROWS + EDGE + half_edge, :]
    query_all[0:ROWS, :] = queries_ref[...]
    choose_blocks(
        window,
        odd,
        (
            (back4_ref, back4_ref),
            (peer_back2_ref, peer_back4_ref),
            (back2_ref, back2_ref),
            (peer_ref, peer_back2_ref),
            (kept_ref, kept_ref),
            (after_ref, after_ref),
        ),
    )
    query_all[ROWS : ROWS + half_edge, :] = packed[:, 0:wide]
    query_all[ROWS + half_edge : ROWS + EDGE, :] = packed[:, wide : 2 * wide]
    key_lane = lax.broadcasted_iota(jnp.int32, (1, ROWS), 1)
    allowed = jnp.concatenate(
        [key_lane < valid_count(valid_ref, place + block - LEFT) for block in range(LEFT + 2)], axis=1
    )
    span = (LEFT + 1) * ROWS
    log_lane = lax.broadcasted_iota(jnp.int32, (ROWS, PAIR), 1)
    logs = jnp.zeros((ROWS, PAIR), F32)
    for pair in range(wide // PAIR):
        lanes = slice(pair * PAIR, (pair + 1) * PAIR)
        value_lanes = slice(wide + pair * PAIR, wide + (pair + 1) * PAIR)
        totals = [None, None]
        for half in range(2):
            scores = dot_nt(query_all[:, lanes], masked_half(window[:, lanes], half)) * SCALE
            value_half = masked_half(window[:, value_lanes], half)
            for group, (low, high, first) in enumerate(((0, ROWS, 0), (ROWS, ROWS + EDGE, ROWS))):
                shares_low, highest, summed = pair_shares(
                    scores[low:high, first : first + span], allowed[:, first : first + span]
                )
                product = dot_nn(shares_low, value_half[first : first + span])
                totals[group] = product if totals[group] is None else totals[group] + product
                if group == 0:
                    logs = jnp.where(log_lane == 2 * pair + half, highest + jnp.log(summed), logs)
        attended_ref[0:ROWS, lanes] = totals[0].astype(BF16)
        attended_ref[ROWS : ROWS + EDGE, lanes] = totals[1].astype(BF16)
    log_ref[...] = logs


def mixer_body(
    count, upstream_ref, next_rows, slope_ref, kernel_ref, w_out_ref, attended, log_ref, total_ref, message_ref, dot_ref, total_low
):
    row_ids = lax.broadcasted_iota(jnp.int32, (ROWS, PAIR), 0)
    taps = kernel_ref.shape[0]

    def conv_step(step, carry):
        lanes = pl.ds(pl.multiple_of(step * PAIR, PAIR), PAIR)
        upper = upstream_ref[:, lanes].astype(F32)
        stacked = jnp.concatenate([upper, next_rows(lanes)], axis=0)
        grads = (stacked * slope_ref[:, lanes]).astype(BF16).astype(F32)
        back = tap_sum(grads, kernel_ref, lanes, taps - 1, -1, ROWS)
        total = upper + jnp.where(row_ids < count, back, 0.0)
        total_ref[:, lanes] = total
        total_low[:, lanes] = total.astype(BF16)
        return carry

    lax.fori_loop(0, upstream_ref.shape[1] // PAIR, conv_step, 0, unroll=True)
    out_grad = dot_nt(total_low[...], w_out_ref[...]).astype(BF16)
    message_ref[0:ROWS, :] = out_grad
    product = out_grad.astype(F32) * attended[...].astype(F32)
    high = product.astype(BF16)
    low = (product - high.astype(F32)).astype(BF16)
    width = product.shape[1]
    head_of = lax.broadcasted_iota(jnp.int32, (PAIR, width), 1) // HEAD_DIM
    chosen = (head_of == lax.broadcasted_iota(jnp.int32, (PAIR, width), 0)).astype(F32).astype(BF16)
    dots = dot_nt(high, chosen) + dot_nt(low, chosen)
    dot_ref[...] = dots
    stacked = jnp.concatenate([log_ref[...].T[0:8], dots.T[0:8]], axis=0)
    message_ref[ROWS : ROWS + 16, :] = jnp.zeros((16, width), BF16)
    for index, part in enumerate(three_parts(stacked)):
        message_ref[ROWS : ROWS + 16, index * PAIR : (index + 1) * PAIR] = part


def mix_kernel(
    valid_ref,
    own_ref,
    top_ref,
    attended_ref,
    log_ref,
    back2_ref,
    back4_ref,
    back5_ref,
    peer_ref,
    peer_back2_ref,
    peer_back4_ref,
    after_ref,
    w_out_ref,
    kernel_ref,
    slope_ref,
    total_ref,
    message_ref,
    dot_ref,
    window,
    query_tail,
    attended_all,
    mixed,
    total_low,
    before_rows,
):
    place = lax.axis_index("tm")
    odd = lax.rem(place, 2) == 1
    wide = query_tail.shape[1]
    half_edge = EDGE // 2
    counts = [valid_count(valid_ref, place + block - LEFT - 1) for block in range(LEFT + 3)]
    choose_rows(before_rows, odd, peer_ref, peer_back2_ref, slice(ROWS, ROWS + EDGE + half_edge))
    choose_blocks(
        window,
        odd,
        (
            (peer_back4_ref, back5_ref),
            (back4_ref, back4_ref),
            (peer_back2_ref, peer_back4_ref),
            (back2_ref, back2_ref),
            (peer_ref, peer_back2_ref),
        ),
    )
    attended_all[EDGE:, :] = attended_ref[...]
    query_tail[0:half_edge, :] = before_rows[EDGE : EDGE + half_edge, 0:wide]
    query_tail[half_edge:EDGE, :] = before_rows[EDGE : EDGE + half_edge, wide : 2 * wide]
    key_lane = lax.broadcasted_iota(jnp.int32, (1, ROWS), 1)
    allowed = jnp.concatenate([key_lane < count for count in counts[: LEFT + 1]], axis=1)
    for pair in range(wide // PAIR):
        lanes = slice(pair * PAIR, (pair + 1) * PAIR)
        value_lanes = slice(wide + pair * PAIR, wide + (pair + 1) * PAIR)
        total = None
        for half in range(2):
            scores = dot_nt(query_tail[:, lanes], masked_half(window[:, lanes], half)) * SCALE
            shares_low, _, _ = pair_shares(scores, allowed)
            product = dot_nn(shares_low, masked_half(window[:, value_lanes], half))
            total = product if total is None else total + product
        attended_all[0:EDGE, lanes] = total.astype(BF16)
    projected = dot_nn(attended_all[...], w_out_ref[...])
    row_ids = lax.broadcasted_iota(jnp.int32, (ROWS, 1), 0)
    edge_ids = lax.broadcasted_iota(jnp.int32, (EDGE, 1), 0)
    before = projected[0:EDGE] + before_rows[0:EDGE, :].astype(F32)
    here = projected[EDGE : EDGE + ROWS] + own_ref[...].astype(F32)
    after = projected[EDGE + ROWS :] + after_ref[ROWS : ROWS + EDGE, :].astype(F32)
    before = jnp.where(edge_ids + (ROWS - EDGE) < counts[LEFT], before, 0.0)
    here = jnp.where(row_ids < counts[LEFT + 1], here, 0.0)
    after = jnp.where(edge_ids < counts[LEFT + 2], after, 0.0)
    mixed[0:EDGE, :] = before.astype(BF16).astype(F32)
    mixed[EDGE : EDGE + ROWS, :] = here.astype(BF16).astype(F32)
    mixed[EDGE + ROWS :, :] = after.astype(BF16).astype(F32)
    taps = kernel_ref.shape[0]

    def conv_step(step, carry):
        lanes = pl.ds(pl.multiple_of(step * PAIR, PAIR), PAIR)
        output = tap_sum(mixed[:, lanes], kernel_ref, lanes, EDGE - (taps - 1), 1, ROWS + EDGE)
        gate = 1.0 / (1.0 + jnp.exp(-output))
        slope_ref[:, lanes] = gate * (1.0 + output * (1.0 - gate))
        return carry

    lax.fori_loop(0, own_ref.shape[1] // PAIR, conv_step, 0, unroll=True)
    first = ROWS + EDGE + half_edge
    mixer_body(
        counts[LEFT + 1],
        top_ref,
        lambda lanes: after_ref[first : first + EDGE, lanes].astype(F32),
        slope_ref,
        kernel_ref,
        w_out_ref,
        attended_all[EDGE : EDGE + ROWS, :],
        log_ref,
        total_ref,
        message_ref,
        dot_ref,
        total_low,
    )


def mixer_kernel(
    valid_ref,
    upstream_ref,
    next_ref,
    slope_ref,
    kernel_ref,
    w_out_ref,
    attended_ref,
    log_ref,
    total_ref,
    message_ref,
    dot_ref,
    total_low,
):
    mixer_body(
        valid_count(valid_ref, lax.axis_index("tm")),
        upstream_ref,
        lambda lanes: next_ref[:, lanes].astype(F32),
        slope_ref,
        kernel_ref,
        w_out_ref,
        attended_ref[0:ROWS, :],
        log_ref,
        total_ref,
        message_ref,
        dot_ref,
        total_low,
    )


def key_terms(key_pair, value_pair, query_pair, grad_pair, logs, dots, key_valid):
    share_halves = []
    score_halves = []
    query_halves = [masked_half(query_pair, half) for half in range(2)]
    grad_halves = [masked_half(grad_pair, half) for half in range(2)]
    for half in range(2):
        scores = dot_nt(key_pair, query_halves[half]) * SCALE
        shares = jnp.exp(jnp.where(key_valid, scores, NEGATIVE) - logs[half])
        share_grad = dot_nt(value_pair, grad_halves[half])
        score_halves.append((shares * (share_grad - dots[half])).astype(BF16))
        share_halves.append(shares.astype(BF16))
    key_sum = None
    value_sum = None
    for block in range(query_pair.shape[0] // ROWS):
        rows = slice(block * ROWS, (block + 1) * ROWS)
        key_term = dot_nn(
            jnp.concatenate([score[:, rows] for score in score_halves], axis=1),
            jnp.concatenate([query[rows] for query in query_halves], axis=0),
        )
        value_term = dot_nn(
            jnp.concatenate([share[:, rows] for share in share_halves], axis=1),
            jnp.concatenate([grad[rows] for grad in grad_halves], axis=0),
        )
        key_term = (key_term * SCALE).astype(BF16).astype(F32)
        value_term = value_term.astype(BF16).astype(F32)
        key_sum = key_term if key_sum is None else key_sum + key_term
        value_sum = value_term if value_sum is None else value_sum + value_term
    return key_sum, value_sum


def message_stats(tail):
    tail = tail.astype(F32)
    return tail[:, 0:PAIR] + tail[:, PAIR : 2 * PAIR] + tail[:, 2 * PAIR : 3 * PAIR]


def query_kernel(
    valid_ref,
    queries_ref,
    kept_ref,
    back2_ref,
    back4_ref,
    peer_ref,
    peer_back2_ref,
    peer_back4_ref,
    message_ref,
    log_ref,
    dot_ref,
    w_query_ref,
    out_ref,
    key_sum_ref,
    value_sum_ref,
    window,
    query_grad,
):
    place = lax.axis_index("tm")
    odd = lax.rem(place, 2) == 1
    wide = queries_ref.shape[1]
    choose_blocks(
        window,
        odd,
        (
            (back4_ref, back4_ref),
            (peer_back2_ref, peer_back4_ref),
            (back2_ref, back2_ref),
            (peer_ref, peer_back2_ref),
            (kept_ref, kept_ref),
        ),
    )
    own_rows = slice(LEFT * ROWS, (LEFT + 1) * ROWS)
    key_lane = lax.broadcasted_iota(jnp.int32, (1, ROWS), 1)
    allowed = jnp.concatenate(
        [key_lane < valid_count(valid_ref, place + block - LEFT) for block in range(LEFT + 1)], axis=1
    )
    key_valid = lax.broadcasted_iota(jnp.int32, (ROWS, ROWS), 0) < valid_count(valid_ref, place)
    stats = message_stats(message_ref[ROWS : ROWS + 16, :])
    for pair in range(wide // PAIR):
        lanes = slice(pair * PAIR, (pair + 1) * PAIR)
        value_lanes = slice(wide + pair * PAIR, wide + (pair + 1) * PAIR)
        query_pair = queries_ref[:, lanes]
        grad_pair = message_ref[0:ROWS, lanes]
        total = None
        for half in range(2):
            key_half = masked_half(window[:, lanes], half)
            value_half = masked_half(window[:, value_lanes], half)
            head = 2 * pair + half
            scores = dot_nt(query_pair, key_half) * SCALE
            shares = jnp.exp(jnp.where(allowed, scores, NEGATIVE) - log_ref[:, head : head + 1])
            share_grad = dot_nt(grad_pair, value_half)
            score_grad = (shares * (share_grad - dot_ref[:, head : head + 1])).astype(BF16)
            product = dot_nn(score_grad, key_half)
            total = product if total is None else total + product
        query_grad[:, lanes] = (total * SCALE).astype(BF16)
        heads = (2 * pair, 2 * pair + 1)
        key_sum_ref[:, lanes], value_sum_ref[:, lanes] = key_terms(
            window[own_rows, lanes],
            window[own_rows, value_lanes],
            query_pair,
            grad_pair,
            [stats[head : head + 1] for head in heads],
            [stats[8 + head : 9 + head] for head in heads],
            key_valid,
        )
    out_ref[...] = dot_nt(query_grad[...], w_query_ref[...])


def key_kernel(
    valid_ref,
    kept_ref,
    query_peer_ref,
    query_far_ref,
    query_peer_far_ref,
    next2_ref,
    next4_ref,
    peer_ref,
    peer_next2_ref,
    peer_next4_ref,
    w_key_ref,
    w_value_ref,
    gain_ref,
    own_ref,
    total_ref,
    partial_ref,
    key_sum_ref,
    value_sum_ref,
    result_ref,
    keep_ref,
    out_ref,
    edge_ref,
    held_ref,
    grads,
    queries,
    tails,
    stats,
    key_grad,
    value_grad,
):
    place = lax.axis_index("tm")
    odd = lax.rem(place, 2) == 1
    count = valid_count(valid_ref, place)
    wide = grads.shape[1]
    messages = (
        (peer_next2_ref, peer_ref),
        (next2_ref, next2_ref),
        (peer_next4_ref, peer_next2_ref),
        (next4_ref, next4_ref),
    )
    choose_blocks(grads, odd, messages)
    for block, (when_odd, when_even) in enumerate(messages):
        target = tails.at[block * 16 : block * 16 + 16]
        choose_rows(target, odd, when_odd, when_even, slice(ROWS, ROWS + 16))
    choose_blocks(
        queries,
        odd,
        (
            (query_peer_far_ref.at[0:ROWS], query_peer_ref),
            (query_peer_far_ref.at[ROWS : 2 * ROWS], query_far_ref.at[0:ROWS]),
            (query_far_ref.at[ROWS : 2 * ROWS], query_far_ref.at[ROWS : 2 * ROWS]),
            (query_far_ref.at[0:ROWS], query_peer_far_ref.at[ROWS : 2 * ROWS]),
        ),
    )
    for block in range(LEFT):
        stats[:, block * ROWS : (block + 1) * ROWS] = message_stats(tails[block * 16 : block * 16 + 16, :])
    key_valid = lax.broadcasted_iota(jnp.int32, (ROWS, LEFT * ROWS), 0) < count
    for pair in range(wide // PAIR):
        lanes = slice(pair * PAIR, (pair + 1) * PAIR)
        heads = (2 * pair, 2 * pair + 1)
        key_sum, value_sum = key_terms(
            kept_ref[:, lanes],
            kept_ref[:, slice(wide + pair * PAIR, wide + (pair + 1) * PAIR)],
            queries[:, lanes],
            grads[:, lanes],
            [stats[head : head + 1, :] for head in heads],
            [stats[8 + head : 9 + head, :] for head in heads],
            key_valid,
        )
        key_grad[:, lanes] = (key_sum_ref[:, lanes] + key_sum).astype(BF16)
        value_grad[:, lanes] = (value_sum_ref[:, lanes] + value_sum).astype(BF16)
    normed_grad = partial_ref[...] + dot_nt(key_grad[...], w_key_ref[...])
    normed_grad = normed_grad + dot_nt(value_grad[...], w_value_ref[...])
    scaled = normed_grad * gain_ref[...]
    unit, inverse = unit_rows(own_ref[...].astype(F32))
    back = inverse * (
        scaled
        - jnp.mean(scaled, axis=-1, keepdims=True)
        - unit * jnp.mean(scaled * unit, axis=-1, keepdims=True)
    )
    grad = total_ref[...] + back
    if out_ref is not None:
        out_ref[...] = grad.astype(BF16)
        edge_ref[...] = grad[0:EDGE].astype(BF16)
    mine = lax.axis_index("section") == keep_ref[0]
    held_ref[...] = jnp.where(mine, grad, result_ref[...].astype(F32)).astype(BF16)


def last_key_kernel(operands, *refs):
    key_kernel(*refs[:operands], None, None, *refs[operands:])


def call(kernel, name, operands, outs, scratch, copies=0, limit=VMEM_LIMIT):
    kinds = {
        "s": pl.BlockSpec(memory_space=pltpu.SMEM),
        "v": pl.BlockSpec(memory_space=pltpu.VMEM),
        "h": pl.BlockSpec(memory_space=pltpu.HBM),
    }
    return pl.pallas_call(
        kernel,
        name=name,
        in_specs=[kinds[place] for _, place in operands],
        out_specs=[kinds["v"]] * len(outs),
        out_shape=[jax.ShapeDtypeStruct(shape, dtype) for shape, dtype in outs],
        scratch_shapes=[pltpu.VMEM(shape, dtype) for shape, dtype in scratch]
        + [pltpu.SemaphoreType.DMA((copies,))] * (copies > 0),
        compiler_params=pltpu.CompilerParams(vmem_limit_bytes=limit),
        cost_estimate=pl.CostEstimate(flops=1 << 30, bytes_accessed=4 << 20, transcendentals=0),
    )(*[array for array, _ in operands])


def placed(kinds, *arrays):
    return list(zip(arrays, kinds, strict=True))


def after(value, *others):
    return lax.optimization_barrier((value, *others))[0]


def shards(
    layer_inputs, top_grad, w_query, w_key, w_value, w_out, conv_kernel, norm_gain, group_valid
):
    own = layer_inputs[0]
    width = own.shape[1]
    wide = w_query.shape[2]
    query_weight = w_query[0]
    key_weight = w_key[0]
    value_weight = w_value[0]
    out_weight = w_out[0]
    kernel = conv_kernel[0]
    sections = lax.axis_size("section")
    count = lax.axis_size("tm")

    def moved(value, pairs):
        return lax.ppermute(value, ("tm", "section"), pairs)

    def at(layer, frame):
        return frame * sections + layer

    def across(steps, chosen):
        return [
            (at(section, source), at(section, source + steps))
            for section in chosen
            for source in range(max(0, -steps), min(count, count - steps))
        ]

    every = range(sections)
    half_edge = EDGE // 2
    swap = [(at(section, source), at(section, source ^ 1)) for section in every for source in range(count)]
    weight = ((width, wide), BF16)
    queries, kept, ahead, behind = call(
        project_kernel,
        "project",
        placed("hhvhhh", own, top_grad, norm_gain, query_weight, key_weight, value_weight),
        [
            ((ROWS, wide), BF16),
            ((ROWS, 2 * wide), BF16),
            ((ROWS + EDGE + half_edge, width), BF16),
            ((ROWS + 2 * EDGE + half_edge, width), BF16),
        ],
        [((ROWS, width), BF16), ((ROWS, width), BF16), ((EDGE, width), BF16), weight, weight, weight],
        5,
        VMEM_WHOLE,
    )
    back2 = moved(ahead, across(2, every))
    back4 = moved(kept, across(4, every))
    after1 = moved(behind, across(-1, every))
    peer = moved(ahead, swap)
    query_peer = moved(queries, swap)
    peer_back2 = moved(back2, swap)
    peer_back4 = moved(back4, swap)
    chip_pairs = [
        (at(section, source), at(section, source - 2 - 2 * (source % 2)))
        for section in every
        for source in range(count)
        if source >= 2 + 2 * (source % 2)
    ]
    query_far = moved(jnp.concatenate([queries, after(query_peer, peer)]), chip_pairs)
    query_peer_far = moved(query_far, swap)
    far_pairs = [
        (at(section, source), at(section, source + 5))
        for section in every
        for source in range(1, count - 5, 2)
    ]
    back5 = moved(after(kept, back2), far_pairs)
    query_peer, query_far, query_peer_far, after1 = lax.optimization_barrier(
        (query_peer, query_far, query_peer_far, after1)
    )

    span = (LEFT + 1) * ROWS
    attended, logs = call(
        attend_kernel,
        "attend",
        placed("svvvvvvvv", group_valid, queries, kept, back2, back4, peer, peer_back2, peer_back4, after1),
        [((ROWS + EDGE, wide), BF16), ((ROWS, PAIR), F32)],
        [(((LEFT + 2) * ROWS, 2 * wide), BF16), ((ROWS + EDGE, wide), BF16)],
    )
    back5 = after(back5, attended)
    step_outs = [((ROWS, width), F32), ((ROWS + 16, wide), BF16), ((ROWS, PAIR), F32)]
    slope, total, message, dots = call(
        mix_kernel,
        "mix",
        placed(
            "svvvvvvvvvvvvv",
            group_valid,
            own,
            top_grad,
            attended,
            logs,
            back2,
            back4,
            back5,
            peer,
            peer_back2,
            peer_back4,
            after1,
            out_weight,
            kernel,
        ),
        [((ROWS + EDGE, width), F32)] + step_outs,
        [
            ((span, 2 * wide), BF16),
            ((EDGE, wide), BF16),
            ((ROWS + 2 * EDGE, wide), BF16),
            ((ROWS + 2 * EDGE, width), F32),
            ((ROWS, width), BF16),
            ((EDGE + half_edge, width), BF16),
        ],
    )

    result = own
    upstream = None
    upstream_next = None
    for step in range(sections):
        layer = sections - 1 - step
        if step > 0:
            total, message, dots = call(
                mixer_kernel,
                "mixer",
                placed(
                    "svvvvvvv", group_valid, upstream, upstream_next, slope, kernel, out_weight, attended, logs
                ),
                step_outs,
                [((ROWS, width), BF16)],
                    )
        here = [layer]
        grad2 = moved(message, across(-2, here))
        grad4 = moved(message, across(-4, here))
        peer_grad = moved(message, swap)
        partial, key_sum, value_sum = call(
            query_kernel,
            "own_queries",
            placed(
                "svvvvvvvvvvv",
                group_valid,
                queries,
                kept,
                back2,
                back4,
                peer,
                peer_back2,
                peer_back4,
                message,
                logs,
                dots,
                query_weight,
            ),
            [((ROWS, width), F32), ((ROWS, wide), F32), ((ROWS, wide), F32)],
            [
                ((span, 2 * wide), BF16),
                ((ROWS, wide), BF16),
            ],
            )
        grad2 = after(grad2, partial)
        grad4 = after(grad4, partial)
        peer_grad2 = moved(grad2, swap)
        peer_grad4 = moved(grad4, swap)
        key_operands = placed(
            "svvvvvvvvvvvvvvvvvvs",
            group_valid,
            kept,
            query_peer,
            query_far,
            query_peer_far,
            grad2,
            grad4,
            peer_grad,
            peer_grad2,
            peer_grad4,
            key_weight,
            value_weight,
            norm_gain,
            own,
            total,
            partial,
            key_sum,
            value_sum,
            result,
            jnp.full((1,), layer, jnp.int32),
            )
        key_scratch = [
            ((LEFT * ROWS, wide), BF16),
            ((LEFT * ROWS, wide), BF16),
            ((LEFT * 16, wide), BF16),
            ((16, LEFT * ROWS), F32),
            ((ROWS, wide), BF16),
            ((ROWS, wide), BF16),
        ]
        whole = ((ROWS, width), BF16)
        if layer > 0:
            input_grad, edge, result = call(
                key_kernel, "own_keys", key_operands, [whole, ((EDGE, width), BF16), whole], key_scratch
            )
        else:
            (result,) = call(
                functools.partial(last_key_kernel, len(key_operands)),
                "last_keys",
                key_operands,
                [whole],
                key_scratch,
            )
        if layer > 0:
            upstream = moved(
                input_grad,
                [(at(layer, source), at(layer - 1, source)) for source in range(count)]
                + [(at(layer - 1, source), at(layer, source)) for source in range(count)],
            )
            upstream_next = moved(
                edge, [(at(layer, source), at(layer - 1, source - 1)) for source in range(1, count)]
            )
    return result[None]


def solution(mesh):
    placed = (
        P("section", "tm", None),
        P("tm", None),
        P("section", None, None),
        P("section", None, None),
        P("section", None, None),
        P("section", None, None),
        P("section", None, None),
        P("section", None),
        P(),
    )
    return jax.shard_map(
        shards, mesh=mesh, in_specs=placed, out_specs=P("section", "tm", None), check_vma=False
    )
```

```python
import functools

import jax
import jax.numpy as jnp
from jax import lax
from jax.experimental import pallas as pl
from jax.experimental.pallas import tpu as pltpu
from jax.sharding import PartitionSpec as P

HEAD_DIM = 64
PAIR = 128
ROWS = 128
LEFT = 4
EDGE = 32
SCALE = HEAD_DIM ** (-0.5)
NEGATIVE = -1e30
EPSILON = 1e-05
F32 = jnp.float32
BF16 = jnp.bfloat16
VMEM_LIMIT = 20 << 20
VMEM_WHOLE = 60 << 20


def dot_nn(a, b):
    return lax.dot_general(a, b, (((1,), (0,)), ((), ())), preferred_element_type=F32)


def dot_nt(a, b):
    return lax.dot_general(a, b, (((1,), (1,)), ((), ())), preferred_element_type=F32)


def valid_count(valid_ref, block):
    groups = valid_ref.shape[0]
    inside = (block >= 0) & (block < groups)
    return jnp.where(inside, valid_ref[jnp.clip(block, 0, groups - 1)], 0)


def even_half(rows):
    return lax.broadcasted_iota(jnp.int32, (rows, PAIR), 1) < HEAD_DIM


def unit_rows(values):
    center = values - jnp.mean(values, axis=-1, keepdims=True)
    spread = jnp.mean(center * center, axis=-1, keepdims=True)
    inverse = lax.rsqrt(spread + EPSILON)
    return center * inverse, inverse


def three_parts(value):
    first = value.astype(BF16)
    rest = value - first.astype(F32)
    second = rest.astype(BF16)
    third = (rest - second.astype(F32)).astype(BF16)
    return first, second, third


def shift_rows(value, amount):
    if amount == 0:
        return value
    return pltpu.roll(value, value.shape[0] - amount, 0)


def tap_sum(padded, kernel_ref, lanes, first, step, rows):
    taps = kernel_ref.shape[0]
    total = jnp.zeros((rows, padded.shape[1]), F32)
    for phase in range(8):
        moved = None
        for tap in range(taps):
            offset = first + step * tap
            if offset % 8 != phase:
                continue
            if moved is None:
                moved = shift_rows(padded, phase)
            base = offset - phase
            total = total + kernel_ref[tap : tap + 1, lanes] * moved[base : base + rows]
    return total


def project_kernel(
    own_ref,
    top_ref,
    gain_ref,
    w_query_ref,
    w_key_ref,
    w_value_ref,
    queries_ref,
    kept_ref,
    ahead_ref,
    behind_ref,
    normed,
    own,
    top,
    w_query,
    w_key,
    w_value,
    semaphores,
):
    chunk = 16
    loads = [
        pltpu.make_async_copy(source, target, semaphores.at[index])
        for index, (source, target) in enumerate(
            (
                (own_ref, own),
                (w_key_ref, w_key),
                (w_value_ref, w_value),
                (w_query_ref, w_query),
                (top_ref.at[0:EDGE], top),
            )
        )
    ]
    for load in loads:
        load.start()
    loads[0].wait()

    def norm_step(step, carry):
        rows = pl.ds(pl.multiple_of(step * chunk, chunk), chunk)
        unit, _ = unit_rows(own[rows, :].astype(F32))
        normed[rows, :] = (unit * gain_ref[...]).astype(BF16)
        return carry

    lax.fori_loop(0, ROWS // chunk, norm_step, 0, unroll=True)
    wide = w_key_ref.shape[1]
    half = EDGE // 2
    loads[1].wait()
    keys = dot_nn(normed[...], w_key[...]).astype(BF16)
    loads[2].wait()
    values = dot_nn(normed[...], w_value[...]).astype(BF16)
    for ref in (kept_ref, ahead_ref, behind_ref):
        ref[0:ROWS, 0:wide] = keys
        ref[0:ROWS, wide : 2 * wide] = values
    loads[3].wait()
    loads[4].wait()
    queries = dot_nn(normed[...], w_query[...]).astype(BF16)
    queries_ref[...] = queries
    ahead_ref[ROWS : ROWS + EDGE, :] = own[ROWS - EDGE : ROWS, :]
    ahead_ref[ROWS + EDGE : ROWS + EDGE + half, 0:wide] = queries[ROWS - EDGE : ROWS - half]
    ahead_ref[ROWS + EDGE : ROWS + EDGE + half, wide : 2 * wide] = queries[ROWS - half : ROWS]
    behind_ref[ROWS : ROWS + EDGE, :] = own[0:EDGE, :]
    behind_ref[ROWS + EDGE : ROWS + EDGE + half, 0:wide] = queries[0:half]
    behind_ref[ROWS + EDGE : ROWS + EDGE + half, wide : 2 * wide] = queries[half:EDGE]
    behind_ref[ROWS + EDGE + half : ROWS + 2 * EDGE + half, :] = top[...]


def choose_rows(target, odd, when_odd, when_even, rows):
    if when_even is when_odd:
        target[...] = when_odd[rows, :]
        return

    @pl.when(odd)
    def _():
        target[...] = when_odd[rows, :]

    @pl.when(jnp.logical_not(odd))
    def _():
        target[...] = when_even[rows, :]


def choose_blocks(target, odd, sources):
    for index, (when_odd, when_even) in enumerate(sources):
        choose_rows(target.at[index * ROWS : (index + 1) * ROWS], odd, when_odd, when_even, slice(0, ROWS))


def masked_half(value, half):
    keep = even_half(value.shape[0])
    if half:
        keep = jnp.logical_not(keep)
    return jnp.where(keep, value, jnp.zeros_like(value))


def pair_shares(scores, allowed):
    part = jnp.where(allowed, scores, NEGATIVE)
    highest = jnp.max(part, axis=-1, keepdims=True)
    exped = jnp.exp(part - highest)
    summed = jnp.sum(exped, axis=-1, keepdims=True)
    return (exped * (1.0 / summed)).astype(BF16), highest, summed


def attend_kernel(
    valid_ref,
    queries_ref,
    kept_ref,
    back2_ref,
    back4_ref,
    peer_ref,
    peer_back2_ref,
    peer_back4_ref,
    after_ref,
    attended_ref,
    log_ref,
    window,
    query_all,
):
    place = lax.axis_index("tm")
    odd = lax.rem(place, 2) == 1
    wide = queries_ref.shape[1]
    half_edge = EDGE // 2
    packed = after_ref[ROWS + EDGE : ROWS + EDGE + half_edge, :]
    query_all[0:ROWS, :] = queries_ref[...]
    choose_blocks(
        window,
        odd,
        (
            (back4_ref, back4_ref),
            (peer_back2_ref, peer_back4_ref),
            (back2_ref, back2_ref),
            (peer_ref, peer_back2_ref),
            (kept_ref, kept_ref),
            (after_ref, after_ref),
        ),
    )
    query_all[ROWS : ROWS + half_edge, :] = packed[:, 0:wide]
    query_all[ROWS + half_edge : ROWS + EDGE, :] = packed[:, wide : 2 * wide]
    key_lane = lax.broadcasted_iota(jnp.int32, (1, ROWS), 1)
    allowed = jnp.concatenate(
        [key_lane < valid_count(valid_ref, place + block - LEFT) for block in range(LEFT + 2)], axis=1
    )
    span = (LEFT + 1) * ROWS
    log_lane = lax.broadcasted_iota(jnp.int32, (ROWS, PAIR), 1)
    logs = jnp.zeros((ROWS, PAIR), F32)
    for pair in range(wide // PAIR):
        lanes = slice(pair * PAIR, (pair + 1) * PAIR)
        value_lanes = slice(wide + pair * PAIR, wide + (pair + 1) * PAIR)
        totals = [None, None]
        for half in range(2):
            scores = dot_nt(query_all[:, lanes], masked_half(window[:, lanes], half)) * SCALE
            value_half = masked_half(window[:, value_lanes], half)
            for group, (low, high, first) in enumerate(((0, ROWS, 0), (ROWS, ROWS + EDGE, ROWS))):
                shares_low, highest, summed = pair_shares(
                    scores[low:high, first : first + span], allowed[:, first : first + span]
                )
                product = dot_nn(shares_low, value_half[first : first + span])
                totals[group] = product if totals[group] is None else totals[group] + product
                if group == 0:
                    logs = jnp.where(log_lane == 2 * pair + half, highest + jnp.log(summed), logs)
        attended_ref[0:ROWS, lanes] = totals[0].astype(BF16)
        attended_ref[ROWS : ROWS + EDGE, lanes] = totals[1].astype(BF16)
    log_ref[...] = logs


def mixer_body(
    count, upstream_ref, next_rows, slope_ref, kernel_ref, w_out_ref, attended, log_ref, total_ref, message_ref, dot_ref, total_low
):
    row_ids = lax.broadcasted_iota(jnp.int32, (ROWS, PAIR), 0)
    taps = kernel_ref.shape[0]

    def conv_step(step, carry):
        lanes = pl.ds(pl.multiple_of(step * PAIR, PAIR), PAIR)
        upper = upstream_ref[:, lanes].astype(F32)
        stacked = jnp.concatenate([upper, next_rows(lanes)], axis=0)
        grads = (stacked * slope_ref[:, lanes]).astype(BF16).astype(F32)
        back = tap_sum(grads, kernel_ref, lanes, taps - 1, -1, ROWS)
        total = upper + jnp.where(row_ids < count, back, 0.0)
        total_ref[:, lanes] = total
        total_low[:, lanes] = total.astype(BF16)
        return carry

    lax.fori_loop(0, upstream_ref.shape[1] // PAIR, conv_step, 0, unroll=True)
    out_grad = dot_nt(total_low[...], w_out_ref[...]).astype(BF16)
    message_ref[0:ROWS, :] = out_grad
    product = out_grad.astype(F32) * attended[...].astype(F32)
    high = product.astype(BF16)
    low = (product - high.astype(F32)).astype(BF16)
    width = product.shape[1]
    head_of = lax.broadcasted_iota(jnp.int32, (PAIR, width), 1) // HEAD_DIM
    chosen = (head_of == lax.broadcasted_iota(jnp.int32, (PAIR, width), 0)).astype(F32).astype(BF16)
    dots = dot_nt(high, chosen) + dot_nt(low, chosen)
    dot_ref[...] = dots
    stacked = jnp.concatenate([log_ref[...].T[0:8], dots.T[0:8]], axis=0)
    message_ref[ROWS : ROWS + 16, :] = jnp.zeros((16, width), BF16)
    for index, part in enumerate(three_parts(stacked)):
        message_ref[ROWS : ROWS + 16, index * PAIR : (index + 1) * PAIR] = part


def mix_kernel(
    valid_ref,
    own_ref,
    top_ref,
    attended_ref,
    log_ref,
    back2_ref,
    back4_ref,
    back5_ref,
    peer_ref,
    peer_back2_ref,
    peer_back4_ref,
    after_ref,
    w_out_ref,
    kernel_ref,
    slope_ref,
    total_ref,
    message_ref,
    dot_ref,
    window,
    query_tail,
    attended_all,
    mixed,
    total_low,
    before_rows,
):
    place = lax.axis_index("tm")
    odd = lax.rem(place, 2) == 1
    wide = query_tail.shape[1]
    half_edge = EDGE // 2
    counts = [valid_count(valid_ref, place + block - LEFT - 1) for block in range(LEFT + 3)]
    choose_rows(before_rows, odd, peer_ref, peer_back2_ref, slice(ROWS, ROWS + EDGE + half_edge))
    choose_blocks(
        window,
        odd,
        (
            (peer_back4_ref, back5_ref),
            (back4_ref, back4_ref),
            (peer_back2_ref, peer_back4_ref),
            (back2_ref, back2_ref),
            (peer_ref, peer_back2_ref),
        ),
    )
    attended_all[EDGE:, :] = attended_ref[...]
    query_tail[0:half_edge, :] = before_rows[EDGE : EDGE + half_edge, 0:wide]
    query_tail[half_edge:EDGE, :] = before_rows[EDGE : EDGE + half_edge, wide : 2 * wide]
    key_lane = lax.broadcasted_iota(jnp.int32, (1, ROWS), 1)
    allowed = jnp.concatenate([key_lane < count for count in counts[: LEFT + 1]], axis=1)
    for pair in range(wide // PAIR):
        lanes = slice(pair * PAIR, (pair + 1) * PAIR)
        value_lanes = slice(wide + pair * PAIR, wide + (pair + 1) * PAIR)
        total = None
        for half in range(2):
            scores = dot_nt(query_tail[:, lanes], masked_half(window[:, lanes], half)) * SCALE
            shares_low, _, _ = pair_shares(scores, allowed)
            product = dot_nn(shares_low, masked_half(window[:, value_lanes], half))
            total = product if total is None else total + product
        attended_all[0:EDGE, lanes] = total.astype(BF16)
    projected = dot_nn(attended_all[...], w_out_ref[...])
    row_ids = lax.broadcasted_iota(jnp.int32, (ROWS, 1), 0)
    edge_ids = lax.broadcasted_iota(jnp.int32, (EDGE, 1), 0)
    before = projected[0:EDGE] + before_rows[0:EDGE, :].astype(F32)
    here = projected[EDGE : EDGE + ROWS] + own_ref[...].astype(F32)
    after = projected[EDGE + ROWS :] + after_ref[ROWS : ROWS + EDGE, :].astype(F32)
    before = jnp.where(edge_ids + (ROWS - EDGE) < counts[LEFT], before, 0.0)
    here = jnp.where(row_ids < counts[LEFT + 1], here, 0.0)
    after = jnp.where(edge_ids < counts[LEFT + 2], after, 0.0)
    mixed[0:EDGE, :] = before.astype(BF16).astype(F32)
    mixed[EDGE : EDGE + ROWS, :] = here.astype(BF16).astype(F32)
    mixed[EDGE + ROWS :, :] = after.astype(BF16).astype(F32)
    taps = kernel_ref.shape[0]

    def conv_step(step, carry):
        lanes = pl.ds(pl.multiple_of(step * PAIR, PAIR), PAIR)
        output = tap_sum(mixed[:, lanes], kernel_ref, lanes, EDGE - (taps - 1), 1, ROWS + EDGE)
        gate = 1.0 / (1.0 + jnp.exp(-output))
        slope_ref[:, lanes] = gate * (1.0 + output * (1.0 - gate))
        return carry

    lax.fori_loop(0, own_ref.shape[1] // PAIR, conv_step, 0, unroll=True)
    first = ROWS + EDGE + half_edge
    mixer_body(
        counts[LEFT + 1],
        top_ref,
        lambda lanes: after_ref[first : first + EDGE, lanes].astype(F32),
        slope_ref,
        kernel_ref,
        w_out_ref,
        attended_all[EDGE : EDGE + ROWS, :],
        log_ref,
        total_ref,
        message_ref,
        dot_ref,
        total_low,
    )


def mixer_kernel(
    valid_ref,
    upstream_ref,
    next_ref,
    slope_ref,
    kernel_ref,
    w_out_ref,
    attended_ref,
    log_ref,
    total_ref,
    message_ref,
    dot_ref,
    total_low,
):
    mixer_body(
        valid_count(valid_ref, lax.axis_index("tm")),
        upstream_ref,
        lambda lanes: next_ref[:, lanes].astype(F32),
        slope_ref,
        kernel_ref,
        w_out_ref,
        attended_ref[0:ROWS, :],
        log_ref,
        total_ref,
        message_ref,
        dot_ref,
        total_low,
    )


def key_terms(key_pair, value_pair, query_pair, grad_pair, logs, dots, key_valid):
    share_halves = []
    score_halves = []
    query_halves = [masked_half(query_pair, half) for half in range(2)]
    grad_halves = [masked_half(grad_pair, half) for half in range(2)]
    for half in range(2):
        scores = dot_nt(key_pair, query_halves[half]) * SCALE
        shares = jnp.exp(jnp.where(key_valid, scores, NEGATIVE) - logs[half])
        share_grad = dot_nt(value_pair, grad_halves[half])
        score_halves.append((shares * (share_grad - dots[half])).astype(BF16))
        share_halves.append(shares.astype(BF16))
    key_sum = None
    value_sum = None
    for block in range(query_pair.shape[0] // ROWS):
        rows = slice(block * ROWS, (block + 1) * ROWS)
        key_term = dot_nn(
            jnp.concatenate([score[:, rows] for score in score_halves], axis=1),
            jnp.concatenate([query[rows] for query in query_halves], axis=0),
        )
        value_term = dot_nn(
            jnp.concatenate([share[:, rows] for share in share_halves], axis=1),
            jnp.concatenate([grad[rows] for grad in grad_halves], axis=0),
        )
        key_term = (key_term * SCALE).astype(BF16).astype(F32)
        value_term = value_term.astype(BF16).astype(F32)
        key_sum = key_term if key_sum is None else key_sum + key_term
        value_sum = value_term if value_sum is None else value_sum + value_term
    return key_sum, value_sum


def message_stats(tail):
    tail = tail.astype(F32)
    return tail[:, 0:PAIR] + tail[:, PAIR : 2 * PAIR] + tail[:, 2 * PAIR : 3 * PAIR]


def query_kernel(
    valid_ref,
    queries_ref,
    kept_ref,
    back2_ref,
    back4_ref,
    peer_ref,
    peer_back2_ref,
    peer_back4_ref,
    message_ref,
    log_ref,
    dot_ref,
    w_query_ref,
    out_ref,
    key_sum_ref,
    value_sum_ref,
    window,
    query_grad,
):
    place = lax.axis_index("tm")
    odd = lax.rem(place, 2) == 1
    wide = queries_ref.shape[1]
    choose_blocks(
        window,
        odd,
        (
            (back4_ref, back4_ref),
            (peer_back2_ref, peer_back4_ref),
            (back2_ref, back2_ref),
            (peer_ref, peer_back2_ref),
            (kept_ref, kept_ref),
        ),
    )
    own_rows = slice(LEFT * ROWS, (LEFT + 1) * ROWS)
    key_lane = lax.broadcasted_iota(jnp.int32, (1, ROWS), 1)
    allowed = jnp.concatenate(
        [key_lane < valid_count(valid_ref, place + block - LEFT) for block in range(LEFT + 1)], axis=1
    )
    key_valid = lax.broadcasted_iota(jnp.int32, (ROWS, ROWS), 0) < valid_count(valid_ref, place)
    stats = message_stats(message_ref[ROWS : ROWS + 16, :])
    for pair in range(wide // PAIR):
        lanes = slice(pair * PAIR, (pair + 1) * PAIR)
        value_lanes = slice(wide + pair * PAIR, wide + (pair + 1) * PAIR)
        query_pair = queries_ref[:, lanes]
        grad_pair = message_ref[0:ROWS, lanes]
        total = None
        for half in range(2):
            key_half = masked_half(window[:, lanes], half)
            value_half = masked_half(window[:, value_lanes], half)
            head = 2 * pair + half
            scores = dot_nt(query_pair, key_half) * SCALE
            shares = jnp.exp(jnp.where(allowed, scores, NEGATIVE) - log_ref[:, head : head + 1])
            share_grad = dot_nt(grad_pair, value_half)
            score_grad = (shares * (share_grad - dot_ref[:, head : head + 1])).astype(BF16)
            product = dot_nn(score_grad, key_half)
            total = product if total is None else total + product
        query_grad[:, lanes] = (total * SCALE).astype(BF16)
        heads = (2 * pair, 2 * pair + 1)
        key_sum_ref[:, lanes], value_sum_ref[:, lanes] = key_terms(
            window[own_rows, lanes],
            window[own_rows, value_lanes],
            query_pair,
            grad_pair,
            [stats[head : head + 1] for head in heads],
            [stats[8 + head : 9 + head] for head in heads],
            key_valid,
        )
    out_ref[...] = dot_nt(query_grad[...], w_query_ref[...])


def key_kernel(
    valid_ref,
    kept_ref,
    query_peer_ref,
    query_far_ref,
    query_peer_far_ref,
    next2_ref,
    next4_ref,
    peer_ref,
    peer_next2_ref,
    peer_next4_ref,
    w_key_ref,
    w_value_ref,
    gain_ref,
    own_ref,
    total_ref,
    partial_ref,
    key_sum_ref,
    value_sum_ref,
    result_ref,
    keep_ref,
    out_ref,
    edge_ref,
    held_ref,
    grads,
    queries,
    tails,
    stats,
    key_grad,
    value_grad,
):
    place = lax.axis_index("tm")
    odd = lax.rem(place, 2) == 1
    count = valid_count(valid_ref, place)
    wide = grads.shape[1]
    messages = (
        (peer_next2_ref, peer_ref),
        (next2_ref, next2_ref),
        (peer_next4_ref, peer_next2_ref),
        (next4_ref, next4_ref),
    )
    choose_blocks(grads, odd, messages)
    for block, (when_odd, when_even) in enumerate(messages):
        target = tails.at[block * 16 : block * 16 + 16]
        choose_rows(target, odd, when_odd, when_even, slice(ROWS, ROWS + 16))
    choose_blocks(
        queries,
        odd,
        (
            (query_peer_far_ref.at[0:ROWS], query_peer_ref),
            (query_peer_far_ref.at[ROWS : 2 * ROWS], query_far_ref.at[0:ROWS]),
            (query_far_ref.at[ROWS : 2 * ROWS], query_far_ref.at[ROWS : 2 * ROWS]),
            (query_far_ref.at[0:ROWS], query_peer_far_ref.at[ROWS : 2 * ROWS]),
        ),
    )
    for block in range(LEFT):
        stats[:, block * ROWS : (block + 1) * ROWS] = message_stats(tails[block * 16 : block * 16 + 16, :])
    key_valid = lax.broadcasted_iota(jnp.int32, (ROWS, LEFT * ROWS), 0) < count
    for pair in range(wide // PAIR):
        lanes = slice(pair * PAIR, (pair + 1) * PAIR)
        heads = (2 * pair, 2 * pair + 1)
        key_sum, value_sum = key_terms(
            kept_ref[:, lanes],
            kept_ref[:, slice(wide + pair * PAIR, wide + (pair + 1) * PAIR)],
            queries[:, lanes],
            grads[:, lanes],
            [stats[head : head + 1, :] for head in heads],
            [stats[8 + head : 9 + head, :] for head in heads],
            key_valid,
        )
        key_grad[:, lanes] = (key_sum_ref[:, lanes] + key_sum).astype(BF16)
        value_grad[:, lanes] = (value_sum_ref[:, lanes] + value_sum).astype(BF16)
    normed_grad = partial_ref[...] + dot_nt(key_grad[...], w_key_ref[...])
    normed_grad = normed_grad + dot_nt(value_grad[...], w_value_ref[...])
    scaled = normed_grad * gain_ref[...]
    unit, inverse = unit_rows(own_ref[...].astype(F32))
    back = inverse * (
        scaled
        - jnp.mean(scaled, axis=-1, keepdims=True)
        - unit * jnp.mean(scaled * unit, axis=-1, keepdims=True)
    )
    grad = total_ref[...] + back
    if out_ref is not None:
        out_ref[...] = grad.astype(BF16)
        edge_ref[...] = grad[0:EDGE].astype(BF16)
    mine = lax.axis_index("section") == keep_ref[0]
    held_ref[...] = jnp.where(mine, grad, result_ref[...].astype(F32)).astype(BF16)


def last_key_kernel(operands, *refs):
    key_kernel(*refs[:operands], None, None, *refs[operands:])


def call(kernel, name, operands, outs, scratch, copies=0, limit=VMEM_LIMIT):
    kinds = {
        "s": pl.BlockSpec(memory_space=pltpu.SMEM),
        "v": pl.BlockSpec(memory_space=pltpu.VMEM),
        "h": pl.BlockSpec(memory_space=pltpu.HBM),
    }
    return pl.pallas_call(
        kernel,
        name=name,
        in_specs=[kinds[place] for _, place in operands],
        out_specs=[kinds["v"]] * len(outs),
        out_shape=[jax.ShapeDtypeStruct(shape, dtype) for shape, dtype in outs],
        scratch_shapes=[pltpu.VMEM(shape, dtype) for shape, dtype in scratch]
        + [pltpu.SemaphoreType.DMA((copies,))] * (copies > 0),
        compiler_params=pltpu.CompilerParams(vmem_limit_bytes=limit),
        cost_estimate=pl.CostEstimate(flops=1 << 30, bytes_accessed=4 << 20, transcendentals=0),
    )(*[array for array, _ in operands])


def placed(kinds, *arrays):
    return list(zip(arrays, kinds, strict=True))


def after(value, *others):
    return lax.optimization_barrier((value, *others))[0]


def shards(
    layer_inputs, top_grad, w_query, w_key, w_value, w_out, conv_kernel, norm_gain, group_valid
):
    own = layer_inputs[0]
    width = own.shape[1]
    wide = w_query.shape[2]
    query_weight = w_query[0]
    key_weight = w_key[0]
    value_weight = w_value[0]
    out_weight = w_out[0]
    kernel = conv_kernel[0]
    sections = lax.axis_size("section")
    count = lax.axis_size("tm")

    def moved(value, pairs):
        return lax.ppermute(value, ("tm", "section"), pairs)

    def at(layer, frame):
        return frame * sections + layer

    def across(steps, chosen):
        return [
            (at(section, source), at(section, source + steps))
            for section in chosen
            for source in range(max(0, -steps), min(count, count - steps))
        ]

    every = range(sections)
    half_edge = EDGE // 2
    swap = [(at(section, source), at(section, source ^ 1)) for section in every for source in range(count)]
    weight = ((width, wide), BF16)
    queries, kept, ahead, behind = call(
        project_kernel,
        "project",
        placed("hhvhhh", own, top_grad, norm_gain, query_weight, key_weight, value_weight),
        [
            ((ROWS, wide), BF16),
            ((ROWS, 2 * wide), BF16),
            ((ROWS + EDGE + half_edge, width), BF16),
            ((ROWS + 2 * EDGE + half_edge, width), BF16),
        ],
        [((ROWS, width), BF16), ((ROWS, width), BF16), ((EDGE, width), BF16), weight, weight, weight],
        5,
        VMEM_WHOLE,
    )
    back2 = moved(ahead, across(2, every))
    back4 = moved(kept, across(4, every))
    after1 = moved(behind, across(-1, every))
    peer = moved(ahead, swap)
    query_peer = moved(queries, swap)
    peer_back2 = moved(back2, swap)
    peer_back4 = moved(back4, swap)
    chip_pairs = [
        (at(section, source), at(section, source - 2 - 2 * (source % 2)))
        for section in every
        for source in range(count)
        if source >= 2 + 2 * (source % 2)
    ]
    query_far = moved(jnp.concatenate([queries, after(query_peer, peer)]), chip_pairs)
    query_peer_far = moved(query_far, swap)
    far_pairs = [
        (at(section, source), at(section, source + 5))
        for section in every
        for source in range(1, count - 5, 2)
    ]
    back5 = moved(after(kept, back2), far_pairs)
    query_peer, query_far, query_peer_far, after1 = lax.optimization_barrier(
        (query_peer, query_far, query_peer_far, after1)
    )

    span = (LEFT + 1) * ROWS
    attended, logs = call(
        attend_kernel,
        "attend",
        placed("svvvvvvvv", group_valid, queries, kept, back2, back4, peer, peer_back2, peer_back4, after1),
        [((ROWS + EDGE, wide), BF16), ((ROWS, PAIR), F32)],
        [(((LEFT + 2) * ROWS, 2 * wide), BF16), ((ROWS + EDGE, wide), BF16)],
    )
    back5 = after(back5, attended)
    step_outs = [((ROWS, width), F32), ((ROWS + 16, wide), BF16), ((ROWS, PAIR), F32)]
    slope, total, message, dots = call(
        mix_kernel,
        "mix",
        placed(
            "svvvvvvvvvvvvv",
            group_valid,
            own,
            top_grad,
            attended,
            logs,
            back2,
            back4,
            back5,
            peer,
            peer_back2,
            peer_back4,
            after1,
            out_weight,
            kernel,
        ),
        [((ROWS + EDGE, width), F32)] + step_outs,
        [
            ((span, 2 * wide), BF16),
            ((EDGE, wide), BF16),
            ((ROWS + 2 * EDGE, wide), BF16),
            ((ROWS + 2 * EDGE, width), F32),
            ((ROWS, width), BF16),
            ((EDGE + half_edge, width), BF16),
        ],
    )

    result = own
    upstream = None
    upstream_next = None
    for step in range(sections):
        layer = sections - 1 - step
        if step > 0:
            total, message, dots = call(
                mixer_kernel,
                "mixer",
                placed(
                    "svvvvvvv", group_valid, upstream, upstream_next, slope, kernel, out_weight, attended, logs
                ),
                step_outs,
                [((ROWS, width), BF16)],
                    )
        here = [layer]
        grad2 = moved(message, across(-2, here))
        grad4 = moved(message, across(-4, here))
        peer_grad = moved(message, swap)
        partial, key_sum, value_sum = call(
            query_kernel,
            "own_queries",
            placed(
                "svvvvvvvvvvv",
                group_valid,
                queries,
                kept,
                back2,
                back4,
                peer,
                peer_back2,
                peer_back4,
                message,
                logs,
                dots,
                query_weight,
            ),
            [((ROWS, width), F32), ((ROWS, wide), F32), ((ROWS, wide), F32)],
            [
                ((span, 2 * wide), BF16),
                ((ROWS, wide), BF16),
            ],
            )
        grad2 = after(grad2, partial)
        grad4 = after(grad4, partial)
        peer_grad2 = moved(grad2, swap)
        peer_grad4 = moved(grad4, swap)
        key_operands = placed(
            "svvvvvvvvvvvvvvvvvvs",
            group_valid,
            kept,
            query_peer,
            query_far,
            query_peer_far,
            grad2,
            grad4,
            peer_grad,
            peer_grad2,
            peer_grad4,
            key_weight,
            value_weight,
            norm_gain,
            own,
            total,
            partial,
            key_sum,
            value_sum,
            result,
            jnp.full((1,), layer, jnp.int32),
            )
        key_scratch = [
            ((LEFT * ROWS, wide), BF16),
            ((LEFT * ROWS, wide), BF16),
            ((LEFT * 16, wide), BF16),
            ((16, LEFT * ROWS), F32),
            ((ROWS, wide), BF16),
            ((ROWS, wide), BF16),
        ]
        whole = ((ROWS, width), BF16)
        if layer > 0:
            input_grad, edge, result = call(
                key_kernel, "own_keys", key_operands, [whole, ((EDGE, width), BF16), whole], key_scratch
            )
        else:
            (result,) = call(
                functools.partial(last_key_kernel, len(key_operands)),
                "last_keys",
                key_operands,
                [whole],
                key_scratch,
            )
        if layer > 0:
            upstream = moved(
                input_grad,
                [(at(layer, source), at(layer - 1, source)) for source in range(count)]
                + [(at(layer - 1, source), at(layer, source)) for source in range(count)],
            )
            upstream_next = moved(
                edge, [(at(layer, source), at(layer - 1, source - 1)) for source in range(1, count)]
            )
    return result[None]


def solution(mesh):
    placed = (
        P("section", "tm", None),
        P("tm", None),
        P("section", None, None),
        P("section", None, None),
        P("section", None, None),
        P("section", None, None),
        P("section", None, None),
        P("section", None),
        P(),
    )
    return jax.shard_map(
        shards, mesh=mesh, in_specs=placed, out_specs=P("section", "tm", None), check_vma=False
    )
```

```python
import functools

import jax
import jax.numpy as jnp
from jax import lax
from jax.experimental import pallas as pl
from jax.experimental.pallas import tpu as pltpu
from jax.sharding import PartitionSpec as P

HEAD_DIM = 64
PAIR = 128
ROWS = 128
LEFT = 4
EDGE = 32
SCALE = HEAD_DIM ** (-0.5)
NEGATIVE = -1e30
EPSILON = 1e-05
F32 = jnp.float32
BF16 = jnp.bfloat16
VMEM_LIMIT = 20 << 20
VMEM_WHOLE = 60 << 20


def dot_nn(a, b):
    return lax.dot_general(a, b, (((1,), (0,)), ((), ())), preferred_element_type=F32)


def dot_nt(a, b):
    return lax.dot_general(a, b, (((1,), (1,)), ((), ())), preferred_element_type=F32)


def valid_count(valid_ref, block):
    groups = valid_ref.shape[0]
    inside = (block >= 0) & (block < groups)
    return jnp.where(inside, valid_ref[jnp.clip(block, 0, groups - 1)], 0)


def even_half(rows):
    return lax.broadcasted_iota(jnp.int32, (rows, PAIR), 1) < HEAD_DIM


def unit_rows(values):
    center = values - jnp.mean(values, axis=-1, keepdims=True)
    spread = jnp.mean(center * center, axis=-1, keepdims=True)
    inverse = lax.rsqrt(spread + EPSILON)
    return center * inverse, inverse


def three_parts(value):
    first = value.astype(BF16)
    rest = value - first.astype(F32)
    second = rest.astype(BF16)
    third = (rest - second.astype(F32)).astype(BF16)
    return first, second, third


def shift_rows(value, amount):
    if amount == 0:
        return value
    return pltpu.roll(value, value.shape[0] - amount, 0)


def tap_sum(padded, kernel_ref, lanes, first, step, rows):
    taps = kernel_ref.shape[0]
    total = jnp.zeros((rows, padded.shape[1]), F32)
    for phase in range(8):
        moved = None
        for tap in range(taps):
            offset = first + step * tap
            if offset % 8 != phase:
                continue
            if moved is None:
                moved = shift_rows(padded, phase)
            base = offset - phase
            total = total + kernel_ref[tap : tap + 1, lanes] * moved[base : base + rows]
    return total


def project_kernel(
    own_ref,
    top_ref,
    gain_ref,
    w_query_ref,
    w_key_ref,
    w_value_ref,
    queries_ref,
    kept_ref,
    ahead_ref,
    behind_ref,
    normed,
    own,
    top,
    w_query,
    w_key,
    w_value,
    semaphores,
):
    chunk = 16
    loads = [
        pltpu.make_async_copy(source, target, semaphores.at[index])
        for index, (source, target) in enumerate(
            (
                (own_ref, own),
                (w_key_ref, w_key),
                (w_value_ref, w_value),
                (w_query_ref, w_query),
                (top_ref.at[0:EDGE], top),
            )
        )
    ]
    for load in loads:
        load.start()
    loads[0].wait()

    def norm_step(step, carry):
        rows = pl.ds(pl.multiple_of(step * chunk, chunk), chunk)
        unit, _ = unit_rows(own[rows, :].astype(F32))
        normed[rows, :] = (unit * gain_ref[...]).astype(BF16)
        return carry

    lax.fori_loop(0, ROWS // chunk, norm_step, 0, unroll=True)
    wide = w_key_ref.shape[1]
    half = EDGE // 2
    loads[1].wait()
    keys = dot_nn(normed[...], w_key[...]).astype(BF16)
    loads[2].wait()
    values = dot_nn(normed[...], w_value[...]).astype(BF16)
    for ref in (kept_ref, ahead_ref, behind_ref):
        ref[0:ROWS, 0:wide] = keys
        ref[0:ROWS, wide : 2 * wide] = values
    loads[3].wait()
    loads[4].wait()
    queries = dot_nn(normed[...], w_query[...]).astype(BF16)
    queries_ref[...] = queries
    ahead_ref[ROWS : ROWS + EDGE, :] = own[ROWS - EDGE : ROWS, :]
    ahead_ref[ROWS + EDGE : ROWS + EDGE + half, 0:wide] = queries[ROWS - EDGE : ROWS - half]
    ahead_ref[ROWS + EDGE : ROWS + EDGE + half, wide : 2 * wide] = queries[ROWS - half : ROWS]
    behind_ref[ROWS : ROWS + EDGE, :] = own[0:EDGE, :]
    behind_ref[ROWS + EDGE : ROWS + EDGE + half, 0:wide] = queries[0:half]
    behind_ref[ROWS + EDGE : ROWS + EDGE + half, wide : 2 * wide] = queries[half:EDGE]
    behind_ref[ROWS + EDGE + half : ROWS + 2 * EDGE + half, :] = top[...]


def choose_rows(target, odd, when_odd, when_even, rows):
    if when_even is when_odd:
        target[...] = when_odd[rows, :]
        return

    @pl.when(odd)
    def _():
        target[...] = when_odd[rows, :]

    @pl.when(jnp.logical_not(odd))
    def _():
        target[...] = when_even[rows, :]


def choose_blocks(target, odd, sources):
    for index, (when_odd, when_even) in enumerate(sources):
        choose_rows(target.at[index * ROWS : (index + 1) * ROWS], odd, when_odd, when_even, slice(0, ROWS))


def masked_half(value, half):
    keep = even_half(value.shape[0])
    if half:
        keep = jnp.logical_not(keep)
    return jnp.where(keep, value, jnp.zeros_like(value))


def pair_shares(scores, allowed):
    part = jnp.where(allowed, scores, NEGATIVE)
    highest = jnp.max(part, axis=-1, keepdims=True)
    exped = jnp.exp(part - highest)
    summed = jnp.sum(exped, axis=-1, keepdims=True)
    return (exped * (1.0 / summed)).astype(BF16), highest, summed


def attend_kernel(
    valid_ref,
    queries_ref,
    kept_ref,
    back2_ref,
    back4_ref,
    peer_ref,
    peer_back2_ref,
    peer_back4_ref,
    after_ref,
    attended_ref,
    log_ref,
    window,
    query_all,
):
    place = lax.axis_index("tm")
    odd = lax.rem(place, 2) == 1
    wide = queries_ref.shape[1]
    half_edge = EDGE // 2
    packed = after_ref[ROWS + EDGE : ROWS + EDGE + half_edge, :]
    query_all[0:ROWS, :] = queries_ref[...]
    choose_blocks(
        window,
        odd,
        (
            (back4_ref, back4_ref),
            (peer_back2_ref, peer_back4_ref),
            (back2_ref, back2_ref),
            (peer_ref, peer_back2_ref),
            (kept_ref, kept_ref),
            (after_ref, after_ref),
        ),
    )
    query_all[ROWS : ROWS + half_edge, :] = packed[:, 0:wide]
    query_all[ROWS + half_edge : ROWS + EDGE, :] = packed[:, wide : 2 * wide]
    key_lane = lax.broadcasted_iota(jnp.int32, (1, ROWS), 1)
    allowed = jnp.concatenate(
        [key_lane < valid_count(valid_ref, place + block - LEFT) for block in range(LEFT + 2)], axis=1
    )
    span = (LEFT + 1) * ROWS
    log_lane = lax.broadcasted_iota(jnp.int32, (ROWS, PAIR), 1)
    logs = jnp.zeros((ROWS, PAIR), F32)
    for pair in range(wide // PAIR):
        lanes = slice(pair * PAIR, (pair + 1) * PAIR)
        value_lanes = slice(wide + pair * PAIR, wide + (pair + 1) * PAIR)
        totals = [None, None]
        for half in range(2):
            scores = dot_nt(query_all[:, lanes], masked_half(window[:, lanes], half)) * SCALE
            value_half = masked_half(window[:, value_lanes], half)
            for group, (low, high, first) in enumerate(((0, ROWS, 0), (ROWS, ROWS + EDGE, ROWS))):
                shares_low, highest, summed = pair_shares(
                    scores[low:high, first : first + span], allowed[:, first : first + span]
                )
                product = dot_nn(shares_low, value_half[first : first + span])
                totals[group] = product if totals[group] is None else totals[group] + product
                if group == 0:
                    logs = jnp.where(log_lane == 2 * pair + half, highest + jnp.log(summed), logs)
        attended_ref[0:ROWS, lanes] = totals[0].astype(BF16)
        attended_ref[ROWS : ROWS + EDGE, lanes] = totals[1].astype(BF16)
    log_ref[...] = logs


def mixer_body(
    count, upstream_ref, next_rows, slope_ref, kernel_ref, w_out_ref, attended, log_ref, total_ref, message_ref, dot_ref, total_low
):
    row_ids = lax.broadcasted_iota(jnp.int32, (ROWS, PAIR), 0)
    taps = kernel_ref.shape[0]

    def conv_step(step, carry):
        lanes = pl.ds(pl.multiple_of(step * PAIR, PAIR), PAIR)
        upper = upstream_ref[:, lanes].astype(F32)
        stacked = jnp.concatenate([upper, next_rows(lanes)], axis=0)
        grads = (stacked * slope_ref[:, lanes]).astype(BF16).astype(F32)
        back = tap_sum(grads, kernel_ref, lanes, taps - 1, -1, ROWS)
        total = upper + jnp.where(row_ids < count, back, 0.0)
        total_ref[:, lanes] = total
        total_low[:, lanes] = total.astype(BF16)
        return carry

    lax.fori_loop(0, upstream_ref.shape[1] // PAIR, conv_step, 0, unroll=True)
    out_grad = dot_nt(total_low[...], w_out_ref[...]).astype(BF16)
    message_ref[0:ROWS, :] = out_grad
    product = out_grad.astype(F32) * attended[...].astype(F32)
    high = product.astype(BF16)
    low = (product - high.astype(F32)).astype(BF16)
    width = product.shape[1]
    head_of = lax.broadcasted_iota(jnp.int32, (PAIR, width), 1) // HEAD_DIM
    chosen = (head_of == lax.broadcasted_iota(jnp.int32, (PAIR, width), 0)).astype(F32).astype(BF16)
    dots = dot_nt(high, chosen) + dot_nt(low, chosen)
    dot_ref[...] = dots
    stacked = jnp.concatenate([log_ref[...].T[0:8], dots.T[0:8]], axis=0)
    message_ref[ROWS : ROWS + 16, :] = jnp.zeros((16, width), BF16)
    for index, part in enumerate(three_parts(stacked)):
        message_ref[ROWS : ROWS + 16, index * PAIR : (index + 1) * PAIR] = part


def slope_of(output):
    gate = 1.0 / (1.0 + jnp.exp(-output))
    return gate * (1.0 + output * (1.0 - gate))


def body_kernel(valid_ref, own_ref, attended_ref, after_ref, w_out_ref, kernel_ref, mixed_ref, slope_ref):
    place = lax.axis_index("tm")
    projected = dot_nn(attended_ref[...], w_out_ref[...])
    row_ids = lax.broadcasted_iota(jnp.int32, (ROWS, 1), 0)
    edge_ids = lax.broadcasted_iota(jnp.int32, (EDGE, 1), 0)
    here = projected[0:ROWS] + own_ref[...].astype(F32)
    after = projected[ROWS:] + after_ref[ROWS : ROWS + EDGE, :].astype(F32)
    here = jnp.where(row_ids < valid_count(valid_ref, place), here, 0.0)
    after = jnp.where(edge_ids < valid_count(valid_ref, place + 1), after, 0.0)
    mixed_ref[0:ROWS, :] = here.astype(BF16).astype(F32)
    mixed_ref[ROWS:, :] = after.astype(BF16).astype(F32)
    taps = kernel_ref.shape[0]

    def conv_step(step, carry):
        lanes = pl.ds(pl.multiple_of(step * PAIR, PAIR), PAIR)
        output = tap_sum(mixed_ref[:, lanes], kernel_ref, lanes, EDGE - (taps - 1), 1, ROWS)
        slope_ref[:, lanes] = slope_of(output)
        return carry

    lax.fori_loop(0, own_ref.shape[1] // PAIR, conv_step, 0, unroll=True)


def mix_kernel(
    valid_ref,
    mixed_ref,
    late_slope_ref,
    top_ref,
    attended_ref,
    log_ref,
    back2_ref,
    back4_ref,
    back5_ref,
    peer_ref,
    peer_back2_ref,
    peer_back4_ref,
    after_ref,
    w_out_ref,
    kernel_ref,
    slope_ref,
    total_ref,
    message_ref,
    dot_ref,
    window,
    query_tail,
    attended_all,
    mixed,
    total_low,
    before_rows,
):
    place = lax.axis_index("tm")
    odd = lax.rem(place, 2) == 1
    wide = query_tail.shape[1]
    half_edge = EDGE // 2
    counts = [valid_count(valid_ref, place + block - LEFT - 1) for block in range(LEFT + 3)]
    choose_rows(before_rows, odd, peer_ref, peer_back2_ref, slice(ROWS, ROWS + EDGE + half_edge))
    choose_blocks(
        window,
        odd,
        (
            (peer_back4_ref, back5_ref),
            (back4_ref, back4_ref),
            (peer_back2_ref, peer_back4_ref),
            (back2_ref, back2_ref),
            (peer_ref, peer_back2_ref),
        ),
    )
    query_tail[0:half_edge, :] = before_rows[EDGE : EDGE + half_edge, 0:wide]
    query_tail[half_edge:EDGE, :] = before_rows[EDGE : EDGE + half_edge, wide : 2 * wide]
    key_lane = lax.broadcasted_iota(jnp.int32, (1, ROWS), 1)
    allowed = jnp.concatenate([key_lane < count for count in counts[: LEFT + 1]], axis=1)
    for pair in range(wide // PAIR):
        lanes = slice(pair * PAIR, (pair + 1) * PAIR)
        value_lanes = slice(wide + pair * PAIR, wide + (pair + 1) * PAIR)
        total = None
        for half in range(2):
            scores = dot_nt(query_tail[:, lanes], masked_half(window[:, lanes], half)) * SCALE
            shares_low, _, _ = pair_shares(scores, allowed)
            product = dot_nn(shares_low, masked_half(window[:, value_lanes], half))
            total = product if total is None else total + product
        attended_all[:, lanes] = total.astype(BF16)
    projected = dot_nn(attended_all[...], w_out_ref[...])
    edge_ids = lax.broadcasted_iota(jnp.int32, (EDGE, 1), 0)
    before = projected + before_rows[0:EDGE, :].astype(F32)
    before = jnp.where(edge_ids + (ROWS - EDGE) < counts[LEFT], before, 0.0)
    mixed[0:EDGE, :] = before.astype(BF16).astype(F32)
    mixed[EDGE:, :] = mixed_ref[0:EDGE, :]
    slope_ref[EDGE:, :] = late_slope_ref[...]
    taps = kernel_ref.shape[0]

    def conv_step(step, carry):
        lanes = pl.ds(pl.multiple_of(step * PAIR, PAIR), PAIR)
        output = tap_sum(mixed[:, lanes], kernel_ref, lanes, EDGE - (taps - 1), 1, EDGE)
        slope_ref[0:EDGE, lanes] = slope_of(output)
        return carry

    lax.fori_loop(0, mixed.shape[1] // PAIR, conv_step, 0, unroll=True)
    first = ROWS + EDGE + half_edge
    mixer_body(
        counts[LEFT + 1],
        top_ref,
        lambda lanes: after_ref[first : first + EDGE, lanes].astype(F32),
        slope_ref,
        kernel_ref,
        w_out_ref,
        attended_ref[0:ROWS, :],
        log_ref,
        total_ref,
        message_ref,
        dot_ref,
        total_low,
    )


def mixer_kernel(
    valid_ref,
    upstream_ref,
    next_ref,
    slope_ref,
    kernel_ref,
    w_out_ref,
    attended_ref,
    log_ref,
    total_ref,
    message_ref,
    dot_ref,
    total_low,
):
    mixer_body(
        valid_count(valid_ref, lax.axis_index("tm")),
        upstream_ref,
        lambda lanes: next_ref[:, lanes].astype(F32),
        slope_ref,
        kernel_ref,
        w_out_ref,
        attended_ref[0:ROWS, :],
        log_ref,
        total_ref,
        message_ref,
        dot_ref,
        total_low,
    )


def key_terms(key_pair, value_pair, query_pair, grad_pair, logs, dots, key_valid):
    share_halves = []
    score_halves = []
    query_halves = [masked_half(query_pair, half) for half in range(2)]
    grad_halves = [masked_half(grad_pair, half) for half in range(2)]
    for half in range(2):
        scores = dot_nt(key_pair, query_halves[half]) * SCALE
        shares = jnp.exp(jnp.where(key_valid, scores, NEGATIVE) - logs[half])
        share_grad = dot_nt(value_pair, grad_halves[half])
        score_halves.append((shares * (share_grad - dots[half])).astype(BF16))
        share_halves.append(shares.astype(BF16))
    key_sum = None
    value_sum = None
    for block in range(query_pair.shape[0] // ROWS):
        rows = slice(block * ROWS, (block + 1) * ROWS)
        key_term = dot_nn(
            jnp.concatenate([score[:, rows] for score in score_halves], axis=1),
            jnp.concatenate([query[rows] for query in query_halves], axis=0),
        )
        value_term = dot_nn(
            jnp.concatenate([share[:, rows] for share in share_halves], axis=1),
            jnp.concatenate([grad[rows] for grad in grad_halves], axis=0),
        )
        key_term = (key_term * SCALE).astype(BF16).astype(F32)
        value_term = value_term.astype(BF16).astype(F32)
        key_sum = key_term if key_sum is None else key_sum + key_term
        value_sum = value_term if value_sum is None else value_sum + value_term
    return key_sum, value_sum


def message_stats(tail):
    tail = tail.astype(F32)
    return tail[:, 0:PAIR] + tail[:, PAIR : 2 * PAIR] + tail[:, 2 * PAIR : 3 * PAIR]


def query_kernel(
    valid_ref,
    queries_ref,
    kept_ref,
    back2_ref,
    back4_ref,
    peer_ref,
    peer_back2_ref,
    peer_back4_ref,
    message_ref,
    log_ref,
    dot_ref,
    w_query_ref,
    out_ref,
    key_sum_ref,
    value_sum_ref,
    window,
    query_grad,
):
    place = lax.axis_index("tm")
    odd = lax.rem(place, 2) == 1
    wide = queries_ref.shape[1]
    choose_blocks(
        window,
        odd,
        (
            (back4_ref, back4_ref),
            (peer_back2_ref, peer_back4_ref),
            (back2_ref, back2_ref),
            (peer_ref, peer_back2_ref),
            (kept_ref, kept_ref),
        ),
    )
    own_rows = slice(LEFT * ROWS, (LEFT + 1) * ROWS)
    key_lane = lax.broadcasted_iota(jnp.int32, (1, ROWS), 1)
    allowed = jnp.concatenate(
        [key_lane < valid_count(valid_ref, place + block - LEFT) for block in range(LEFT + 1)], axis=1
    )
    key_valid = lax.broadcasted_iota(jnp.int32, (ROWS, ROWS), 0) < valid_count(valid_ref, place)
    stats = message_stats(message_ref[ROWS : ROWS + 16, :])
    for pair in range(wide // PAIR):
        lanes = slice(pair * PAIR, (pair + 1) * PAIR)
        value_lanes = slice(wide + pair * PAIR, wide + (pair + 1) * PAIR)
        query_pair = queries_ref[:, lanes]
        grad_pair = message_ref[0:ROWS, lanes]
        total = None
        for half in range(2):
            key_half = masked_half(window[:, lanes], half)
            value_half = masked_half(window[:, value_lanes], half)
            head = 2 * pair + half
            scores = dot_nt(query_pair, key_half) * SCALE
            shares = jnp.exp(jnp.where(allowed, scores, NEGATIVE) - log_ref[:, head : head + 1])
            share_grad = dot_nt(grad_pair, value_half)
            score_grad = (shares * (share_grad - dot_ref[:, head : head + 1])).astype(BF16)
            product = dot_nn(score_grad, key_half)
            total = product if total is None else total + product
        query_grad[:, lanes] = (total * SCALE).astype(BF16)
        heads = (2 * pair, 2 * pair + 1)
        key_sum_ref[:, lanes], value_sum_ref[:, lanes] = key_terms(
            window[own_rows, lanes],
            window[own_rows, value_lanes],
            query_pair,
            grad_pair,
            [stats[head : head + 1] for head in heads],
            [stats[8 + head : 9 + head] for head in heads],
            key_valid,
        )
    out_ref[...] = dot_nt(query_grad[...], w_query_ref[...])


def key_kernel(
    valid_ref,
    kept_ref,
    query_peer_ref,
    query_far_ref,
    query_peer_far_ref,
    next2_ref,
    next4_ref,
    peer_ref,
    peer_next2_ref,
    peer_next4_ref,
    w_key_ref,
    w_value_ref,
    gain_ref,
    own_ref,
    total_ref,
    partial_ref,
    key_sum_ref,
    value_sum_ref,
    result_ref,
    keep_ref,
    out_ref,
    edge_ref,
    held_ref,
    grads,
    queries,
    tails,
    stats,
    key_grad,
    value_grad,
):
    place = lax.axis_index("tm")
    odd = lax.rem(place, 2) == 1
    count = valid_count(valid_ref, place)
    wide = grads.shape[1]
    messages = (
        (peer_next2_ref, peer_ref),
        (next2_ref, next2_ref),
        (peer_next4_ref, peer_next2_ref),
        (next4_ref, next4_ref),
    )
    choose_blocks(grads, odd, messages)
    for block, (when_odd, when_even) in enumerate(messages):
        target = tails.at[block * 16 : block * 16 + 16]
        choose_rows(target, odd, when_odd, when_even, slice(ROWS, ROWS + 16))
    choose_blocks(
        queries,
        odd,
        (
            (query_peer_far_ref.at[0:ROWS], query_peer_ref),
            (query_peer_far_ref.at[ROWS : 2 * ROWS], query_far_ref.at[0:ROWS]),
            (query_far_ref.at[ROWS : 2 * ROWS], query_far_ref.at[ROWS : 2 * ROWS]),
            (query_far_ref.at[0:ROWS], query_peer_far_ref.at[ROWS : 2 * ROWS]),
        ),
    )
    for block in range(LEFT):
        stats[:, block * ROWS : (block + 1) * ROWS] = message_stats(tails[block * 16 : block * 16 + 16, :])
    key_valid = lax.broadcasted_iota(jnp.int32, (ROWS, LEFT * ROWS), 0) < count
    for pair in range(wide // PAIR):
        lanes = slice(pair * PAIR, (pair + 1) * PAIR)
        heads = (2 * pair, 2 * pair + 1)
        key_sum, value_sum = key_terms(
            kept_ref[:, lanes],
            kept_ref[:, slice(wide + pair * PAIR, wide + (pair + 1) * PAIR)],
            queries[:, lanes],
            grads[:, lanes],
            [stats[head : head + 1, :] for head in heads],
            [stats[8 + head : 9 + head, :] for head in heads],
            key_valid,
        )
        key_grad[:, lanes] = (key_sum_ref[:, lanes] + key_sum).astype(BF16)
        value_grad[:, lanes] = (value_sum_ref[:, lanes] + value_sum).astype(BF16)
    normed_grad = partial_ref[...] + dot_nt(key_grad[...], w_key_ref[...])
    normed_grad = normed_grad + dot_nt(value_grad[...], w_value_ref[...])
    scaled = normed_grad * gain_ref[...]
    unit, inverse = unit_rows(own_ref[...].astype(F32))
    back = inverse * (
        scaled
        - jnp.mean(scaled, axis=-1, keepdims=True)
        - unit * jnp.mean(scaled * unit, axis=-1, keepdims=True)
    )
    grad = total_ref[...] + back
    if out_ref is not None:
        out_ref[...] = grad.astype(BF16)
        edge_ref[...] = grad[0:EDGE].astype(BF16)
    mine = lax.axis_index("section") == keep_ref[0]
    held_ref[...] = jnp.where(mine, grad, result_ref[...].astype(F32)).astype(BF16)


def last_key_kernel(operands, *refs):
    key_kernel(*refs[:operands], None, None, *refs[operands:])


def call(kernel, name, operands, outs, scratch, copies=0, limit=VMEM_LIMIT):
    kinds = {
        "s": pl.BlockSpec(memory_space=pltpu.SMEM),
        "v": pl.BlockSpec(memory_space=pltpu.VMEM),
        "h": pl.BlockSpec(memory_space=pltpu.HBM),
    }
    return pl.pallas_call(
        kernel,
        name=name,
        in_specs=[kinds[place] for _, place in operands],
        out_specs=[kinds["v"]] * len(outs),
        out_shape=[jax.ShapeDtypeStruct(shape, dtype) for shape, dtype in outs],
        scratch_shapes=[pltpu.VMEM(shape, dtype) for shape, dtype in scratch]
        + [pltpu.SemaphoreType.DMA((copies,))] * (copies > 0),
        compiler_params=pltpu.CompilerParams(vmem_limit_bytes=limit),
        cost_estimate=pl.CostEstimate(flops=1 << 30, bytes_accessed=4 << 20, transcendentals=0),
    )(*[array for array, _ in operands])


def placed(kinds, *arrays):
    return list(zip(arrays, kinds, strict=True))


def after(value, *others):
    return lax.optimization_barrier((value, *others))[0]


def shards(
    layer_inputs, top_grad, w_query, w_key, w_value, w_out, conv_kernel, norm_gain, group_valid
):
    own = layer_inputs[0]
    width = own.shape[1]
    wide = w_query.shape[2]
    query_weight = w_query[0]
    key_weight = w_key[0]
    value_weight = w_value[0]
    out_weight = w_out[0]
    kernel = conv_kernel[0]
    sections = lax.axis_size("section")
    count = lax.axis_size("tm")

    def moved(value, pairs):
        return lax.ppermute(value, ("tm", "section"), pairs)

    def at(layer, frame):
        return frame * sections + layer

    def across(steps, chosen):
        return [
            (at(section, source), at(section, source + steps))
            for section in chosen
            for source in range(max(0, -steps), min(count, count - steps))
        ]

    every = range(sections)
    half_edge = EDGE // 2
    swap = [(at(section, source), at(section, source ^ 1)) for section in every for source in range(count)]
    weight = ((width, wide), BF16)
    queries, kept, ahead, behind = call(
        project_kernel,
        "project",
        placed("hhvhhh", own, top_grad, norm_gain, query_weight, key_weight, value_weight),
        [
            ((ROWS, wide), BF16),
            ((ROWS, 2 * wide), BF16),
            ((ROWS + EDGE + half_edge, width), BF16),
            ((ROWS + 2 * EDGE + half_edge, width), BF16),
        ],
        [((ROWS, width), BF16), ((ROWS, width), BF16), ((EDGE, width), BF16), weight, weight, weight],
        5,
        VMEM_WHOLE,
    )
    back2 = moved(ahead, across(2, every))
    back4 = moved(kept, across(4, every))
    after1 = moved(behind, across(-1, every))
    peer = moved(ahead, swap)
    query_peer = moved(queries, swap)
    peer_back2 = moved(back2, swap)
    peer_back4 = moved(back4, swap)
    chip_pairs = [
        (at(section, source), at(section, source - 2 - 2 * (source % 2)))
        for section in every
        for source in range(count)
        if source >= 2 + 2 * (source % 2)
    ]
    query_far = moved(jnp.concatenate([queries, after(query_peer, peer)]), chip_pairs)
    query_peer_far = moved(query_far, swap)
    far_pairs = [
        (at(section, source), at(section, source + 5))
        for section in every
        for source in range(1, count - 5, 2)
    ]
    back5 = moved(after(kept, back2), far_pairs)
    query_peer, query_far, query_peer_far, after1 = lax.optimization_barrier(
        (query_peer, query_far, query_peer_far, after1)
    )

    span = (LEFT + 1) * ROWS
    attended, logs = call(
        attend_kernel,
        "attend",
        placed("svvvvvvvv", group_valid, queries, kept, back2, back4, peer, peer_back2, peer_back4, after1),
        [((ROWS + EDGE, wide), BF16), ((ROWS, PAIR), F32)],
        [(((LEFT + 2) * ROWS, 2 * wide), BF16), ((ROWS + EDGE, wide), BF16)],
    )
    step_outs = [((ROWS, width), F32), ((ROWS + 16, wide), BF16), ((ROWS, PAIR), F32)]
    mixed, late_slope = call(
        body_kernel,
        "body",
        placed("svvvvv", group_valid, own, attended, after1, out_weight, kernel),
        [((ROWS + EDGE, width), F32), ((ROWS, width), F32)],
        [],
    )
    back5 = after(back5, mixed)
    slope, total, message, dots = call(
        mix_kernel,
        "mix",
        placed(
            "svvvvvvvvvvvvvv",
            group_valid,
            mixed,
            late_slope,
            top_grad,
            attended,
            logs,
            back2,
            back4,
            back5,
            peer,
            peer_back2,
            peer_back4,
            after1,
            out_weight,
            kernel,
        ),
        [((ROWS + EDGE, width), F32)] + step_outs,
        [
            ((span, 2 * wide), BF16),
            ((EDGE, wide), BF16),
            ((EDGE, wide), BF16),
            ((2 * EDGE, width), F32),
            ((ROWS, width), BF16),
            ((EDGE + half_edge, width), BF16),
        ],
    )

    result = own
    upstream = None
    upstream_next = None
    for step in range(sections):
        layer = sections - 1 - step
        if step > 0:
            total, message, dots = call(
                mixer_kernel,
                "mixer",
                placed(
                    "svvvvvvv", group_valid, upstream, upstream_next, slope, kernel, out_weight, attended, logs
                ),
                step_outs,
                [((ROWS, width), BF16)],
                    )
        here = [layer]
        grad2 = moved(message, across(-2, here))
        grad4 = moved(message, across(-4, here))
        peer_grad = moved(message, swap)
        partial, key_sum, value_sum = call(
            query_kernel,
            "own_queries",
            placed(
                "svvvvvvvvvvv",
                group_valid,
                queries,
                kept,
                back2,
                back4,
                peer,
                peer_back2,
                peer_back4,
                message,
                logs,
                dots,
                query_weight,
            ),
            [((ROWS, width), F32), ((ROWS, wide), F32), ((ROWS, wide), F32)],
            [
                ((span, 2 * wide), BF16),
                ((ROWS, wide), BF16),
            ],
            )
        grad2 = after(grad2, partial)
        grad4 = after(grad4, partial)
        peer_grad2 = moved(grad2, swap)
        peer_grad4 = moved(grad4, swap)
        key_operands = placed(
            "svvvvvvvvvvvvvvvvvvs",
            group_valid,
            kept,
            query_peer,
            query_far,
            query_peer_far,
            grad2,
            grad4,
            peer_grad,
            peer_grad2,
            peer_grad4,
            key_weight,
            value_weight,
            norm_gain,
            own,
            total,
            partial,
            key_sum,
            value_sum,
            result,
            jnp.full((1,), layer, jnp.int32),
            )
        key_scratch = [
            ((LEFT * ROWS, wide), BF16),
            ((LEFT * ROWS, wide), BF16),
            ((LEFT * 16, wide), BF16),
            ((16, LEFT * ROWS), F32),
            ((ROWS, wide), BF16),
            ((ROWS, wide), BF16),
        ]
        whole = ((ROWS, width), BF16)
        if layer > 0:
            input_grad, edge, result = call(
                key_kernel, "own_keys", key_operands, [whole, ((EDGE, width), BF16), whole], key_scratch
            )
        else:
            (result,) = call(
                functools.partial(last_key_kernel, len(key_operands)),
                "last_keys",
                key_operands,
                [whole],
                key_scratch,
            )
        if layer > 0:
            upstream = moved(
                input_grad,
                [(at(layer, source), at(layer - 1, source)) for source in range(count)]
                + [(at(layer - 1, source), at(layer, source)) for source in range(count)],
            )
            upstream_next = moved(
                edge, [(at(layer, source), at(layer - 1, source - 1)) for source in range(1, count)]
            )
    return result[None]


def solution(mesh):
    placed = (
        P("section", "tm", None),
        P("tm", None),
        P("section", None, None),
        P("section", None, None),
        P("section", None, None),
        P("section", None, None),
        P("section", None, None),
        P("section", None),
        P(),
    )
    return jax.shard_map(
        shards, mesh=mesh, in_specs=placed, out_specs=P("section", "tm", None), check_vma=False
    )
```

```python
import functools

import jax
import jax.numpy as jnp
from jax import lax
from jax.experimental import pallas as pl
from jax.experimental.pallas import tpu as pltpu
from jax.sharding import PartitionSpec as P

HEAD_DIM = 64
PAIR = 128
ROWS = 128
LEFT = 4
EDGE = 32
SCALE = HEAD_DIM ** (-0.5)
NEGATIVE = -1e30
EPSILON = 1e-05
F32 = jnp.float32
BF16 = jnp.bfloat16
VMEM_LIMIT = 20 << 20
VMEM_WHOLE = 60 << 20


def dot_nn(a, b):
    return lax.dot_general(a, b, (((1,), (0,)), ((), ())), preferred_element_type=F32)


def dot_nt(a, b):
    return lax.dot_general(a, b, (((1,), (1,)), ((), ())), preferred_element_type=F32)


def valid_count(valid_ref, block):
    groups = valid_ref.shape[0]
    inside = (block >= 0) & (block < groups)
    return jnp.where(inside, valid_ref[jnp.clip(block, 0, groups - 1)], 0)


def even_half(rows):
    return lax.broadcasted_iota(jnp.int32, (rows, PAIR), 1) < HEAD_DIM


def unit_rows(values):
    center = values - jnp.mean(values, axis=-1, keepdims=True)
    spread = jnp.mean(center * center, axis=-1, keepdims=True)
    inverse = lax.rsqrt(spread + EPSILON)
    return center * inverse, inverse


def three_parts(value):
    first = value.astype(BF16)
    rest = value - first.astype(F32)
    second = rest.astype(BF16)
    third = (rest - second.astype(F32)).astype(BF16)
    return first, second, third


def shift_rows(value, amount):
    if amount == 0:
        return value
    return pltpu.roll(value, value.shape[0] - amount, 0)


def tap_sum(padded, kernel_ref, lanes, first, step, rows):
    taps = kernel_ref.shape[0]
    total = jnp.zeros((rows, padded.shape[1]), F32)
    for phase in range(8):
        moved = None
        for tap in range(taps):
            offset = first + step * tap
            if offset % 8 != phase:
                continue
            if moved is None:
                moved = shift_rows(padded, phase)
            base = offset - phase
            total = total + kernel_ref[tap : tap + 1, lanes] * moved[base : base + rows]
    return total


def project_kernel(
    own_ref,
    top_ref,
    gain_ref,
    w_query_ref,
    w_key_ref,
    w_value_ref,
    queries_ref,
    kept_ref,
    ahead_ref,
    behind_ref,
    normed,
    own,
    top,
    w_query,
    w_key,
    w_value,
    semaphores,
):
    chunk = 16
    loads = [
        pltpu.make_async_copy(source, target, semaphores.at[index])
        for index, (source, target) in enumerate(
            (
                (own_ref, own),
                (w_key_ref, w_key),
                (w_value_ref, w_value),
                (w_query_ref, w_query),
                (top_ref.at[0:EDGE], top),
            )
        )
    ]
    for load in loads:
        load.start()
    loads[0].wait()

    def norm_step(step, carry):
        rows = pl.ds(pl.multiple_of(step * chunk, chunk), chunk)
        unit, _ = unit_rows(own[rows, :].astype(F32))
        normed[rows, :] = (unit * gain_ref[...]).astype(BF16)
        return carry

    lax.fori_loop(0, ROWS // chunk, norm_step, 0, unroll=True)
    wide = w_key_ref.shape[1]
    half = EDGE // 2
    loads[1].wait()
    keys = dot_nn(normed[...], w_key[...]).astype(BF16)
    loads[2].wait()
    values = dot_nn(normed[...], w_value[...]).astype(BF16)
    for ref in (kept_ref, ahead_ref, behind_ref):
        ref[0:ROWS, 0:wide] = keys
        ref[0:ROWS, wide : 2 * wide] = values
    loads[3].wait()
    loads[4].wait()
    queries = dot_nn(normed[...], w_query[...]).astype(BF16)
    queries_ref[...] = queries
    ahead_ref[ROWS : ROWS + EDGE, :] = own[ROWS - EDGE : ROWS, :]
    ahead_ref[ROWS + EDGE : ROWS + EDGE + half, 0:wide] = queries[ROWS - EDGE : ROWS - half]
    ahead_ref[ROWS + EDGE : ROWS + EDGE + half, wide : 2 * wide] = queries[ROWS - half : ROWS]
    behind_ref[ROWS : ROWS + EDGE, :] = own[0:EDGE, :]
    behind_ref[ROWS + EDGE : ROWS + EDGE + half, 0:wide] = queries[0:half]
    behind_ref[ROWS + EDGE : ROWS + EDGE + half, wide : 2 * wide] = queries[half:EDGE]
    behind_ref[ROWS + EDGE + half : ROWS + 2 * EDGE + half, :] = top[...]


def choose_rows(target, odd, when_odd, when_even, rows):
    if when_even is when_odd:
        target[...] = when_odd[rows, :]
        return

    @pl.when(odd)
    def _():
        target[...] = when_odd[rows, :]

    @pl.when(jnp.logical_not(odd))
    def _():
        target[...] = when_even[rows, :]


def choose_blocks(target, odd, sources):
    for index, (when_odd, when_even) in enumerate(sources):
        choose_rows(target.at[index * ROWS : (index + 1) * ROWS], odd, when_odd, when_even, slice(0, ROWS))


def masked_half(value, half):
    keep = even_half(value.shape[0])
    if half:
        keep = jnp.logical_not(keep)
    return jnp.where(keep, value, jnp.zeros_like(value))


def pair_shares(scores, allowed):
    part = jnp.where(allowed, scores, NEGATIVE)
    highest = jnp.max(part, axis=-1, keepdims=True)
    exped = jnp.exp(part - highest)
    summed = jnp.sum(exped, axis=-1, keepdims=True)
    return (exped * (1.0 / summed)).astype(BF16), highest, summed


def attend_kernel(
    valid_ref,
    queries_ref,
    kept_ref,
    back2_ref,
    back4_ref,
    peer_ref,
    peer_back2_ref,
    peer_back4_ref,
    after_ref,
    attended_ref,
    log_ref,
    window,
    query_all,
):
    place = lax.axis_index("tm")
    odd = lax.rem(place, 2) == 1
    wide = queries_ref.shape[1]
    half_edge = EDGE // 2
    packed = after_ref[ROWS + EDGE : ROWS + EDGE + half_edge, :]
    query_all[0:ROWS, :] = queries_ref[...]
    choose_blocks(
        window,
        odd,
        (
            (back4_ref, back4_ref),
            (peer_back2_ref, peer_back4_ref),
            (back2_ref, back2_ref),
            (peer_ref, peer_back2_ref),
            (kept_ref, kept_ref),
            (after_ref, after_ref),
        ),
    )
    query_all[ROWS : ROWS + half_edge, :] = packed[:, 0:wide]
    query_all[ROWS + half_edge : ROWS + EDGE, :] = packed[:, wide : 2 * wide]
    key_lane = lax.broadcasted_iota(jnp.int32, (1, ROWS), 1)
    allowed = jnp.concatenate(
        [key_lane < valid_count(valid_ref, place + block - LEFT) for block in range(LEFT + 2)], axis=1
    )
    span = (LEFT + 1) * ROWS
    log_lane = lax.broadcasted_iota(jnp.int32, (ROWS, PAIR), 1)
    logs = jnp.zeros((ROWS, PAIR), F32)
    for pair in range(wide // PAIR):
        lanes = slice(pair * PAIR, (pair + 1) * PAIR)
        value_lanes = slice(wide + pair * PAIR, wide + (pair + 1) * PAIR)
        totals = [None, None]
        for half in range(2):
            scores = dot_nt(query_all[:, lanes], masked_half(window[:, lanes], half)) * SCALE
            value_half = masked_half(window[:, value_lanes], half)
            for group, (low, high, first) in enumerate(((0, ROWS, 0), (ROWS, ROWS + EDGE, ROWS))):
                shares_low, highest, summed = pair_shares(
                    scores[low:high, first : first + span], allowed[:, first : first + span]
                )
                product = dot_nn(shares_low, value_half[first : first + span])
                totals[group] = product if totals[group] is None else totals[group] + product
                if group == 0:
                    logs = jnp.where(log_lane == 2 * pair + half, highest + jnp.log(summed), logs)
        attended_ref[0:ROWS, lanes] = totals[0].astype(BF16)
        attended_ref[ROWS : ROWS + EDGE, lanes] = totals[1].astype(BF16)
    log_ref[...] = logs


def mixer_body(
    count, upstream_ref, next_rows, slope_ref, kernel_ref, w_out_ref, attended, log_ref, total_ref, message_ref, dot_ref, total_low
):
    row_ids = lax.broadcasted_iota(jnp.int32, (ROWS, PAIR), 0)
    taps = kernel_ref.shape[0]

    def conv_step(step, carry):
        lanes = pl.ds(pl.multiple_of(step * PAIR, PAIR), PAIR)
        upper = upstream_ref[:, lanes].astype(F32)
        stacked = jnp.concatenate([upper, next_rows(lanes)], axis=0)
        grads = (stacked * slope_ref[:, lanes]).astype(BF16).astype(F32)
        back = tap_sum(grads, kernel_ref, lanes, taps - 1, -1, ROWS)
        total = upper + jnp.where(row_ids < count, back, 0.0)
        total_ref[:, lanes] = total
        total_low[:, lanes] = total.astype(BF16)
        return carry

    lax.fori_loop(0, upstream_ref.shape[1] // PAIR, conv_step, 0, unroll=True)
    out_grad = dot_nt(total_low[...], w_out_ref[...]).astype(BF16)
    message_ref[0:ROWS, :] = out_grad
    product = out_grad.astype(F32) * attended[...].astype(F32)
    high = product.astype(BF16)
    low = (product - high.astype(F32)).astype(BF16)
    width = product.shape[1]
    head_of = lax.broadcasted_iota(jnp.int32, (PAIR, width), 1) // HEAD_DIM
    chosen = (head_of == lax.broadcasted_iota(jnp.int32, (PAIR, width), 0)).astype(F32).astype(BF16)
    dots = dot_nt(high, chosen) + dot_nt(low, chosen)
    dot_ref[...] = dots
    stacked = jnp.concatenate([log_ref[...].T[0:8], dots.T[0:8]], axis=0)
    message_ref[ROWS : ROWS + 16, :] = jnp.zeros((16, width), BF16)
    for index, part in enumerate(three_parts(stacked)):
        message_ref[ROWS : ROWS + 16, index * PAIR : (index + 1) * PAIR] = part


def slope_of(output):
    gate = 1.0 / (1.0 + jnp.exp(-output))
    return gate * (1.0 + output * (1.0 - gate))


def body_kernel(valid_ref, own_ref, attended_ref, after_ref, w_out_ref, kernel_ref, mixed_ref, slope_ref):
    place = lax.axis_index("tm")
    projected = dot_nn(attended_ref[...], w_out_ref[...])
    row_ids = lax.broadcasted_iota(jnp.int32, (ROWS, 1), 0)
    edge_ids = lax.broadcasted_iota(jnp.int32, (EDGE, 1), 0)
    here = projected[0:ROWS] + own_ref[...].astype(F32)
    after = projected[ROWS:] + after_ref[ROWS : ROWS + EDGE, :].astype(F32)
    here = jnp.where(row_ids < valid_count(valid_ref, place), here, 0.0)
    after = jnp.where(edge_ids < valid_count(valid_ref, place + 1), after, 0.0)
    mixed_ref[0:ROWS, :] = here.astype(BF16).astype(F32)
    mixed_ref[ROWS:, :] = after.astype(BF16).astype(F32)
    taps = kernel_ref.shape[0]

    def conv_step(step, carry):
        lanes = pl.ds(pl.multiple_of(step * PAIR, PAIR), PAIR)
        output = tap_sum(mixed_ref[:, lanes], kernel_ref, lanes, EDGE - (taps - 1), 1, ROWS)
        slope_ref[:, lanes] = slope_of(output)
        return carry

    lax.fori_loop(0, own_ref.shape[1] // PAIR, conv_step, 0, unroll=True)


def mix_kernel(
    valid_ref,
    mixed_ref,
    late_slope_ref,
    top_ref,
    attended_ref,
    log_ref,
    back2_ref,
    back4_ref,
    back5_ref,
    peer_ref,
    peer_back2_ref,
    peer_back4_ref,
    after_ref,
    w_out_ref,
    kernel_ref,
    slope_ref,
    total_ref,
    message_ref,
    dot_ref,
    window,
    query_tail,
    attended_all,
    mixed,
    total_low,
    before_rows,
):
    place = lax.axis_index("tm")
    odd = lax.rem(place, 2) == 1
    wide = query_tail.shape[1]
    half_edge = EDGE // 2
    counts = [valid_count(valid_ref, place + block - LEFT - 1) for block in range(LEFT + 3)]
    choose_rows(before_rows, odd, peer_ref, peer_back2_ref, slice(ROWS, ROWS + EDGE + half_edge))
    choose_blocks(
        window,
        odd,
        (
            (peer_back4_ref, back5_ref),
            (back4_ref, back4_ref),
            (peer_back2_ref, peer_back4_ref),
            (back2_ref, back2_ref),
            (peer_ref, peer_back2_ref),
        ),
    )
    query_tail[0:half_edge, :] = before_rows[EDGE : EDGE + half_edge, 0:wide]
    query_tail[half_edge:EDGE, :] = before_rows[EDGE : EDGE + half_edge, wide : 2 * wide]
    key_lane = lax.broadcasted_iota(jnp.int32, (1, ROWS), 1)
    allowed = jnp.concatenate([key_lane < count for count in counts[: LEFT + 1]], axis=1)
    for pair in range(wide // PAIR):
        lanes = slice(pair * PAIR, (pair + 1) * PAIR)
        value_lanes = slice(wide + pair * PAIR, wide + (pair + 1) * PAIR)
        total = None
        for half in range(2):
            scores = dot_nt(query_tail[:, lanes], masked_half(window[:, lanes], half)) * SCALE
            shares_low, _, _ = pair_shares(scores, allowed)
            product = dot_nn(shares_low, masked_half(window[:, value_lanes], half))
            total = product if total is None else total + product
        attended_all[:, lanes] = total.astype(BF16)
    projected = dot_nn(attended_all[...], w_out_ref[...])
    edge_ids = lax.broadcasted_iota(jnp.int32, (EDGE, 1), 0)
    before = projected + before_rows[0:EDGE, :].astype(F32)
    before = jnp.where(edge_ids + (ROWS - EDGE) < counts[LEFT], before, 0.0)
    mixed[0:EDGE, :] = before.astype(BF16).astype(F32)
    mixed[EDGE:, :] = mixed_ref[0:EDGE, :]
    slope_ref[EDGE:, :] = late_slope_ref[...]
    taps = kernel_ref.shape[0]

    def conv_step(step, carry):
        lanes = pl.ds(pl.multiple_of(step * PAIR, PAIR), PAIR)
        output = tap_sum(mixed[:, lanes], kernel_ref, lanes, EDGE - (taps - 1), 1, EDGE)
        slope_ref[0:EDGE, lanes] = slope_of(output)
        return carry

    lax.fori_loop(0, mixed.shape[1] // PAIR, conv_step, 0, unroll=True)
    first = ROWS + EDGE + half_edge
    mixer_body(
        counts[LEFT + 1],
        top_ref,
        lambda lanes: after_ref[first : first + EDGE, lanes].astype(F32),
        slope_ref,
        kernel_ref,
        w_out_ref,
        attended_ref[0:ROWS, :],
        log_ref,
        total_ref,
        message_ref,
        dot_ref,
        total_low,
    )


def mixer_kernel(
    valid_ref,
    upstream_ref,
    next_ref,
    slope_ref,
    kernel_ref,
    w_out_ref,
    attended_ref,
    log_ref,
    total_ref,
    message_ref,
    dot_ref,
    total_low,
):
    mixer_body(
        valid_count(valid_ref, lax.axis_index("tm")),
        upstream_ref,
        lambda lanes: next_ref[:, lanes].astype(F32),
        slope_ref,
        kernel_ref,
        w_out_ref,
        attended_ref[0:ROWS, :],
        log_ref,
        total_ref,
        message_ref,
        dot_ref,
        total_low,
    )


def key_terms(key_pair, value_pair, query_pair, grad_pair, logs, dots, key_valid):
    share_halves = []
    score_halves = []
    query_halves = [masked_half(query_pair, half) for half in range(2)]
    grad_halves = [masked_half(grad_pair, half) for half in range(2)]
    for half in range(2):
        scores = dot_nt(key_pair, query_halves[half]) * SCALE
        shares = jnp.exp(jnp.where(key_valid, scores, NEGATIVE) - logs[half])
        share_grad = dot_nt(value_pair, grad_halves[half])
        score_halves.append((shares * (share_grad - dots[half])).astype(BF16))
        share_halves.append(shares.astype(BF16))
    key_sum = None
    value_sum = None
    for block in range(query_pair.shape[0] // ROWS):
        rows = slice(block * ROWS, (block + 1) * ROWS)
        key_term = dot_nn(
            jnp.concatenate([score[:, rows] for score in score_halves], axis=1),
            jnp.concatenate([query[rows] for query in query_halves], axis=0),
        )
        value_term = dot_nn(
            jnp.concatenate([share[:, rows] for share in share_halves], axis=1),
            jnp.concatenate([grad[rows] for grad in grad_halves], axis=0),
        )
        key_term = (key_term * SCALE).astype(BF16).astype(F32)
        value_term = value_term.astype(BF16).astype(F32)
        key_sum = key_term if key_sum is None else key_sum + key_term
        value_sum = value_term if value_sum is None else value_sum + value_term
    return key_sum, value_sum


def message_stats(tail):
    tail = tail.astype(F32)
    return tail[:, 0:PAIR] + tail[:, PAIR : 2 * PAIR] + tail[:, 2 * PAIR : 3 * PAIR]


def query_kernel(
    valid_ref,
    queries_ref,
    kept_ref,
    back2_ref,
    back4_ref,
    peer_ref,
    peer_back2_ref,
    peer_back4_ref,
    message_ref,
    log_ref,
    dot_ref,
    w_query_ref,
    own_ref,
    out_ref,
    key_sum_ref,
    value_sum_ref,
    unit_ref,
    inverse_ref,
    window,
    query_grad,
):
    place = lax.axis_index("tm")
    odd = lax.rem(place, 2) == 1
    wide = queries_ref.shape[1]
    choose_blocks(
        window,
        odd,
        (
            (back4_ref, back4_ref),
            (peer_back2_ref, peer_back4_ref),
            (back2_ref, back2_ref),
            (peer_ref, peer_back2_ref),
            (kept_ref, kept_ref),
        ),
    )
    own_rows = slice(LEFT * ROWS, (LEFT + 1) * ROWS)
    key_lane = lax.broadcasted_iota(jnp.int32, (1, ROWS), 1)
    allowed = jnp.concatenate(
        [key_lane < valid_count(valid_ref, place + block - LEFT) for block in range(LEFT + 1)], axis=1
    )
    key_valid = lax.broadcasted_iota(jnp.int32, (ROWS, ROWS), 0) < valid_count(valid_ref, place)
    stats = message_stats(message_ref[ROWS : ROWS + 16, :])
    for pair in range(wide // PAIR):
        lanes = slice(pair * PAIR, (pair + 1) * PAIR)
        value_lanes = slice(wide + pair * PAIR, wide + (pair + 1) * PAIR)
        query_pair = queries_ref[:, lanes]
        grad_pair = message_ref[0:ROWS, lanes]
        total = None
        for half in range(2):
            key_half = masked_half(window[:, lanes], half)
            value_half = masked_half(window[:, value_lanes], half)
            head = 2 * pair + half
            scores = dot_nt(query_pair, key_half) * SCALE
            shares = jnp.exp(jnp.where(allowed, scores, NEGATIVE) - log_ref[:, head : head + 1])
            share_grad = dot_nt(grad_pair, value_half)
            score_grad = (shares * (share_grad - dot_ref[:, head : head + 1])).astype(BF16)
            product = dot_nn(score_grad, key_half)
            total = product if total is None else total + product
        query_grad[:, lanes] = (total * SCALE).astype(BF16)
        heads = (2 * pair, 2 * pair + 1)
        key_sum_ref[:, lanes], value_sum_ref[:, lanes] = key_terms(
            window[own_rows, lanes],
            window[own_rows, value_lanes],
            query_pair,
            grad_pair,
            [stats[head : head + 1] for head in heads],
            [stats[8 + head : 9 + head] for head in heads],
            key_valid,
        )
    out_ref[...] = dot_nt(query_grad[...], w_query_ref[...])
    unit, inverse = unit_rows(own_ref[...].astype(F32))
    unit_ref[...] = unit
    inverse_ref[...] = jnp.broadcast_to(inverse, inverse_ref.shape)


def key_kernel(
    valid_ref,
    kept_ref,
    query_peer_ref,
    query_far_ref,
    query_peer_far_ref,
    next2_ref,
    next4_ref,
    peer_ref,
    peer_next2_ref,
    peer_next4_ref,
    w_key_ref,
    w_value_ref,
    gain_ref,
    unit_ref,
    inverse_ref,
    total_ref,
    partial_ref,
    key_sum_ref,
    value_sum_ref,
    result_ref,
    keep_ref,
    out_ref,
    edge_ref,
    held_ref,
    grads,
    queries,
    tails,
    stats,
    key_grad,
    value_grad,
):
    place = lax.axis_index("tm")
    odd = lax.rem(place, 2) == 1
    count = valid_count(valid_ref, place)
    wide = grads.shape[1]
    messages = (
        (peer_next2_ref, peer_ref),
        (next2_ref, next2_ref),
        (peer_next4_ref, peer_next2_ref),
        (next4_ref, next4_ref),
    )
    choose_blocks(grads, odd, messages)
    for block, (when_odd, when_even) in enumerate(messages):
        target = tails.at[block * 16 : block * 16 + 16]
        choose_rows(target, odd, when_odd, when_even, slice(ROWS, ROWS + 16))
    choose_blocks(
        queries,
        odd,
        (
            (query_peer_far_ref.at[0:ROWS], query_peer_ref),
            (query_peer_far_ref.at[ROWS : 2 * ROWS], query_far_ref.at[0:ROWS]),
            (query_far_ref.at[ROWS : 2 * ROWS], query_far_ref.at[ROWS : 2 * ROWS]),
            (query_far_ref.at[0:ROWS], query_peer_far_ref.at[ROWS : 2 * ROWS]),
        ),
    )
    for block in range(LEFT):
        stats[:, block * ROWS : (block + 1) * ROWS] = message_stats(tails[block * 16 : block * 16 + 16, :])
    key_valid = lax.broadcasted_iota(jnp.int32, (ROWS, LEFT * ROWS), 0) < count
    for pair in range(wide // PAIR):
        lanes = slice(pair * PAIR, (pair + 1) * PAIR)
        heads = (2 * pair, 2 * pair + 1)
        key_sum, value_sum = key_terms(
            kept_ref[:, lanes],
            kept_ref[:, slice(wide + pair * PAIR, wide + (pair + 1) * PAIR)],
            queries[:, lanes],
            grads[:, lanes],
            [stats[head : head + 1, :] for head in heads],
            [stats[8 + head : 9 + head, :] for head in heads],
            key_valid,
        )
        key_grad[:, lanes] = (key_sum_ref[:, lanes] + key_sum).astype(BF16)
        value_grad[:, lanes] = (value_sum_ref[:, lanes] + value_sum).astype(BF16)
    normed_grad = partial_ref[...] + dot_nt(key_grad[...], w_key_ref[...])
    normed_grad = normed_grad + dot_nt(value_grad[...], w_value_ref[...])
    scaled = normed_grad * gain_ref[...]
    unit, inverse = unit_ref[...], inverse_ref[:, 0:1]
    back = inverse * (
        scaled
        - jnp.mean(scaled, axis=-1, keepdims=True)
        - unit * jnp.mean(scaled * unit, axis=-1, keepdims=True)
    )
    grad = total_ref[...] + back
    if out_ref is not None:
        out_ref[...] = grad.astype(BF16)
        edge_ref[...] = grad[0:EDGE].astype(BF16)
    mine = lax.axis_index("section") == keep_ref[0]
    held_ref[...] = jnp.where(mine, grad, result_ref[...].astype(F32)).astype(BF16)


def last_key_kernel(operands, *refs):
    key_kernel(*refs[:operands], None, None, *refs[operands:])


def call(kernel, name, operands, outs, scratch, copies=0, limit=VMEM_LIMIT):
    kinds = {
        "s": pl.BlockSpec(memory_space=pltpu.SMEM),
        "v": pl.BlockSpec(memory_space=pltpu.VMEM),
        "h": pl.BlockSpec(memory_space=pltpu.HBM),
    }
    return pl.pallas_call(
        kernel,
        name=name,
        in_specs=[kinds[place] for _, place in operands],
        out_specs=[kinds["v"]] * len(outs),
        out_shape=[jax.ShapeDtypeStruct(shape, dtype) for shape, dtype in outs],
        scratch_shapes=[pltpu.VMEM(shape, dtype) for shape, dtype in scratch]
        + [pltpu.SemaphoreType.DMA((copies,))] * (copies > 0),
        compiler_params=pltpu.CompilerParams(vmem_limit_bytes=limit),
        cost_estimate=pl.CostEstimate(flops=1 << 30, bytes_accessed=4 << 20, transcendentals=0),
    )(*[array for array, _ in operands])


def placed(kinds, *arrays):
    return list(zip(arrays, kinds, strict=True))


def after(value, *others):
    return lax.optimization_barrier((value, *others))[0]


def shards(
    layer_inputs, top_grad, w_query, w_key, w_value, w_out, conv_kernel, norm_gain, group_valid
):
    own = layer_inputs[0]
    width = own.shape[1]
    wide = w_query.shape[2]
    query_weight = w_query[0]
    key_weight = w_key[0]
    value_weight = w_value[0]
    out_weight = w_out[0]
    kernel = conv_kernel[0]
    sections = lax.axis_size("section")
    count = lax.axis_size("tm")

    def moved(value, pairs):
        return lax.ppermute(value, ("tm", "section"), pairs)

    def at(layer, frame):
        return frame * sections + layer

    def across(steps, chosen):
        return [
            (at(section, source), at(section, source + steps))
            for section in chosen
            for source in range(max(0, -steps), min(count, count - steps))
        ]

    every = range(sections)
    half_edge = EDGE // 2
    swap = [(at(section, source), at(section, source ^ 1)) for section in every for source in range(count)]
    weight = ((width, wide), BF16)
    queries, kept, ahead, behind = call(
        project_kernel,
        "project",
        placed("hhvhhh", own, top_grad, norm_gain, query_weight, key_weight, value_weight),
        [
            ((ROWS, wide), BF16),
            ((ROWS, 2 * wide), BF16),
            ((ROWS + EDGE + half_edge, width), BF16),
            ((ROWS + 2 * EDGE + half_edge, width), BF16),
        ],
        [((ROWS, width), BF16), ((ROWS, width), BF16), ((EDGE, width), BF16), weight, weight, weight],
        5,
        VMEM_WHOLE,
    )
    back2 = moved(ahead, across(2, every))
    back4 = moved(kept, across(4, every))
    after1 = moved(behind, across(-1, every))
    peer = moved(ahead, swap)
    query_peer = moved(queries, swap)
    peer_back2 = moved(back2, swap)
    peer_back4 = moved(back4, swap)
    chip_pairs = [
        (at(section, source), at(section, source - 2 - 2 * (source % 2)))
        for section in every
        for source in range(count)
        if source >= 2 + 2 * (source % 2)
    ]
    query_far = moved(jnp.concatenate([queries, after(query_peer, peer)]), chip_pairs)
    query_peer_far = moved(query_far, swap)
    far_pairs = [
        (at(section, source), at(section, source + 5))
        for section in every
        for source in range(1, count - 5, 2)
    ]
    back5 = moved(after(kept, back2), far_pairs)
    query_peer, query_far, query_peer_far, after1 = lax.optimization_barrier(
        (query_peer, query_far, query_peer_far, after1)
    )

    span = (LEFT + 1) * ROWS
    attended, logs = call(
        attend_kernel,
        "attend",
        placed("svvvvvvvv", group_valid, queries, kept, back2, back4, peer, peer_back2, peer_back4, after1),
        [((ROWS + EDGE, wide), BF16), ((ROWS, PAIR), F32)],
        [(((LEFT + 2) * ROWS, 2 * wide), BF16), ((ROWS + EDGE, wide), BF16)],
    )
    step_outs = [((ROWS, width), F32), ((ROWS + 16, wide), BF16), ((ROWS, PAIR), F32)]
    mixed, late_slope = call(
        body_kernel,
        "body",
        placed("svvvvv", group_valid, own, attended, after1, out_weight, kernel),
        [((ROWS + EDGE, width), F32), ((ROWS, width), F32)],
        [],
    )
    back5 = after(back5, mixed)
    slope, total, message, dots = call(
        mix_kernel,
        "mix",
        placed(
            "svvvvvvvvvvvvvv",
            group_valid,
            mixed,
            late_slope,
            top_grad,
            attended,
            logs,
            back2,
            back4,
            back5,
            peer,
            peer_back2,
            peer_back4,
            after1,
            out_weight,
            kernel,
        ),
        [((ROWS + EDGE, width), F32)] + step_outs,
        [
            ((span, 2 * wide), BF16),
            ((EDGE, wide), BF16),
            ((EDGE, wide), BF16),
            ((2 * EDGE, width), F32),
            ((ROWS, width), BF16),
            ((EDGE + half_edge, width), BF16),
        ],
    )

    result = own
    upstream = None
    upstream_next = None
    for step in range(sections):
        layer = sections - 1 - step
        if step > 0:
            total, message, dots = call(
                mixer_kernel,
                "mixer",
                placed(
                    "svvvvvvv", group_valid, upstream, upstream_next, slope, kernel, out_weight, attended, logs
                ),
                step_outs,
                [((ROWS, width), BF16)],
                    )
        here = [layer]
        grad2 = moved(message, across(-2, here))
        grad4 = moved(message, across(-4, here))
        peer_grad = moved(message, swap)
        partial, key_sum, value_sum, unit, inverse = call(
            query_kernel,
            "own_queries",
            placed(
                "svvvvvvvvvvvv",
                group_valid,
                queries,
                kept,
                back2,
                back4,
                peer,
                peer_back2,
                peer_back4,
                message,
                logs,
                dots,
                query_weight,
                own,
            ),
            [
                ((ROWS, width), F32),
                ((ROWS, wide), F32),
                ((ROWS, wide), F32),
                ((ROWS, width), F32),
                ((ROWS, PAIR), F32),
            ],
            [
                ((span, 2 * wide), BF16),
                ((ROWS, wide), BF16),
            ],
            )
        grad2 = after(grad2, partial)
        grad4 = after(grad4, partial)
        peer_grad2 = moved(grad2, swap)
        peer_grad4 = moved(grad4, swap)
        key_operands = placed(
            "svvvvvvvvvvvvvvvvvvvs",
            group_valid,
            kept,
            query_peer,
            query_far,
            query_peer_far,
            grad2,
            grad4,
            peer_grad,
            peer_grad2,
            peer_grad4,
            key_weight,
            value_weight,
            norm_gain,
            unit,
            inverse,
            total,
            partial,
            key_sum,
            value_sum,
            result,
            jnp.full((1,), layer, jnp.int32),
            )
        key_scratch = [
            ((LEFT * ROWS, wide), BF16),
            ((LEFT * ROWS, wide), BF16),
            ((LEFT * 16, wide), BF16),
            ((16, LEFT * ROWS), F32),
            ((ROWS, wide), BF16),
            ((ROWS, wide), BF16),
        ]
        whole = ((ROWS, width), BF16)
        if layer > 0:
            input_grad, edge, result = call(
                key_kernel, "own_keys", key_operands, [whole, ((EDGE, width), BF16), whole], key_scratch
            )
        else:
            (result,) = call(
                functools.partial(last_key_kernel, len(key_operands)),
                "last_keys",
                key_operands,
                [whole],
                key_scratch,
            )
        if layer > 0:
            upstream = moved(
                input_grad,
                [(at(layer, source), at(layer - 1, source)) for source in range(count)]
                + [(at(layer - 1, source), at(layer, source)) for source in range(count)],
            )
            upstream_next = moved(
                edge, [(at(layer, source), at(layer - 1, source - 1)) for source in range(1, count)]
            )
    return result[None]


def solution(mesh):
    placed = (
        P("section", "tm", None),
        P("tm", None),
        P("section", None, None),
        P("section", None, None),
        P("section", None, None),
        P("section", None, None),
        P("section", None, None),
        P("section", None),
        P(),
    )
    return jax.shard_map(
        shards, mesh=mesh, in_specs=placed, out_specs=P("section", "tm", None), check_vma=False
    )
```
